32 devices in a mesh: clip: 2 (over x), tm: 2 (over core), space: 8 (over z, y).
Axes of the slice: x: 2, y: 2, z: 4, core: 2. Of those that a mesh axis runs over, the one named last changes fastest.
Arguments:
- queue_latents: float32 [16, 2, 16, 128], P(('clip', 'tm'), None, None, 'space'), parts along dimension 0, may hold values from -6 to 6
- fresh_noise: float32 [6, 2, 16, 128], P('clip', None, None, 'space'), parts along dimension 0, may hold values from -6 to 6
- slot_levels: int32 [16], P('clip'), parts along dimension 0, may hold values from 1 to 15, as said below
- level_table: float32 [16, 8, 1152], replicated, may hold values from -2.5 to 2.5
- embed_weight: float32 [16, 1152], replicated, may hold values from -1.5 to 1.5
- spatial_in: bfloat16 [1152, 1728], replicated, may hold values from -0.1875 to 0.1875
- spatial_out: bfloat16 [576, 1152], replicated, may hold values from -0.25 to 0.25
- temporal_in: bfloat16 [1152, 1728], replicated, may hold values from -0.1875 to 0.1875
- temporal_out: bfloat16 [576, 1152], replicated, may hold values from -0.25 to 0.25
- norm_gains: float32 [4, 72], replicated, may hold values from 0.1 to 1.9
- final_weight: float32 [1152, 16], replicated, may hold values from -0.1875 to 0.1875
Outputs:
- next_queue: float32 [16, 2, 16, 128], P(('clip', 'tm'), None, None, 'space'), parts along dimension 0
- denoised: float32 [16, 2, 16, 128], P(('clip', 'tm'), None, None, 'space'), parts along dimension 0
The draws below stay inside these ranges and needn't reach their ends.
There are 2 independent parts, one for each index of `clip`. The reference program is written for one: setup_inputs(seed, part) draws one part's arguments, and reference() takes and returns one part's arrays. A program takes and returns all parts, laid end to end along the dimension named above; an argument that names none is the same for every part. Nothing has to cross between parts.
Inputs may be any that keep to these rules, and one draw needn't show every extreme that they name: `slot_levels`: strictly rising along the queue; neighbouring slots differ by 1 or 2; the last slot holds 15.
All inputs are finite; a program needn't handle non-finite values.
Results may differ from the reference program's by a relative error of at most 0.0023.
Values may be sent and summed in bfloat16 or wider, within the bound.
No kernel may reach another device: no remote copies, remote signals or barrier semaphores. Data moves between devices by JAX's collectives and lax.ppermute only.
A program may use at most 128 MiB of HBM per device.

```python
import math
import jax
import jax.numpy as jnp
from jax import lax

D = 1152
HEADS = 8
HD = 72
CH = 16
QUEUE = 8
FRAMES = 2
STEPS = 3
LEVELS = 16
SPACE_TOK = 128


def draw_slot_levels(key, part):
    gap_key = jax.random.fold_in(key, 11)
    gaps = jax.random.randint(gap_key, (QUEUE - 1,), 1, 3).astype(jnp.int32)
    above = jnp.cumsum(gaps[::-1])[::-1]
    top = jnp.full((1,), LEVELS - 1, jnp.int32)
    return jnp.concatenate([LEVELS - 1 - above, top]).astype(jnp.int32)


def steps_of(rng, extent, cuts, smallest, high):
    factor_of, own = 1.0, jax.random.fold_in(rng, 6)
    for position, blocks in cuts:
        draws = jnp.exp(jax.random.uniform(jax.random.fold_in(own, position), (blocks,), jnp.float32, smallest / len(cuts), high / len(cuts)))
        factor_of = factor_of * jnp.repeat(draws, extent[position] // blocks).reshape([-1 if axis == position else 1 for axis in range(len(extent))])
    return factor_of


def bell_draw(rng, dims, deviation, most, cuts=(), kind=jnp.bfloat16):
    values = jax.random.normal(rng, dims, jnp.float32) * deviation
    if len(cuts) > 0:
        values = steps_of(rng, dims, cuts, -0.22, 0.18) * values
    return jnp.clip(values, min=-most, max=most).astype(kind)


def setup_inputs(seed: int = 0, part: int = 0) -> dict:
    key_list = jax.random.split(jax.random.key(seed), 12)
    part_splits = jax.random.split(jax.random.fold_in(key_list[11], part), 12)
    queue_latents = bell_draw(part_splits[0], (QUEUE, FRAMES, CH, SPACE_TOK), 1.0, 6.0, ((0, 2), (3, 8)), jnp.float32)
    fresh_noise = bell_draw(part_splits[1], (STEPS, FRAMES, CH, SPACE_TOK), 1.0, 6.0, ((3, 8),), jnp.float32)
    slot_levels = draw_slot_levels(jax.random.fold_in(jax.random.fold_in(key_list[11], part), 71), part)
    level_table = bell_draw(key_list[3], (LEVELS, 8, D), 0.5, 2.5, (), jnp.float32)
    embed_weight = bell_draw(key_list[4], (CH, D), CH ** -0.5, 1.5, (), jnp.float32)
    spatial_in = bell_draw(key_list[5], (D, 3 * HEADS * HD), D ** -0.5, 0.1875)
    spatial_out = bell_draw(key_list[6], (HEADS * HD, D), (HEADS * HD) ** -0.5, 0.25)
    temporal_in = bell_draw(key_list[7], (D, 3 * HEADS * HD), D ** -0.5, 0.1875)
    temporal_out = bell_draw(key_list[8], (HEADS * HD, D), (HEADS * HD) ** -0.5, 0.25)
    norm_gains = jnp.clip(1.0 + 0.18 * jax.random.normal(key_list[9], (4, HD), jnp.float32), 0.1, 1.9)
    final_weight = bell_draw(key_list[10], (D, CH), D ** -0.5, 0.1875, (), jnp.float32)
    return dict(queue_latents=queue_latents, fresh_noise=fresh_noise, slot_levels=slot_levels, level_table=level_table, embed_weight=embed_weight, spatial_in=spatial_in, spatial_out=spatial_out, temporal_in=temporal_in, temporal_out=temporal_out, norm_gains=norm_gains, final_weight=final_weight)


epsilon = 1e-06
highest = lax.Precision.HIGHEST

def sincos(positions, width):
    half = width // 2
    rates = jnp.exp(-jnp.log(10000.0) * jnp.arange(half).astype(jnp.float32) / half)
    angles = positions.astype(jnp.float32)[:, None] * rates[None, :]
    return jnp.concatenate([jnp.sin(angles), jnp.cos(angles)], axis=-1)

def stored(values):
    return lax.optimization_barrier(values.astype(jnp.bfloat16))

def layer_norm(values):
    centered = values - lax.optimization_barrier(jnp.mean(values, axis=-1, keepdims=True))
    return centered * lax.rsqrt(lax.optimization_barrier(jnp.mean(centered * centered, axis=-1, keepdims=True)) + epsilon)

def modulate(hidden, table, shift_row, scale_row):
    shift = table[:, shift_row][:, None, None, :]
    scale = table[:, scale_row][:, None, None, :]
    return layer_norm(hidden) * (1.0 + scale) + shift

def head_norm(values, gain):
    values = values.astype(jnp.float32)
    scaled = values * lax.rsqrt(lax.optimization_barrier(jnp.mean(values * values, axis=-1, keepdims=True)) + epsilon)
    return stored(scaled * gain)

def project_heads(normed, weight, gains, first):
    projected = stored(jnp.dot(normed.reshape(-1, D), weight, preferred_element_type=jnp.float32))
    projected = projected.reshape(QUEUE * FRAMES, SPACE_TOK, 3, HEADS, HD)
    queries = head_norm(projected[:, :, 0], gains[first])
    keys = head_norm(projected[:, :, 1], gains[first + 1])
    return (queries, keys, projected[:, :, 2])

def spatial_frame(pieces):
    queries, keys, values = pieces
    scores = jnp.einsum('the,rhe->htr', queries.astype(jnp.float32), keys.astype(jnp.float32)) / math.sqrt(HD)
    weights = jnp.exp(scores)
    totals = lax.optimization_barrier(jnp.sum(weights, axis=-1))
    rounded = stored(weights).astype(jnp.float32)
    mixed = jnp.einsum('htr,rhe->the', rounded, values.astype(jnp.float32))
    return stored(mixed / jnp.transpose(totals)[:, :, None])

def temporal_mix(queries, keys, values):
    scores = jnp.einsum('fthe,gthe->thfg', queries.astype(jnp.float32), keys.astype(jnp.float32)) / math.sqrt(HD)
    weights = jnp.exp(scores)
    totals = jnp.transpose(lax.optimization_barrier(jnp.sum(weights, axis=-1)), (2, 0, 1))
    rounded = stored(weights).astype(jnp.float32)
    mixed = jnp.einsum('thfg,gthe->fthe', rounded, values.astype(jnp.float32))
    return stored(mixed / totals[..., None])

def denoise(latents, table, token_pos, frame_pos, embed_weight, spatial_in, spatial_out, temporal_in, temporal_out, norm_gains, final_weight):
    hidden = jnp.einsum('qfcp,cd->qfpd', latents, embed_weight, precision=highest) + token_pos
    normed = stored(modulate(hidden, table, 0, 1))
    queries, keys, values = project_heads(normed, spatial_in, norm_gains, 0)
    mixed = lax.map(spatial_frame, (queries, keys, values))
    branch = jnp.dot(mixed.reshape(-1, HEADS * HD), spatial_out, preferred_element_type=jnp.float32)
    hidden = hidden + table[:, 2][:, None, None, :] * branch.reshape(hidden.shape) + frame_pos
    normed = stored(modulate(hidden, table, 3, 4))
    queries, keys, values = project_heads(normed, temporal_in, norm_gains, 2)
    mixed = temporal_mix(queries, keys, values)
    branch = jnp.dot(mixed.reshape(-1, HEADS * HD), temporal_out, preferred_element_type=jnp.float32)
    hidden = hidden + table[:, 5][:, None, None, :] * branch.reshape(hidden.shape)
    final = modulate(hidden, table, 6, 7)
    return jnp.einsum('qfpd,dc->qfcp', final, final_weight, precision=highest)

def reference(queue_latents, fresh_noise, slot_levels, level_table, embed_weight, spatial_in, spatial_out, temporal_in, temporal_out, norm_gains, final_weight):
    times = (slot_levels.astype(jnp.float32) + 1.0) / LEVELS
    before = jnp.concatenate([jnp.zeros((1,), jnp.float32), times[:-1]])
    stride = times - before
    table = level_table[slot_levels]
    token_pos = sincos(jnp.arange(SPACE_TOK), D)
    frame_pos = sincos(jnp.arange(QUEUE * FRAMES), D).reshape(QUEUE, FRAMES, 1, D)
    latents = queue_latents
    denoised = latents
    for step in range(STEPS):
        velocity = denoise(latents, table, token_pos, frame_pos, embed_weight, spatial_in, spatial_out, temporal_in, temporal_out, norm_gains, final_weight)
        denoised = latents - times[:, None, None, None] * velocity
        moved = latents - stride[:, None, None, None] * velocity
        latents = jnp.concatenate([moved[1:], fresh_noise[step][None]], axis=0)
    return (latents, denoised)
```

```python
import functools
import math

import jax
import jax.numpy as jnp
import numpy as np
from jax import lax
from jax.experimental import pallas as pl
from jax.experimental.pallas import tpu as pltpu
from jax.sharding import PartitionSpec as P

D = 1152
HEADS = 8
HD = 72
INNER = HEADS * HD
CH = 16
FRAMES = 2
STEPS = 3
LEVELS = 16

LANES = 128
SHIFT = (-INNER) % LANES
WIDE = INNER + SHIFT
PIECE = 32
PACK = LANES // PIECE

epsilon = 1e-06
f32 = jnp.float32
bf16 = jnp.bfloat16


def dot(a, b):
    return lax.dot_general(a, b, (((1,), (0,)), ((), ())), preferred_element_type=f32)


def dot_nt(a, b):
    return lax.dot_general(a, b, (((1,), (1,)), ((), ())), preferred_element_type=f32)


def split(x):
    high = x.astype(bf16)
    return high, (x - high.astype(f32)).astype(bf16)


def sincos(count, width):
    half = width // 2
    rates = np.exp(-np.log(10000.0) * np.arange(half) / half)
    angles = np.arange(count)[:, None] * rates[None, :]
    return np.concatenate([np.sin(angles), np.cos(angles)], axis=-1)


def head_of_lane(shape, axis, shift):
    position = lax.broadcasted_iota(jnp.int32, shape, axis) - shift
    return position


def in_head(shape, axis, shift, head):
    position = lax.broadcasted_iota(jnp.int32, shape, axis) - shift
    return (position >= head * HD) & (position < (head + 1) * HD)


def head_masks(width, shift):
    shape = (HEADS, 1, width)
    head = lax.broadcasted_iota(jnp.int32, shape, 0)
    position = lax.broadcasted_iota(jnp.int32, shape, 2) - shift
    return ((position >= head * HD) & (position < (head + 1) * HD)).astype(f32)


def normalized(values):
    centered = values - jnp.mean(values, axis=-1, keepdims=True)
    return centered * lax.rsqrt(jnp.mean(centered * centered, axis=-1, keepdims=True) + epsilon)


def modulated(values, shift, scale, rows):
    slots = shift.shape[0]
    out = values.reshape(slots, -1, D) * (1.0 + scale)[:, None, :] + shift[:, None, :]
    return out.reshape(values.shape)


def own_hidden(lat, embed, pos_own, lanes):
    lat_high, lat_low = split(lat)
    stacked = jnp.concatenate(
        [lat_high.astype(f32), lat_low.astype(f32), lat_high.astype(f32), jnp.zeros((lanes - 3 * CH, lanes), f32)], axis=0
    )
    rows = stacked.T.astype(bf16)
    embed_high, embed_low = split(embed)
    weights = jnp.concatenate(
        [embed_high, embed_high, embed_low, jnp.zeros((lanes - 3 * CH, D), bf16)], axis=0
    )
    out = dot(rows, weights)
    own = pos_own.shape[0]
    return (out.reshape(lanes // own, own, D) + pos_own[None]).reshape(lanes, D)


def make_piece(lat, embed, pos_own, lanes):
    hidden = own_hidden(lat, embed, pos_own, lanes)
    centered = hidden - jnp.mean(hidden, axis=-1, keepdims=True)
    deviation = jnp.sqrt(jnp.mean(centered * centered, axis=-1, keepdims=True) + epsilon)
    row = jnp.broadcast_to(deviation, (lanes, LANES)).T[:1]
    high, low = split(row)
    return jnp.concatenate(
        [
            lat,
            high.astype(f32),
            high.astype(f32),
            low.astype(f32),
            jnp.zeros((PIECE - CH - 3, lanes), f32),
        ],
        axis=0,
    ).astype(bf16)


def first_kernel(lat_ref, embed_ref, pos_ref, piece_ref):
    lanes = lat_ref.shape[1]
    piece = make_piece(lat_ref[...], embed_ref[...], pos_ref[...], lanes)
    for peer in range(piece_ref.shape[0]):
        piece_ref[peer] = piece


def prepare_kernel(levels_ref, table_ref, pos_ref, embed_ref, weight_ref, gains_ref, plan_ref, mods_ref, gain_rows_ref):
    slot = pl.program_id(1)
    rows = table_ref[levels_ref[slot]]
    mods_ref[0] = rows
    scale = 1.0 + rows[1:2]
    embed = embed_ref[...]
    embed = embed - jnp.mean(embed, axis=-1, keepdims=True)
    pos = pos_ref[...]
    pos = pos - jnp.mean(pos, axis=-1, keepdims=True)
    left = jnp.concatenate(
        [pos * scale, embed * scale, rows[0:1], jnp.zeros((CH - 1, D), f32)], axis=0
    ).astype(bf16)
    product = dot(left, weight_ref[:, INNER - SHIFT :])
    tokens = pos.shape[0]
    plan_ref[0, 0, :tokens] = product[:tokens].astype(bf16)
    shift_row = product[tokens + CH : tokens + CH + 1]
    high, low = split(shift_row)
    group = jnp.concatenate(
        [
            product[tokens : tokens + CH],
            high.astype(f32),
            low.astype(f32),
            high.astype(f32),
            jnp.zeros((PIECE - CH - 3, product.shape[1]), f32),
        ],
        axis=0,
    ).astype(bf16)
    for copy in range(PACK):
        plan_ref[0, 0, tokens + copy * PIECE : tokens + (copy + 1) * PIECE] = group

    @pl.when((pl.program_id(0) == 0) & (slot == 0))
    def _():
        gains = gains_ref[...]
        products = jnp.concatenate(
            [gains[0:1] * gains[1:2], gains[2:3] * gains[3:4], jnp.zeros((6, HD), f32)], axis=0
        ) / math.sqrt(HD)
        place = lax.broadcasted_iota(jnp.int32, (HD, WIDE), 1) - SHIFT
        feature = lax.broadcasted_iota(jnp.int32, (HD, WIDE), 0)
        spread = ((place >= 0) & (lax.rem(place + HD, HD) == feature)).astype(f32)
        gain_rows_ref[...] = lax.dot_general(
            products, spread, (((1,), (0,)), ((), ())), preferred_element_type=f32, precision=lax.Precision.HIGHEST
        )


def step_kernel(
    levels_ref,
    pieces_ref,
    lat_ref,
    noise_ref,
    embed_ref,
    pos_own_ref,
    pos_frame_ref,
    mods_ref,
    gain_rows_ref,
    same_head_ref,
    final_ref,
    plan_hbm,
    spatial_in_hbm,
    spatial_out_hbm,
    temporal_in_hbm,
    temporal_out_hbm,
    *refs,
    last,
):
    if last:
        lat_out, denoised_out = refs[:2]
        refs = refs[2:]
    else:
        lat_out, piece_out = refs[:2]
        refs = refs[2:]
    plan_ref, wq_ref, wso_ref, wti_ref, wto_ref, cross_ref, mixed_ref, plan_sem, weight_sem = refs
    lanes = lat_ref.shape[1]
    blocks, slots = plan_hbm.shape[:2]
    frames = slots * FRAMES
    own = lanes // frames
    devices = pieces_ref.shape[0]
    tokens = LANES
    per_block = devices // blocks

    weight_copies = [
        pltpu.make_async_copy(spatial_in_hbm.at[:, :WIDE], wq_ref, weight_sem.at[0]),
        pltpu.make_async_copy(spatial_out_hbm, wso_ref, weight_sem.at[1]),
        pltpu.make_async_copy(temporal_in_hbm, wti_ref, weight_sem.at[2]),
        pltpu.make_async_copy(temporal_out_hbm, wto_ref, weight_sem.at[3]),
    ]
    plan_copies = [
        [pltpu.make_async_copy(plan_hbm.at[b, q], plan_ref.at[b, q], plan_sem.at[b, q]) for q in range(slots)]
        for b in range(blocks)
    ]
    weight_copies[0].start()
    for b in range(blocks):
        for q in range(slots):
            plan_copies[b][q].start()
    for copy in weight_copies[1:]:
        copy.start()

    lat = lat_ref[...]
    embed = embed_ref[...]
    pos_own = pos_own_ref[...]
    mods = [mods_ref[:, row] for row in range(8)]
    same_head = same_head_ref[...]

    def head_normed(values, gain):
        total = dot((values * values).astype(bf16), same_head)
        return values * lax.rsqrt(total * (1.0 / HD) + epsilon) * gain

    hidden = own_hidden(lat, embed, pos_own, lanes)
    normed = modulated(normalized(hidden), mods[0], mods[1], own).astype(bf16)
    weight_copies[0].wait()
    queries = dot(normed, wq_ref[...]).astype(bf16).astype(f32)
    queries = head_normed(pltpu.roll(queries, SHIFT, 1), gain_rows_ref[0:1])

    for group in range(devices // PACK):
        stacked = pieces_ref[group * PACK : (group + 1) * PACK].astype(f32).reshape(LANES, lanes)
        cross_ref[group] = stacked.T
    lane = lax.broadcasted_iota(jnp.int32, (PACK, 1, LANES), 2)
    part = lax.broadcasted_iota(jnp.int32, (PACK, 1, LANES), 0)
    pack_mask = (lane // PIECE == part).astype(f32)
    row = lax.broadcasted_iota(jnp.int32, (2 * tokens, tokens), 0)
    column = lax.broadcasted_iota(jnp.int32, (2 * tokens, tokens), 1)
    identity = (lax.rem(row, tokens) == column).astype(bf16)
    place = lax.rem(lax.broadcasted_iota(jnp.int32, (8, LANES), 1), PIECE)
    deviation_lanes = ((place == CH + 1) | (place == CH + 2)).astype(bf16)
    masks = head_masks(WIDE, SHIFT)
    value_masks = head_masks(INNER, 0)
    head_rows = masks.reshape(HEADS, WIDE).astype(bf16)

    for q in range(slots):
        totals = [0.0] * FRAMES
        sums = [0.0] * FRAMES
        for b in range(blocks):
            turned = []
            for f in range(FRAMES):
                g = q * FRAMES + f
                tiles = []
                for group in range(per_block // PACK):
                    tile = cross_ref[b * (per_block // PACK) + group, g * own : (g + 1) * own]
                    tiles.append((tile[None] * pack_mask).reshape(PACK * own, LANES))
                turned.append(jnp.concatenate(tiles, axis=0).astype(bf16))
            left = jnp.concatenate([identity, jnp.concatenate(turned, axis=0)], axis=1)
            plan_copies[b][q].wait()
            product = dot(left, plan_ref[b, q])
            keys = product[:, :WIDE]
            values = product[:, WIDE:].astype(bf16)
            squares = (keys * keys).astype(bf16)
            keys = keys.astype(bf16)
            for f in range(FRAMES):
                g = q * FRAMES + f
                at = slice(f * tokens, (f + 1) * tokens)
                deviation = dot_nt(deviation_lanes, turned[f])
                key_scale = lax.rsqrt(
                    dot_nt(head_rows, squares[at]) * (1.0 / HD) + epsilon * deviation * deviation
                )
                own_queries = queries[g * own : (g + 1) * own]
                spread = (own_queries[None] * masks).reshape(HEADS * own, WIDE).astype(bf16)
                scores = dot_nt(spread, keys[at]).reshape(HEADS, own, tokens) * key_scale[:, None, :]
                weights = jnp.exp(scores)
                totals[f] = totals[f] + jnp.sum(weights, axis=-1, keepdims=True)
                scaled = (weights * (1.0 / deviation[:own])[None]).reshape(HEADS * own, tokens).astype(bf16)
                sums[f] = sums[f] + dot(scaled, values[at])
        for f in range(FRAMES):
            g = q * FRAMES + f
            result = sums[f].reshape(HEADS, own, INNER) * (1.0 / totals[f])
            mixed_ref[g * own : (g + 1) * own] = jnp.sum(result * value_masks, axis=0)

    weight_copies[1].wait()
    branch = dot(mixed_ref[...].astype(bf16), wso_ref[...])
    hidden = (
        hidden.reshape(slots, FRAMES, own, D)
        + mods[2][:, None, None, :] * branch.reshape(slots, FRAMES, own, D)
        + pos_frame_ref[...].reshape(slots, FRAMES, 1, D)
    ).reshape(lanes, D)
    normed = modulated(normalized(hidden), mods[3], mods[4], own).astype(bf16)
    weight_copies[2].wait()
    projected = dot(normed, wti_ref[...])
    values = projected[:, 2 * INNER :].astype(bf16)
    queries = projected[:, :WIDE].astype(bf16).astype(f32)
    keys = projected[:, INNER - SHIFT : 2 * INNER].astype(bf16).astype(f32)
    queries = head_normed(pltpu.roll(queries, SHIFT, 1), gain_rows_ref[1:2])
    keys = head_normed(keys, 1.0).astype(bf16)
    row = lax.broadcasted_iota(jnp.int32, (lanes, lanes), 0)
    column = lax.broadcasted_iota(jnp.int32, (lanes, lanes), 1)
    same_token = (lax.rem(row, own) == lax.rem(column, own)).astype(f32)
    tiles = -(-INNER // LANES)
    parts = [None] * tiles
    for h in range(HEADS):
        low, high = SHIFT + h * HD, SHIFT + (h + 1) * HD
        start, stop = low // LANES * LANES, -(-high // LANES) * LANES
        spread = (queries[:, start:stop] * masks[h, :, start:stop]).astype(bf16)
        weights = jnp.exp(dot_nt(spread, keys[:, start:stop])) * same_token
        total = jnp.sum(weights, axis=-1, keepdims=True)
        weights = weights.astype(bf16)
        start, stop = h * HD // LANES * LANES, min(-(-(h + 1) * HD // LANES) * LANES, INNER)
        result = dot(weights, values[:, start:stop]) * (1.0 / total) * value_masks[h, :, start:stop]
        for tile in range(start // LANES, -(-stop // LANES)):
            piece = result[:, tile * LANES - start : min((tile + 1) * LANES, stop) - start]
            parts[tile] = piece if parts[tile] is None else parts[tile] + piece
    mixed = jnp.concatenate([p.astype(bf16) for p in parts], axis=1)
    weight_copies[3].wait()
    branch = dot(mixed, wto_ref[...])
    hidden = hidden + (mods[5][:, None, :] * branch.reshape(slots, FRAMES * own, D)).reshape(lanes, D)
    final = modulated(normalized(hidden), mods[6], mods[7], own)
    final_high, final_low = split(final)
    weight_high, weight_low = split(final_ref[...])
    velocity = dot_nt(weight_high, final_high) + dot_nt(weight_low, final_high) + dot_nt(weight_high, final_low)

    slot = lax.broadcasted_iota(jnp.int32, (1, lanes), 1) // (FRAMES * own)
    times = jnp.zeros((1, lanes), f32)
    stride = jnp.zeros((1, lanes), f32)
    before = 0.0
    for q in range(slots):
        time = (levels_ref[q].astype(f32) + 1.0) / LEVELS
        times = jnp.where(slot == q, time, times)
        stride = jnp.where(slot == q, time - before, stride)
        before = time
    moved = pltpu.roll(lat - stride * velocity, lanes - FRAMES * own, 1)
    moved = jnp.where(slot == slots - 1, noise_ref[...], moved)
    lat_out[...] = moved
    if last:
        denoised_out[...] = lat - times * velocity
    else:
        piece = make_piece(moved, embed, pos_own, lanes)
        for peer in range(devices):
            piece_out[peer] = piece


def per_device(
    queue_latents,
    fresh_noise,
    slot_levels,
    level_table,
    embed_weight,
    spatial_in,
    spatial_out,
    temporal_in,
    temporal_out,
    norm_gains,
    final_weight,
):
    blocks, frames_in, channels, tokens = queue_latents.shape
    section = lax.axis_index("tm")
    sections = lax.axis_size("tm")
    shards = lax.axis_size("space")
    axes = ("space", "tm")
    devices = sections * shards
    own = tokens // sections
    slots = blocks * sections
    frames = slots * FRAMES
    lanes = frames * own
    space_tokens = tokens * shards
    token_blocks = space_tokens // LANES

    pos = sincos(space_tokens, D).astype(np.float32)
    pos_frame = sincos(frames, D).astype(np.float32)
    place = np.arange(WIDE) - SHIFT
    head = np.where(place >= 0, place // HD, -1)
    same_head = jnp.asarray(((head[:, None] == head[None, :]) & (head >= 0)[None, :]).astype(np.float32), bf16)

    def exchanged(values):
        parts = values.reshape(*values.shape[:-1], sections, own)
        return lax.all_to_all(parts, "tm", split_axis=parts.ndim - 2, concat_axis=0, tiled=False)

    lat = exchanged(queue_latents.reshape(blocks * FRAMES, CH, tokens))
    lat = jnp.transpose(lat, (2, 0, 1, 3)).reshape(CH, lanes)
    noise = lax.dynamic_slice_in_dim(fresh_noise, section * own, own, axis=3)
    noise = jnp.transpose(noise, (0, 2, 1, 3)).reshape(STEPS, CH, FRAMES * own)
    noise = jnp.pad(noise, ((0, 0), (0, 0), (lanes - FRAMES * own, 0)))
    first_token = lax.axis_index("space") * tokens + section * own
    pos_own = lax.dynamic_slice_in_dim(jnp.asarray(pos), first_token, own)
    final_turned = jnp.transpose(final_weight)

    vmem = pl.BlockSpec(memory_space=pltpu.VMEM)
    smem = pl.BlockSpec(memory_space=pltpu.SMEM)
    anywhere = pl.BlockSpec(memory_space=pl.ANY)
    pieces = pl.pallas_call(
        first_kernel,
        out_shape=jax.ShapeDtypeStruct((devices, PIECE, lanes), bf16),
        in_specs=[vmem] * 3,
        out_specs=vmem,
        name="first_piece",
    )(lat, embed_weight, pos_own)

    plan_rows = 2 * LANES
    plan_columns = 3 * INNER - (INNER - SHIFT)
    plan, mods, gain_rows = pl.pallas_call(
        prepare_kernel,
        grid_spec=pltpu.PrefetchScalarGridSpec(
            num_scalar_prefetch=1,
            grid=(token_blocks, slots),
            in_specs=[
                pl.BlockSpec((LEVELS, 8, D), lambda b, q, levels: (0, 0, 0)),
                pl.BlockSpec((LANES, D), lambda b, q, levels: (b, 0)),
                pl.BlockSpec((CH, D), lambda b, q, levels: (0, 0)),
                pl.BlockSpec((D, 3 * INNER), lambda b, q, levels: (0, 0)),
                pl.BlockSpec((4, HD), lambda b, q, levels: (0, 0)),
            ],
            out_specs=[
                pl.BlockSpec((1, 1, plan_rows, plan_columns), lambda b, q, levels: (b, q, 0, 0)),
                pl.BlockSpec((1, 8, D), lambda b, q, levels: (q, 0, 0)),
                pl.BlockSpec((8, WIDE), lambda b, q, levels: (0, 0)),
            ],
        ),
        out_shape=[
            jax.ShapeDtypeStruct((token_blocks, slots, plan_rows, plan_columns), bf16),
            jax.ShapeDtypeStruct((slots, 8, D), f32),
            jax.ShapeDtypeStruct((8, WIDE), f32),
        ],
        compiler_params=pltpu.CompilerParams(vmem_limit_bytes=32 * 1024 * 1024),
        name="slot_plan",
    )(slot_levels, level_table, jnp.asarray(pos), embed_weight, spatial_in, norm_gains)

    denoised = lat
    for step in range(STEPS):
        last = step == STEPS - 1
        gathered = lax.all_to_all(pieces, axes, split_axis=0, concat_axis=0, tiled=True)
        out_shape = [jax.ShapeDtypeStruct((CH, lanes), f32)]
        if last:
            out_shape.append(jax.ShapeDtypeStruct((CH, lanes), f32))
        else:
            out_shape.append(jax.ShapeDtypeStruct((devices, PIECE, lanes), bf16))
        lat, other = pl.pallas_call(
            functools.partial(step_kernel, last=last),
            out_shape=out_shape,
            in_specs=[smem] + [vmem] * 10 + [anywhere] * 5,
            out_specs=[vmem] * 2,
            scratch_shapes=[
                pltpu.VMEM((token_blocks, slots, plan_rows, plan_columns), bf16),
                pltpu.VMEM((D, WIDE), bf16),
                pltpu.VMEM((INNER, D), bf16),
                pltpu.VMEM((D, 3 * INNER), bf16),
                pltpu.VMEM((INNER, D), bf16),
                pltpu.VMEM((devices // PACK, lanes, LANES), f32),
                pltpu.VMEM((lanes, INNER), f32),
                pltpu.SemaphoreType.DMA((token_blocks, slots)),
                pltpu.SemaphoreType.DMA((4,)),
            ],
            compiler_params=pltpu.CompilerParams(vmem_limit_bytes=50 * 1024 * 1024),
            name="denoise_step",
        )(
            slot_levels,
            gathered,
            lat,
            noise[step],
            embed_weight,
            pos_own,
            jnp.asarray(pos_frame),
            mods,
            gain_rows,
            same_head,
            final_turned,
            plan,
            spatial_in,
            spatial_out,
            temporal_in,
            temporal_out,
        )
        if last:
            denoised = other
        else:
            pieces = other

    results = jnp.stack([lat, denoised]).reshape(2, CH, sections, blocks, FRAMES, own)
    results = lax.all_to_all(results, "tm", split_axis=2, concat_axis=0, tiled=False)
    results = jnp.transpose(results, (1, 3, 4, 2, 0, 5)).reshape(2, blocks, FRAMES, CH, tokens)
    return (results[0], results[1])


def solution(mesh):
    return jax.shard_map(
        per_device,
        mesh=mesh,
        in_specs=(
            P(("clip", "tm"), None, None, "space"),
            P("clip", None, None, "space"),
            P("clip"),
            P(),
            P(),
            P(),
            P(),
            P(),
            P(),
            P(),
            P(),
        ),
        out_specs=(P(("clip", "tm"), None, None, "space"), P(("clip", "tm"), None, None, "space")),
        check_vma=False,
    )
```

```python
import functools
import math

import jax
import jax.numpy as jnp
import numpy as np
from jax import lax
from jax.experimental import pallas as pl
from jax.experimental.pallas import tpu as pltpu
from jax.sharding import PartitionSpec as P

D = 1152
HEADS = 8
HD = 72
INNER = HEADS * HD
CH = 16
FRAMES = 2
STEPS = 3
LEVELS = 16

LANES = 128
WIDE = -(-INNER // LANES) * LANES
PIECE = 32
PACK = LANES // PIECE
PLAN = 2 * LANES

epsilon = 1e-06
f32 = jnp.float32
bf16 = jnp.bfloat16


def dot(a, b):
    return lax.dot_general(a, b, (((1,), (0,)), ((), ())), preferred_element_type=f32)


def dot_nt(a, b):
    return lax.dot_general(a, b, (((1,), (1,)), ((), ())), preferred_element_type=f32)


def split(x):
    high = x.astype(bf16)
    return high, (x - high.astype(f32)).astype(bf16)


def sincos(count, width):
    half = width // 2
    rates = np.exp(-np.log(10000.0) * np.arange(half) / half)
    angles = np.arange(count)[:, None] * rates[None, :]
    return np.concatenate([np.sin(angles), np.cos(angles)], axis=-1)


def head_masks():
    shape = (HEADS, 1, WIDE)
    head = lax.broadcasted_iota(jnp.int32, shape, 0)
    position = lax.broadcasted_iota(jnp.int32, shape, 2)
    return ((position >= head * HD) & (position < (head + 1) * HD)).astype(f32)


def normalized(values):
    centered = values - jnp.mean(values, axis=-1, keepdims=True)
    return centered * lax.rsqrt(jnp.mean(centered * centered, axis=-1, keepdims=True) + epsilon)


def modulated(values, shift, scale):
    slots = shift.shape[0]
    out = values.reshape(slots, -1, D) * (1.0 + scale)[:, None, :] + shift[:, None, :]
    return out.reshape(values.shape)


def own_hidden(lat, embed, pos_own):
    lanes = lat.shape[1]
    lat_high, lat_low = split(lat)
    lat_high = lat_high.astype(f32)
    zeros = jnp.zeros((LANES - 3 * CH, lanes), f32)
    rows = jnp.concatenate([lat_high, lat_low.astype(f32), lat_high, zeros], axis=0).T.astype(bf16)
    embed_high, embed_low = split(embed)
    weights = jnp.concatenate(
        [embed_high, embed_high, embed_low, jnp.zeros((LANES - 3 * CH, D), bf16)], axis=0
    )
    own = pos_own.shape[0]
    return (dot(rows, weights).reshape(lanes // own, own, D) + pos_own[None]).reshape(lanes, D)


def make_piece(lat, embed, pos_own):
    lanes = lat.shape[1]
    hidden = own_hidden(lat, embed, pos_own)
    centered = hidden - jnp.mean(hidden, axis=-1, keepdims=True)
    deviation = jnp.sqrt(jnp.mean(centered * centered, axis=-1, keepdims=True) + epsilon)
    row = jnp.broadcast_to(deviation, (lanes, LANES)).T[:1]
    high, low = split(row)
    high = high.astype(f32)
    zeros = jnp.zeros((PIECE - CH - 3, lanes), f32)
    return jnp.concatenate([lat, high, high, low.astype(f32), zeros], axis=0).astype(bf16)


def placed(block, start):
    rows, width = block.shape
    wide = jnp.concatenate([block, jnp.zeros((rows, LANES - width), f32)], axis=1)
    return pltpu.roll(wide, start, 1) if start else wide


def start_all(copies):
    for copy in copies:
        copy.start()


def first_kernel(queue_ref, embed_hbm, pos_hbm, piece_ref, keep_ref, send_ref, embed_ref, pos_ref, sems):
    frames, _, tokens = queue_ref.shape
    shard, section = lax.axis_index("space"), lax.axis_index("tm")
    first = pl.multiple_of(shard * tokens, 8)
    copies = [
        pltpu.make_async_copy(embed_hbm, embed_ref, sems.at[0]),
        pltpu.make_async_copy(pos_hbm.at[pl.ds(first, tokens)], pos_ref, sems.at[1]),
    ]
    start_all(copies)
    own = tokens // 2
    lat = jnp.zeros((CH, LANES), f32)
    halves = [jnp.zeros((CH, LANES), f32) for _ in range(2)]
    for g in range(frames):
        block = queue_ref[g]
        lat = lat + placed(block, g * tokens)
        for half in range(2):
            halves[half] = halves[half] + placed(block[:, half * own : (half + 1) * own], g * own)
    low = section == 0
    keep_ref[...] = jnp.where(low, halves[0], pltpu.roll(halves[1], frames * own, 1))
    send_ref[...] = jnp.where(low, halves[1], pltpu.roll(halves[0], frames * own, 1))
    for copy in copies:
        copy.wait()
    piece = make_piece(lat, embed_ref[...], pos_ref[...])
    for peer in range(piece_ref.shape[0]):
        piece_ref[peer] = piece


def prepare_kernel(
    levels_ref,
    table_hbm,
    pos_hbm,
    embed_hbm,
    gains_hbm,
    weight_hbm,
    key_plan_hbm,
    value_plan_hbm,
    mods_hbm,
    gain_rows_hbm,
    mods_ref,
    pos_ref,
    embed_ref,
    gains_ref,
    weight_ref,
    left_ref,
    key_plan_ref,
    value_plan_ref,
    gain_rows_ref,
    sems,
    out_sems,
):
    blocks, slots = key_plan_hbm.shape[:2]
    tokens = LANES
    copies = [pltpu.make_async_copy(table_hbm.at[levels_ref[q]], mods_ref.at[q], sems.at[q]) for q in range(slots)]
    copies += [
        pltpu.make_async_copy(pos_hbm, pos_ref, sems.at[slots]),
        pltpu.make_async_copy(embed_hbm, embed_ref, sems.at[slots + 1]),
        pltpu.make_async_copy(gains_hbm, gains_ref, sems.at[slots + 2]),
    ]
    weight_copies = [
        pltpu.make_async_copy(
            weight_hbm.at[(1 + i) * INNER : (2 + i) * INNER],
            weight_ref.at[i * INNER : (i + 1) * INNER],
            sems.at[slots + 3 + i],
        )
        for i in range(2)
    ]
    start_all(copies)
    start_all(weight_copies)
    for copy in copies:
        copy.wait()
    outs = [pltpu.make_async_copy(mods_ref, mods_hbm, out_sems.at[0])]
    outs[0].start()

    gains = gains_ref[...]
    products = jnp.concatenate(
        [gains[0:1] * gains[1:2], gains[2:3] * gains[3:4], jnp.zeros((6, HD), f32)], axis=0
    ) / math.sqrt(HD)
    place = lax.broadcasted_iota(jnp.int32, (HD, WIDE), 1)
    feature = lax.broadcasted_iota(jnp.int32, (HD, WIDE), 0)
    spread = ((place < INNER) & (lax.rem(place, HD) == feature)).astype(f32)
    gain_rows_ref[...] = lax.dot_general(
        products, spread, (((1,), (0,)), ((), ())), preferred_element_type=f32, precision=lax.Precision.HIGHEST
    )
    outs.append(pltpu.make_async_copy(gain_rows_ref, gain_rows_hbm, out_sems.at[1]))
    outs[1].start()

    embed = embed_ref[...]
    embed = embed - jnp.mean(embed, axis=-1, keepdims=True)
    shift_rows = jnp.zeros((PIECE - CH, D), f32)
    row = lax.broadcasted_iota(jnp.int32, (PIECE - CH, 1), 0)
    count = tokens + PIECE
    lane = lax.broadcasted_iota(jnp.int32, (1, PIECE), 1)
    plan_row = lax.broadcasted_iota(jnp.int32, (PLAN, LANES), 0)
    deviation_columns = ((plan_row == tokens + CH + 1) | (plan_row == tokens + CH + 2)).astype(bf16)
    for b in range(blocks):
        pos = pos_ref[b * tokens : (b + 1) * tokens]
        pos = pos - jnp.mean(pos, axis=-1, keepdims=True)
        for q in range(slots):
            scale = 1.0 + mods_ref[q, 1:2]
            shift_rows = jnp.where(row < 3, mods_ref[q, 0:1], 0.0)
            left_ref[q * count : (q + 1) * count] = jnp.concatenate(
                [pos * scale, embed * scale, shift_rows], axis=0
            ).astype(bf16)
        if b == 0:
            weight_copies[0].wait()
        product = dot_nt(left_ref[...], weight_ref[:INNER])
        part = lax.broadcasted_iota(jnp.int32, (PIECE, 1), 0)
        for q in range(slots):
            rows = product[q * count : (q + 1) * count]
            group = rows[tokens:]
            group = jnp.where(part == CH + 1, group - group.astype(bf16).astype(f32), group)
            key_plan_ref[b, q] = jnp.concatenate(
                [
                    jnp.concatenate(
                        [
                            rows[:tokens].astype(bf16),
                            group.astype(bf16),
                            jnp.zeros((PLAN - count, INNER), bf16),
                        ],
                        axis=0,
                    ),
                    jnp.zeros((PLAN, WIDE - INNER), bf16),
                    deviation_columns,
                ],
                axis=1,
            )
            copy = pltpu.make_async_copy(key_plan_ref.at[b, q], key_plan_hbm.at[b, q], out_sems.at[2 + b * slots + q])
            copy.start()
            outs.append(copy)
        if b == 0:
            weight_copies[1].wait()
        for q in range(slots):
            product = dot_nt(weight_ref[INNER:], left_ref[q * count : (q + 1) * count])
            group = product[:, tokens:]
            group = jnp.where(lane == CH + 1, group - group.astype(bf16).astype(f32), group)
            value_plan_ref[b, q] = jnp.concatenate(
                [
                    product[:, :tokens].astype(bf16),
                    jnp.concatenate([group.astype(bf16), jnp.zeros((INNER, PLAN - count), bf16)], axis=1),
                ],
                axis=1,
            )
            copy = pltpu.make_async_copy(
                value_plan_ref.at[b, q], value_plan_hbm.at[b, q], out_sems.at[2 + (blocks + b) * slots + q]
            )
            copy.start()
            outs.append(copy)
    for copy in outs:
        copy.wait()


def step_kernel(
    levels_ref,
    pieces_hbm,
    lat_hbm,
    more_hbm,
    noise_hbm,
    embed_hbm,
    pos_hbm,
    pos_frame_hbm,
    mods_hbm,
    gain_rows_hbm,
    same_head_hbm,
    head_sum_hbm,
    own_head_hbm,
    gather_hbm,
    final_hbm,
    key_plan_hbm,
    value_plan_hbm,
    wsi_hbm,
    wso_hbm,
    wti_hbm,
    wto_hbm,
    *refs,
    step,
):
    first, last = step == 0, step == STEPS - 1
    outs, refs = (refs[:2], refs[2:])
    (
        pieces_ref,
        lat_ref,
        more_ref,
        noise_ref,
        embed_ref,
        pos_own_ref,
        pos_frame_ref,
        mods_ref,
        gain_rows_ref,
        same_head_ref,
        head_sum_ref,
        own_head_ref,
        gather_ref,
        final_ref,
        key_plan_ref,
        value_plan_ref,
        wsi_ref,
        wso_ref,
        wti_ref,
        wto_ref,
        cross_ref,
        mixed_ref,
        sems,
        plan_sems,
    ) = refs
    lanes = lat_ref.shape[1]
    blocks, slots = key_plan_ref.shape[:2]
    frames = slots * FRAMES
    own = lanes // frames
    devices = pieces_ref.shape[0]
    tokens = LANES
    per_block = devices // blocks
    section, sections = lax.axis_index("tm"), lax.axis_size("tm")
    first_token = pl.multiple_of((lax.axis_index("space") * sections + section) * own, 8)

    pairs = [
        (lat_hbm, lat_ref),
        (more_hbm, more_ref),
        (embed_hbm, embed_ref),
        (pos_hbm.at[pl.ds(first_token, own)], pos_own_ref),
        (mods_hbm, mods_ref),
        (wsi_hbm.at[:WIDE], wsi_ref),
        (same_head_hbm, same_head_ref),
        (gain_rows_hbm, gain_rows_ref),
        (pieces_hbm, pieces_ref),
        (head_sum_hbm, head_sum_ref),
        (own_head_hbm, own_head_ref),
        (gather_hbm, gather_ref),
        (wso_hbm, wso_ref),
        (pos_frame_hbm, pos_frame_ref),
        (wti_hbm, wti_ref),
        (wto_hbm, wto_ref),
        (final_hbm, final_ref),
        (noise_hbm.at[step], noise_ref),
    ]
    copies = {}
    for i, (source, target) in enumerate(pairs):
        copies[id(target)] = pltpu.make_async_copy(source, target, sems.at[i])
    plan_copies = [
        [
            (
                pltpu.make_async_copy(key_plan_hbm.at[b, q], key_plan_ref.at[b, q], plan_sems.at[0, b, q]),
                pltpu.make_async_copy(value_plan_hbm.at[b, q], value_plan_ref.at[b, q], plan_sems.at[1, b, q]),
            )
            for q in range(slots)
        ]
        for b in range(blocks)
    ]
    ordered = [copies[id(target)] for _, target in pairs]
    start_all(ordered[:12])
    for b in range(blocks):
        for q in range(slots):
            start_all(plan_copies[b][q])
    start_all(ordered[12:])

    def arrived(*targets):
        for target in targets:
            copies[id(target)].wait()

    arrived(lat_ref, more_ref, embed_ref, pos_own_ref, mods_ref)
    lat = lat_ref[...] + more_ref[...] if first else lat_ref[...]
    embed = embed_ref[...]
    pos_own = pos_own_ref[...]
    mods = [mods_ref[:, row] for row in range(8)]
    hidden = own_hidden(lat, embed, pos_own)
    normed = modulated(normalized(hidden), mods[0], mods[1]).astype(bf16)
    arrived(wsi_ref, same_head_ref, gain_rows_ref)
    same_head = same_head_ref[...]

    def head_normed(values, gain):
        values = values.astype(bf16).astype(f32)
        total = dot((values * values).astype(bf16), same_head)
        return values * lax.rsqrt(total * (1.0 / HD) + epsilon) * gain

    queries = head_normed(dot_nt(normed, wsi_ref[...]), gain_rows_ref[0:1])

    arrived(pieces_ref, head_sum_ref, own_head_ref, gather_ref)
    for group in range(devices // PACK):
        stacked = pieces_ref[group * PACK : (group + 1) * PACK].astype(f32).reshape(LANES, lanes).T
        for part in range(PACK):
            cross_ref[group * PACK + part] = pltpu.roll(stacked, LANES - part * PIECE, 1) if part else stacked

    def turned(b, g):
        if first:
            held, rows = frames // sections, own * sections
            peers = range(b * per_block + g // held, (b + 1) * per_block, sections)
            at = g % held * rows
        else:
            rows, peers, at = own, range(b * per_block, (b + 1) * per_block), g * own
        return [cross_ref[peer, at : at + rows] for peer in peers]

    row = lax.broadcasted_iota(jnp.int32, (FRAMES * tokens, tokens), 0)
    column = lax.broadcasted_iota(jnp.int32, (FRAMES * tokens, tokens), 1)
    identity = (lax.rem(row, tokens) == column).astype(bf16)
    same_frame = (row // tokens == column // (HEADS * own)).astype(f32)
    masks = head_masks()
    head_sum = head_sum_ref[...]
    own_head = own_head_ref[...]

    for q in range(slots):
        spread = jnp.concatenate(
            [
                (queries[g * own : (g + 1) * own][None] * masks).reshape(HEADS * own, WIDE)
                for g in range(q * FRAMES, (q + 1) * FRAMES)
            ],
            axis=0,
        ).astype(bf16)
        total, mixed = 0.0, 0.0
        for b in range(blocks):
            tiles = [tile for f in range(FRAMES) for tile in turned(b, q * FRAMES + f)]
            left = jnp.concatenate([identity, jnp.concatenate(tiles, axis=0).astype(bf16)], axis=1)
            for copy in plan_copies[b][q]:
                copy.wait()
            product = dot(left, key_plan_ref[b, q])
            values = dot_nt(value_plan_ref[b, q], left).astype(bf16)
            deviation = product[:, WIDE:]
            keys = product[:, :WIDE]
            key_scale = lax.rsqrt(
                dot((keys * keys).astype(bf16), head_sum) * (1.0 / HD) + epsilon * deviation * deviation
            )
            scores = dot_nt(keys.astype(bf16), spread)
            weights = jnp.exp(scores * key_scale) * same_frame
            total = total + jnp.sum(weights, axis=0, keepdims=True)
            mixed = mixed + dot(values, (weights / deviation).astype(bf16))
        mixed_ref[:, q * LANES : (q + 1) * LANES] = (mixed * (1.0 / total) * own_head).astype(bf16)
    mixed = dot(mixed_ref[...], gather_ref[...]).T.astype(bf16)

    arrived(wso_ref, pos_frame_ref)
    branch = dot(mixed, wso_ref[...])
    hidden = (
        hidden.reshape(slots, FRAMES, own, D)
        + mods[2][:, None, None, :] * branch.reshape(slots, FRAMES, own, D)
        + pos_frame_ref[...].reshape(slots, FRAMES, 1, D)
    ).reshape(lanes, D)
    normed = modulated(normalized(hidden), mods[3], mods[4]).astype(bf16)
    arrived(wti_ref)
    queries = head_normed(dot_nt(normed, wti_ref[:WIDE]), gain_rows_ref[1:2])
    keys = head_normed(dot_nt(normed, wti_ref[INNER : INNER + WIDE]), 1.0).astype(bf16)
    values = dot_nt(normed, wti_ref[2 * INNER :]).astype(bf16)
    row = lax.broadcasted_iota(jnp.int32, (lanes, lanes), 0)
    column = lax.broadcasted_iota(jnp.int32, (lanes, lanes), 1)
    same_token = (lax.rem(row, own) == lax.rem(column, own)).astype(f32)
    parts = [None] * (WIDE // LANES)
    for h in range(HEADS):
        start, stop = h * HD // LANES * LANES, -(-(h + 1) * HD // LANES) * LANES
        spread = (queries[:, start:stop] * masks[h, :, start:stop]).astype(bf16)
        weights = jnp.exp(dot_nt(spread, keys[:, start:stop])) * same_token
        total = jnp.sum(weights, axis=-1, keepdims=True)
        stop = min(stop, INNER)
        result = dot(weights.astype(bf16), values[:, start:stop]) * (1.0 / total) * masks[h, :, start:stop]
        for tile in range(start // LANES, -(-stop // LANES)):
            piece = result[:, tile * LANES - start : min((tile + 1) * LANES, stop) - start]
            parts[tile] = piece if parts[tile] is None else parts[tile] + piece
    mixed = jnp.concatenate([p.astype(bf16) for p in parts], axis=1)
    arrived(wto_ref)
    branch = dot(mixed, wto_ref[...])
    hidden = hidden + (mods[5][:, None, :] * branch.reshape(slots, FRAMES * own, D)).reshape(lanes, D)
    final = modulated(normalized(hidden), mods[6], mods[7])
    final_high, final_low = split(final)
    arrived(final_ref, noise_ref)
    weight_high, weight_low = split(final_ref[...])
    velocity = dot_nt(weight_high, final_high) + dot_nt(weight_low, final_high) + dot_nt(weight_high, final_low)

    slot = lax.broadcasted_iota(jnp.int32, (1, lanes), 1) // (FRAMES * own)
    times = jnp.zeros((1, lanes), f32)
    stride = jnp.zeros((1, lanes), f32)
    before = 0.0
    for q in range(slots):
        time = (levels_ref[q].astype(f32) + 1.0) / LEVELS
        times = jnp.where(slot == q, time, times)
        stride = jnp.where(slot == q, time - before, stride)
        before = time
    low = section == 0
    noise = 0.0
    for f in range(FRAMES):
        block = noise_ref[f]
        block = jnp.where(low, block[:, :own], block[:, own:])
        noise = noise + placed(block, (frames - FRAMES + f) * own)
    moved = pltpu.roll(lat - stride * velocity, lanes - FRAMES * own, 1)
    moved = jnp.where(slot == slots - 1, noise, moved)
    if not last:
        lat_out, piece_out = outs
        lat_out[...] = moved
        piece = make_piece(moved, embed, pos_own)
        for peer in range(devices):
            piece_out[peer] = piece
    else:
        keep_out, send_out = outs
        held = frames // sections
        for i, result in enumerate((moved, lat - times * velocity)):
            for g in range(held):
                here = [
                    pltpu.roll(result, (lanes - (half * held + g) * own) % lanes, 1)[:, :own] for half in range(2)
                ]
                for out, block in (
                    (keep_out, jnp.where(low, here[0], here[1])),
                    (send_out, jnp.where(low, here[1], here[0])),
                ):
                    zeros = jnp.zeros_like(block)
                    out[i, g] = jnp.concatenate(
                        [jnp.where(low, block, zeros), jnp.where(low, zeros, block)], axis=1
                    )


def per_device(
    queue_latents,
    fresh_noise,
    slot_levels,
    level_table,
    embed_weight,
    spatial_in,
    spatial_out,
    temporal_in,
    temporal_out,
    norm_gains,
    final_weight,
):
    blocks, _, _, tokens = queue_latents.shape
    sections = lax.axis_size("tm")
    shards = lax.axis_size("space")
    axes = ("space", "tm")
    devices = sections * shards
    own = tokens // sections
    slots = blocks * sections
    frames = slots * FRAMES
    lanes = frames * own
    space_tokens = tokens * shards
    token_blocks = space_tokens // LANES
    partner = [(i, sections - 1 - i) for i in range(sections)]

    pos = jnp.asarray(sincos(space_tokens, D).astype(np.float32))
    pos_frame = jnp.asarray(sincos(frames, D).astype(np.float32))
    head = np.where(np.arange(WIDE) < INNER, np.arange(WIDE) // HD, -1)
    same_head = jnp.asarray(((head[:, None] == head[None, :]) & (head >= 0)[None, :]).astype(np.float32), bf16)
    lane = np.arange(LANES)
    lane_head = lane // own % HEADS
    head_sum = jnp.asarray((head[:, None] == lane_head[None, :]).astype(np.float32), bf16)
    own_head = jnp.asarray((head[:INNER, None] == lane_head[None, :]).astype(np.float32))
    packed = np.arange(slots * LANES)
    packed_lane = packed // (HEADS * own) * own + packed % own
    gather = jnp.asarray((packed_lane[:, None] == lane[None, :]).astype(np.float32), bf16)

    final_turned = jnp.transpose(final_weight)
    spatial_turned = jnp.transpose(spatial_in)
    temporal_turned = jnp.transpose(temporal_in)

    vmem = pl.BlockSpec(memory_space=pltpu.VMEM)
    smem = pl.BlockSpec(memory_space=pltpu.SMEM)
    hbm = pl.BlockSpec(memory_space=pltpu.HBM)
    dma = pltpu.SemaphoreType.DMA
    flat = jax.ShapeDtypeStruct((CH, lanes), f32)
    piece_shape = jax.ShapeDtypeStruct((devices, PIECE, lanes), bf16)
    pieces, keep, send = pl.pallas_call(
        first_kernel,
        out_shape=[piece_shape, flat, flat],
        in_specs=[vmem, hbm, hbm],
        out_specs=[vmem] * 3,
        scratch_shapes=[pltpu.VMEM((CH, D), f32), pltpu.VMEM((tokens, D), f32), dma((2,))],
        name="first_piece",
    )(queue_latents.reshape(blocks * FRAMES, CH, tokens), embed_weight, pos)
    more = lax.ppermute(send, "tm", partner)
    lat = keep

    key_shape = (token_blocks, slots, PLAN, WIDE + LANES)
    value_shape = (token_blocks, slots, INNER, PLAN)
    mods_shape = (slots, 8, D)
    key_plan, value_plan, mods, gain_rows = pl.pallas_call(
        prepare_kernel,
        out_shape=[
            jax.ShapeDtypeStruct(key_shape, bf16),
            jax.ShapeDtypeStruct(value_shape, bf16),
            jax.ShapeDtypeStruct(mods_shape, f32),
            jax.ShapeDtypeStruct((8, WIDE), f32),
        ],
        in_specs=[smem] + [hbm] * 5,
        out_specs=[hbm] * 4,
        scratch_shapes=[
            pltpu.VMEM(mods_shape, f32),
            pltpu.VMEM((space_tokens, D), f32),
            pltpu.VMEM((CH, D), f32),
            pltpu.VMEM((4, HD), f32),
            pltpu.VMEM((2 * INNER, D), bf16),
            pltpu.VMEM((slots * (LANES + PIECE), D), bf16),
            pltpu.VMEM(key_shape, bf16),
            pltpu.VMEM(value_shape, bf16),
            pltpu.VMEM((8, WIDE), f32),
            dma((slots + 5,)),
            dma((2 + 2 * token_blocks * slots,)),
        ],
        compiler_params=pltpu.CompilerParams(vmem_limit_bytes=48 * 1024 * 1024),
        name="slot_plan",
    )(slot_levels, level_table, pos, embed_weight, norm_gains, spatial_turned)

    out_shape = jax.ShapeDtypeStruct((2, blocks * FRAMES, CH, tokens), f32)
    for step in range(STEPS):
        last = step == STEPS - 1
        gathered = lax.all_to_all(pieces, axes, split_axis=0, concat_axis=0, tiled=True)
        lat, pieces = pl.pallas_call(
            functools.partial(step_kernel, step=step),
            out_shape=[out_shape] * 2 if last else [flat, piece_shape],
            in_specs=[smem] + [hbm] * 20,
            out_specs=[vmem] * 2,
            scratch_shapes=[
                pltpu.VMEM(piece_shape.shape, bf16),
                pltpu.VMEM((CH, lanes), f32),
                pltpu.VMEM((CH, lanes), f32),
                pltpu.VMEM((FRAMES, CH, tokens), f32),
                pltpu.VMEM((CH, D), f32),
                pltpu.VMEM((own, D), f32),
                pltpu.VMEM((frames, D), f32),
                pltpu.VMEM(mods_shape, f32),
                pltpu.VMEM((8, WIDE), f32),
                pltpu.VMEM((WIDE, WIDE), bf16),
                pltpu.VMEM((WIDE, LANES), bf16),
                pltpu.VMEM((INNER, LANES), f32),
                pltpu.VMEM((slots * LANES, LANES), bf16),
                pltpu.VMEM((CH, D), f32),
                pltpu.VMEM(key_shape, bf16),
                pltpu.VMEM(value_shape, bf16),
                pltpu.VMEM((WIDE, D), bf16),
                pltpu.VMEM((INNER, D), bf16),
                pltpu.VMEM((3 * INNER, D), bf16),
                pltpu.VMEM((INNER, D), bf16),
                pltpu.VMEM((devices, lanes, LANES), f32),
                pltpu.VMEM((INNER, slots * LANES), bf16),
                dma((18,)),
                dma((2, token_blocks, slots)),
            ],
            compiler_params=pltpu.CompilerParams(vmem_limit_bytes=56 * 1024 * 1024),
            name="denoise_step",
        )(
            slot_levels,
            gathered,
            lat,
            more,
            fresh_noise,
            embed_weight,
            pos,
            pos_frame,
            mods,
            gain_rows,
            same_head,
            head_sum,
            own_head,
            gather,
            final_turned,
            key_plan,
            value_plan,
            spatial_turned,
            spatial_out,
            temporal_turned,
            temporal_out,
        )

    results = lat + lax.ppermute(pieces, "tm", partner)
    results = results.reshape(2, *queue_latents.shape)
    return (results[0], results[1])


def solution(mesh):
    return jax.shard_map(
        per_device,
        mesh=mesh,
        in_specs=(
            P(("clip", "tm"), None, None, "space"),
            P("clip", None, None, "space"),
            P("clip"),
            P(),
            P(),
            P(),
            P(),
            P(),
            P(),
            P(),
            P(),
        ),
        out_specs=(P(("clip", "tm"), None, None, "space"), P(("clip", "tm"), None, None, "space")),
        check_vma=False,
    )
```

```python
import functools
import math

import jax
import jax.numpy as jnp
import numpy as np
from jax import lax
from jax.experimental import pallas as pl
from jax.experimental.pallas import tpu as pltpu
from jax.sharding import PartitionSpec as P

D = 1152
HEADS = 8
HD = 72
INNER = HEADS * HD
CH = 16
FRAMES = 2
STEPS = 3
LEVELS = 16

LANES = 128
WIDE = -(-INNER // LANES) * LANES
PIECE = 32
PACK = LANES // PIECE
PLAN = LANES + PIECE

GRANT = 24 * 1024 * 1024

epsilon = 1e-06
f32 = jnp.float32
bf16 = jnp.bfloat16


def dot(a, b):
    return lax.dot_general(a, b, (((1,), (0,)), ((), ())), preferred_element_type=f32)


def dot_nt(a, b):
    return lax.dot_general(a, b, (((1,), (1,)), ((), ())), preferred_element_type=f32)


def split(x):
    high = x.astype(bf16)
    return high, (x - high.astype(f32)).astype(bf16)


def sincos(count, width):
    half = width // 2
    rates = np.exp(-np.log(10000.0) * np.arange(half) / half)
    angles = np.arange(count)[:, None] * rates[None, :]
    return np.concatenate([np.sin(angles), np.cos(angles)], axis=-1)


def head_masks():
    shape = (HEADS, 1, WIDE)
    head = lax.broadcasted_iota(jnp.int32, shape, 0)
    position = lax.broadcasted_iota(jnp.int32, shape, 2)
    return ((position >= head * HD) & (position < (head + 1) * HD)).astype(f32)


def normalized(values):
    centered = values - jnp.mean(values, axis=-1, keepdims=True)
    return centered * lax.rsqrt(jnp.mean(centered * centered, axis=-1, keepdims=True) + epsilon)


def modulated(values, shift, scale):
    slots = shift.shape[0]
    out = values.reshape(slots, -1, D) * (1.0 + scale)[:, None, :] + shift[:, None, :]
    return out.reshape(values.shape)


def own_hidden(lat, embed, pos_own):
    lanes = lat.shape[1]
    lat_high, lat_low = split(lat)
    lat_high = lat_high.astype(f32)
    zeros = jnp.zeros((LANES - 3 * CH, lanes), f32)
    rows = jnp.concatenate([lat_high, lat_low.astype(f32), lat_high, zeros], axis=0).T.astype(bf16)
    embed_high, embed_low = split(embed)
    weights = jnp.concatenate(
        [embed_high, embed_high, embed_low, jnp.zeros((LANES - 3 * CH, D), bf16)], axis=0
    )
    own = pos_own.shape[0]
    return (dot(rows, weights).reshape(lanes // own, own, D) + pos_own[None]).reshape(lanes, D)


def make_piece(lat, embed, pos_own):
    lanes = lat.shape[1]
    hidden = own_hidden(lat, embed, pos_own)
    centered = hidden - jnp.mean(hidden, axis=-1, keepdims=True)
    deviation = jnp.sqrt(jnp.mean(centered * centered, axis=-1, keepdims=True) + epsilon)
    row = jnp.broadcast_to(deviation, (lanes, LANES)).T[:1]
    high, low = split(row)
    high = high.astype(f32)
    zeros = jnp.zeros((PIECE - CH - 3, lanes), f32)
    return jnp.concatenate([lat, high, high, low.astype(f32), zeros], axis=0).astype(bf16)


def placed(block, start):
    rows, width = block.shape
    wide = jnp.concatenate([block, jnp.zeros((rows, LANES - width), f32)], axis=1)
    return pltpu.roll(wide, start, 1) if start else wide


HELD = 17
COPIED = 11


def start_all(copies):
    for copy in copies:
        copy.start()


def first_kernel(queue_ref, embed_hbm, pos_hbm, piece_ref, keep_ref, send_ref, embed_ref, pos_ref, sems):
    frames, _, tokens = queue_ref.shape
    shard, section = lax.axis_index("space"), lax.axis_index("tm")
    first = pl.multiple_of(shard * tokens, 8)
    copies = [
        pltpu.make_async_copy(embed_hbm, embed_ref, sems.at[0]),
        pltpu.make_async_copy(pos_hbm.at[pl.ds(first, tokens)], pos_ref, sems.at[1]),
    ]
    start_all(copies)
    own = tokens // 2
    lat = jnp.zeros((CH, LANES), f32)
    halves = [jnp.zeros((CH, LANES), f32) for _ in range(2)]
    for g in range(frames):
        block = queue_ref[g]
        lat = lat + placed(block, g * tokens)
        for half in range(2):
            halves[half] = halves[half] + placed(block[:, half * own : (half + 1) * own], g * own)
    low = section == 0
    keep_ref[...] = jnp.where(low, halves[0], pltpu.roll(halves[1], frames * own, 1))
    send_ref[...] = jnp.where(low, halves[1], pltpu.roll(halves[0], frames * own, 1))
    for copy in copies:
        copy.wait()
    piece = make_piece(lat, embed_ref[...], pos_ref[...])
    for peer in range(piece_ref.shape[0]):
        piece_ref[peer] = piece


def build_plans(mods_ref, pos_ref, embed_ref, weight_ref, left_ref, key_plan_ref, value_plan_ref):
    blocks, slots = key_plan_ref.shape[:2]
    tokens = LANES
    embed = embed_ref[...]
    embed = embed - jnp.mean(embed, axis=-1, keepdims=True)
    row = lax.broadcasted_iota(jnp.int32, (PIECE - CH, 1), 0)
    part = lax.broadcasted_iota(jnp.int32, (PIECE, 1), 0)
    lane = lax.broadcasted_iota(jnp.int32, (1, PIECE), 1)
    plan_row = lax.broadcasted_iota(jnp.int32, (PLAN, LANES), 0)
    deviation_columns = ((plan_row == tokens + CH + 1) | (plan_row == tokens + CH + 2)).astype(bf16)
    for b in range(blocks):
        pos = pos_ref[b * tokens : (b + 1) * tokens]
        pos = pos - jnp.mean(pos, axis=-1, keepdims=True)
        for q in range(slots):
            scale = 1.0 + mods_ref[q, 1:2]
            shift_rows = jnp.where(row < 3, mods_ref[q, 0:1], 0.0)
            left_ref[q * PLAN : (q + 1) * PLAN] = jnp.concatenate(
                [pos * scale, embed * scale, shift_rows], axis=0
            ).astype(bf16)
        product = dot_nt(left_ref[...], weight_ref[:INNER])
        for q in range(slots):
            rows = product[q * PLAN : (q + 1) * PLAN]
            group = rows[tokens:]
            group = jnp.where(part == CH + 1, group - group.astype(bf16).astype(f32), group)
            key_plan_ref[b, q] = jnp.concatenate(
                [
                    jnp.concatenate([rows[:tokens].astype(bf16), group.astype(bf16)], axis=0),
                    jnp.zeros((PLAN, WIDE - INNER), bf16),
                    deviation_columns,
                ],
                axis=1,
            )
        for q in range(slots):
            product = dot_nt(weight_ref[INNER:], left_ref[q * PLAN : (q + 1) * PLAN])
            group = product[:, tokens:]
            group = jnp.where(lane == CH + 1, group - group.astype(bf16).astype(f32), group)
            value_plan_ref[b, q] = jnp.concatenate(
                [product[:, :tokens].astype(bf16), group.astype(bf16)], axis=1
            )


def gain_products(gains):
    products = jnp.concatenate(
        [gains[0:1] * gains[1:2], gains[2:3] * gains[3:4], jnp.zeros((6, HD), f32)], axis=0
    ) / math.sqrt(HD)
    place = lax.broadcasted_iota(jnp.int32, (HD, WIDE), 1)
    feature = lax.broadcasted_iota(jnp.int32, (HD, WIDE), 0)
    spread = ((place < INNER) & (lax.rem(place, HD) == feature)).astype(f32)
    return lax.dot_general(
        products, spread, (((1,), (0,)), ((), ())), preferred_element_type=f32, precision=lax.Precision.HIGHEST
    )


def step_kernel(levels_ref, pieces_ref, lat_ref, *refs, step):
    first, last = step == 0, step == STEPS - 1
    if first:
        more_ref, pos_hbm, table_hbm, gains_hbm, wsi_hbm = refs[:5]
        sources = refs[5 : 5 + COPIED]
        outs = refs[5 + COPIED : 7 + COPIED]
        held = refs[7 + COPIED : 7 + COPIED + HELD]
        cross_ref, mixed_ref, pos_ref, gains_ref, weight_ref, left_ref, sems = refs[7 + COPIED + HELD :]
    else:
        held, outs, (cross_ref, mixed_ref) = refs[:HELD], refs[HELD : HELD + 2], refs[HELD + 2 :]
    (
        key_plan_ref,
        value_plan_ref,
        mods_ref,
        gain_rows_ref,
        pos_own_ref,
        wsi_ref,
        same_head_ref,
        embed_ref,
        head_sum_ref,
        own_head_ref,
        gather_ref,
        pos_frame_ref,
        noise_ref,
        final_ref,
        wso_ref,
        wti_ref,
        wto_ref,
    ) = held
    lanes = lat_ref.shape[1]
    blocks, slots = key_plan_ref.shape[:2]
    frames = slots * FRAMES
    own = lanes // frames
    devices = pieces_ref.shape[0]
    tokens = LANES
    per_block = devices // blocks
    section, sections = lax.axis_index("tm"), lax.axis_size("tm")

    if first:
        first_token = pl.multiple_of((lax.axis_index("space") * sections + section) * own, 8)
        early = [(table_hbm.at[levels_ref[q]], mods_ref.at[q]) for q in range(slots)]
        early += [(pos_hbm, pos_ref), (sources[1], embed_ref), (wsi_hbm.at[INNER:], weight_ref)]
        late = [
            (gains_hbm, gains_ref),
            (pos_hbm.at[pl.ds(first_token, own)], pos_own_ref),
            (wsi_hbm.at[:WIDE], wsi_ref),
        ]
        late += [pair for pair in zip(sources, held[6:]) if pair[1] is not embed_ref]
        copies = [pltpu.make_async_copy(*pair, sems.at[i]) for i, pair in enumerate(early + late)]
        early, late = copies[: len(early)], copies[len(early) :]
        start_all(early)
        for copy in early:
            copy.wait()
        start_all(late)
        build_plans(mods_ref, pos_ref, embed_ref, weight_ref, left_ref, key_plan_ref, value_plan_ref)
        for copy in late:
            copy.wait()
        gain_rows_ref[...] = gain_products(gains_ref[...])

    lat = lat_ref[...] + more_ref[...] if first else lat_ref[...]
    embed = embed_ref[...]
    pos_own = pos_own_ref[...]
    mods = [mods_ref[:, row] for row in range(8)]
    hidden = own_hidden(lat, embed, pos_own)
    normed = modulated(normalized(hidden), mods[0], mods[1]).astype(bf16)
    same_head = same_head_ref[...]

    def head_normed(values, gain):
        values = values.astype(bf16).astype(f32)
        total = dot((values * values).astype(bf16), same_head)
        return values * lax.rsqrt(total * (1.0 / HD) + epsilon) * gain

    queries = head_normed(dot_nt(normed, wsi_ref[...]), gain_rows_ref[0:1])

    for group in range(devices // PACK):
        stacked = pieces_ref[group * PACK : (group + 1) * PACK].astype(f32).reshape(LANES, lanes).T
        for part in range(PACK):
            cross_ref[group * PACK + part] = pltpu.roll(stacked, LANES - part * PIECE, 1) if part else stacked

    def turned(b, g):
        if first:
            held, rows = frames // sections, own * sections
            peers = range(b * per_block + g // held, (b + 1) * per_block, sections)
            at = g % held * rows
        else:
            rows, peers, at = own, range(b * per_block, (b + 1) * per_block), g * own
        return [cross_ref[peer, at : at + rows] for peer in peers]

    row = lax.broadcasted_iota(jnp.int32, (FRAMES * tokens, tokens), 0)
    column = lax.broadcasted_iota(jnp.int32, (FRAMES * tokens, tokens), 1)
    identity = (lax.rem(row, tokens) == column).astype(bf16)
    same_frame = (row // tokens == column // (HEADS * own)).astype(f32)
    masks = head_masks()
    head_sum = head_sum_ref[...]
    own_head = own_head_ref[...]

    for q in range(slots):
        spread = jnp.concatenate(
            [
                (queries[g * own : (g + 1) * own][None] * masks).reshape(HEADS * own, WIDE)
                for g in range(q * FRAMES, (q + 1) * FRAMES)
            ],
            axis=0,
        ).astype(bf16)
        total, mixed = 0.0, 0.0
        for b in range(blocks):
            tiles = [tile for f in range(FRAMES) for tile in turned(b, q * FRAMES + f)]
            left = jnp.concatenate([identity, jnp.concatenate(tiles, axis=0).astype(bf16)[:, :PIECE]], axis=1)
            product = dot(left, key_plan_ref[b, q])
            values = dot_nt(value_plan_ref[b, q], left).astype(bf16)
            deviation = product[:, WIDE:]
            keys = product[:, :WIDE]
            key_scale = lax.rsqrt(
                dot((keys * keys).astype(bf16), head_sum) * (1.0 / HD) + epsilon * deviation * deviation
            )
            scores = dot_nt(keys.astype(bf16), spread)
            weights = jnp.exp(scores * key_scale) * same_frame
            total = total + jnp.sum(weights, axis=0, keepdims=True)
            mixed = mixed + dot(values, (weights / deviation).astype(bf16))
        mixed_ref[:, q * LANES : (q + 1) * LANES] = (mixed * (1.0 / total) * own_head).astype(bf16)
    mixed = dot(mixed_ref[...], gather_ref[...]).T.astype(bf16)

    branch = dot(mixed, wso_ref[...])
    hidden = (
        hidden.reshape(slots, FRAMES, own, D)
        + mods[2][:, None, None, :] * branch.reshape(slots, FRAMES, own, D)
        + pos_frame_ref[...].reshape(slots, FRAMES, 1, D)
    ).reshape(lanes, D)
    normed = modulated(normalized(hidden), mods[3], mods[4]).astype(bf16)
    queries = head_normed(dot_nt(normed, wti_ref[:WIDE]), gain_rows_ref[1:2])
    keys = head_normed(dot_nt(normed, wti_ref[INNER : INNER + WIDE]), 1.0).astype(bf16)
    values = dot_nt(normed, wti_ref[2 * INNER :]).astype(bf16)
    row = lax.broadcasted_iota(jnp.int32, (lanes, lanes), 0)
    column = lax.broadcasted_iota(jnp.int32, (lanes, lanes), 1)
    same_token = (lax.rem(row, own) == lax.rem(column, own)).astype(f32)
    parts = [None] * (WIDE // LANES)
    for h in range(HEADS):
        start, stop = h * HD // LANES * LANES, -(-(h + 1) * HD // LANES) * LANES
        spread = (queries[:, start:stop] * masks[h, :, start:stop]).astype(bf16)
        weights = jnp.exp(dot_nt(spread, keys[:, start:stop])) * same_token
        total = jnp.sum(weights, axis=-1, keepdims=True)
        stop = min(stop, INNER)
        result = dot(weights.astype(bf16), values[:, start:stop]) * (1.0 / total) * masks[h, :, start:stop]
        for tile in range(start // LANES, -(-stop // LANES)):
            piece = result[:, tile * LANES - start : min((tile + 1) * LANES, stop) - start]
            parts[tile] = piece if parts[tile] is None else parts[tile] + piece
    mixed = jnp.concatenate([p.astype(bf16) for p in parts], axis=1)
    branch = dot(mixed, wto_ref[...])
    hidden = hidden + (mods[5][:, None, :] * branch.reshape(slots, FRAMES * own, D)).reshape(lanes, D)
    final = modulated(normalized(hidden), mods[6], mods[7])
    final_high, final_low = split(final)
    weight_high, weight_low = split(final_ref[...])
    velocity = dot_nt(weight_high, final_high) + dot_nt(weight_low, final_high) + dot_nt(weight_high, final_low)

    slot = lax.broadcasted_iota(jnp.int32, (1, lanes), 1) // (FRAMES * own)
    times = jnp.zeros((1, lanes), f32)
    stride = jnp.zeros((1, lanes), f32)
    before = 0.0
    for q in range(slots):
        time = (levels_ref[q].astype(f32) + 1.0) / LEVELS
        times = jnp.where(slot == q, time, times)
        stride = jnp.where(slot == q, time - before, stride)
        before = time
    low = section == 0
    noise = 0.0
    for f in range(FRAMES):
        block = noise_ref[step, f]
        block = jnp.where(low, block[:, :own], block[:, own:])
        noise = noise + placed(block, (frames - FRAMES + f) * own)
    moved = pltpu.roll(lat - stride * velocity, lanes - FRAMES * own, 1)
    moved = jnp.where(slot == slots - 1, noise, moved)
    if not last:
        lat_out, piece_out = outs
        lat_out[...] = moved
        piece = make_piece(moved, embed, pos_own)
        for peer in range(devices):
            piece_out[peer] = piece
    else:
        keep_out, send_out = outs
        held = frames // sections
        for i, result in enumerate((moved, lat - times * velocity)):
            for g in range(held):
                here = [
                    pltpu.roll(result, (lanes - (half * held + g) * own) % lanes, 1)[:, :own] for half in range(2)
                ]
                for out, block in (
                    (keep_out, jnp.where(low, here[0], here[1])),
                    (send_out, jnp.where(low, here[1], here[0])),
                ):
                    zeros = jnp.zeros_like(block)
                    out[i, g] = jnp.concatenate(
                        [jnp.where(low, block, zeros), jnp.where(low, zeros, block)], axis=1
                    )


def per_device(
    queue_latents,
    fresh_noise,
    slot_levels,
    level_table,
    embed_weight,
    spatial_in,
    spatial_out,
    temporal_in,
    temporal_out,
    norm_gains,
    final_weight,
):
    blocks, _, _, tokens = queue_latents.shape
    sections = lax.axis_size("tm")
    shards = lax.axis_size("space")
    axes = ("space", "tm")
    devices = sections * shards
    own = tokens // sections
    slots = blocks * sections
    frames = slots * FRAMES
    lanes = frames * own
    space_tokens = tokens * shards
    token_blocks = space_tokens // LANES
    partner = [(i, sections - 1 - i) for i in range(sections)]

    pos = jnp.asarray(sincos(space_tokens, D).astype(np.float32))
    pos_frame = jnp.asarray(sincos(frames, D).astype(np.float32))
    head = np.where(np.arange(WIDE) < INNER, np.arange(WIDE) // HD, -1)
    same_head = jnp.asarray(((head[:, None] == head[None, :]) & (head >= 0)[None, :]).astype(np.float32), bf16)
    lane = np.arange(LANES)
    lane_head = lane // own % HEADS
    head_sum = jnp.asarray((head[:, None] == lane_head[None, :]).astype(np.float32), bf16)
    own_head = jnp.asarray((head[:INNER, None] == lane_head[None, :]).astype(np.float32))
    packed = np.arange(slots * LANES)
    packed_lane = packed // (HEADS * own) * own + packed % own
    gather = jnp.asarray((packed_lane[:, None] == lane[None, :]).astype(np.float32), bf16)

    final_turned = jnp.transpose(final_weight)
    spatial_turned = jnp.transpose(spatial_in)
    temporal_turned = jnp.transpose(temporal_in)

    vmem = pl.BlockSpec(memory_space=pltpu.VMEM)
    smem = pl.BlockSpec(memory_space=pltpu.SMEM)
    hbm = pl.BlockSpec(memory_space=pltpu.HBM)
    dma = pltpu.SemaphoreType.DMA

    def call(kernel, out_shape, arguments, scratch, name):
        spaces = {id(vmem): pltpu.VMEM, id(hbm): pltpu.HBM}
        values = [
            pltpu.with_memory_space_constraint(value, spaces[id(spec)]) if id(spec) in spaces else value
            for value, spec in arguments
        ]
        return pl.pallas_call(
            kernel,
            out_shape=out_shape,
            in_specs=[spec for _, spec in arguments],
            out_specs=[vmem] * len(out_shape),
            scratch_shapes=scratch,
            compiler_params=pltpu.CompilerParams(vmem_limit_bytes=GRANT),
            name=name,
        )(*values)

    flat = pltpu.VMEM((CH, lanes), f32)
    piece_shape = pltpu.VMEM((devices, PIECE, lanes), bf16)
    pieces, lat, send = call(
        first_kernel,
        [piece_shape, flat, flat],
        [(queue_latents.reshape(blocks * FRAMES, CH, tokens), vmem), (embed_weight, hbm), (pos, hbm)],
        [pltpu.VMEM((CH, D), f32), pltpu.VMEM((tokens, D), f32), dma((2,))],
        "first_piece",
    )
    more = lax.ppermute(send, "tm", partner)

    copied = [
        same_head,
        embed_weight,
        head_sum,
        own_head,
        gather,
        pos_frame,
        fresh_noise,
        final_turned,
        spatial_out,
        temporal_turned,
        temporal_out,
    ]
    held = [
        pltpu.VMEM((token_blocks, slots, PLAN, WIDE + LANES), bf16),
        pltpu.VMEM((token_blocks, slots, INNER, PLAN), bf16),
        pltpu.VMEM((slots, 8, D), f32),
        pltpu.VMEM((8, WIDE), f32),
        pltpu.VMEM((own, D), f32),
        pltpu.VMEM((WIDE, D), bf16),
        *(pltpu.VMEM(x.shape, x.dtype) for x in copied),
    ]
    result_shape = pltpu.VMEM((2, blocks * FRAMES, CH, tokens), f32)
    for step in range(STEPS):
        first, last = step == 0, step == STEPS - 1
        gathered = lax.all_to_all(pieces, axes, split_axis=0, concat_axis=0, tiled=True)
        out_shape = [result_shape] * 2 if last else [flat, piece_shape]
        arguments = [(slot_levels, smem), (gathered, vmem), (lat, vmem)]
        scratch = [pltpu.VMEM((devices, lanes, LANES), f32), pltpu.VMEM((INNER, slots * LANES), bf16)]
        if first:
            arguments += [(more, vmem)]
            arguments += [(x, hbm) for x in (pos, level_table, norm_gains, spatial_turned, *copied)]
            out_shape = out_shape + held
            scratch += [
                pltpu.VMEM((space_tokens, D), f32),
                pltpu.VMEM((4, HD), f32),
                pltpu.VMEM((2 * INNER, D), bf16),
                pltpu.VMEM((slots * PLAN, D), bf16),
                dma((slots + 3 + 3 + COPIED,)),
            ]
        else:
            arguments += [(x, vmem) for x in held]
        lat, pieces, *made = call(
            functools.partial(step_kernel, step=step), out_shape, arguments, scratch, "denoise_step"
        )
        held = made if first else held

    received = lax.ppermute(pieces, "tm", partner)
    return tuple((lat[i] + received[i]).reshape(queue_latents.shape) for i in range(2))


def solution(mesh):
    return jax.shard_map(
        per_device,
        mesh=mesh,
        in_specs=(
            P(("clip", "tm"), None, None, "space"),
            P("clip", None, None, "space"),
            P("clip"),
            P(),
            P(),
            P(),
            P(),
            P(),
            P(),
            P(),
            P(),
        ),
        out_specs=(P(("clip", "tm"), None, None, "space"), P(("clip", "tm"), None, None, "space")),
        check_vma=False,
    )
```

```python
import functools
import math

import jax
import jax.numpy as jnp
import numpy as np
from jax import lax
from jax.experimental import pallas as pl
from jax.experimental.pallas import tpu as pltpu
from jax.sharding import PartitionSpec as P

D = 1152
HEADS = 8
HD = 72
INNER = HEADS * HD
CH = 16
FRAMES = 2
STEPS = 3
LEVELS = 16

LANES = 128
WIDE = -(-INNER // LANES) * LANES
PIECE = 32
PACK = LANES // PIECE
PLAN = LANES + PIECE

GRANT = 24 * 1024 * 1024

epsilon = 1e-06
f32 = jnp.float32
bf16 = jnp.bfloat16


def dot(a, b):
    return lax.dot_general(a, b, (((1,), (0,)), ((), ())), preferred_element_type=f32)


def dot_nt(a, b):
    return lax.dot_general(a, b, (((1,), (1,)), ((), ())), preferred_element_type=f32)


def split(x):
    high = x.astype(bf16)
    return high, (x - high.astype(f32)).astype(bf16)


def sincos(count, width):
    half = width // 2
    rates = np.exp(-np.log(10000.0) * np.arange(half) / half)
    angles = np.arange(count)[:, None] * rates[None, :]
    return np.concatenate([np.sin(angles), np.cos(angles)], axis=-1)


def head_masks():
    shape = (HEADS, 1, WIDE)
    head = lax.broadcasted_iota(jnp.int32, shape, 0)
    position = lax.broadcasted_iota(jnp.int32, shape, 2)
    return ((position >= head * HD) & (position < (head + 1) * HD)).astype(f32)


def normalized(values):
    centered = values - jnp.mean(values, axis=-1, keepdims=True)
    return centered * lax.rsqrt(jnp.mean(centered * centered, axis=-1, keepdims=True) + epsilon)


def modulated(values, shift, scale):
    slots = shift.shape[0]
    out = values.reshape(slots, -1, D) * (1.0 + scale)[:, None, :] + shift[:, None, :]
    return out.reshape(values.shape)


def own_hidden(lat, embed, pos_own):
    lanes = lat.shape[1]
    lat_high, lat_low = split(lat)
    lat_high = lat_high.astype(f32)
    zeros = jnp.zeros((LANES - 3 * CH, lanes), f32)
    rows = jnp.concatenate([lat_high, lat_low.astype(f32), lat_high, zeros], axis=0).T.astype(bf16)
    embed_high, embed_low = split(embed)
    weights = jnp.concatenate(
        [embed_high, embed_high, embed_low, jnp.zeros((LANES - 3 * CH, D), bf16)], axis=0
    )
    own = pos_own.shape[0]
    return (dot(rows, weights).reshape(lanes // own, own, D) + pos_own[None]).reshape(lanes, D)


def make_piece(lat, hidden, rest=None):
    lanes = lat.shape[1]
    centered = hidden - jnp.mean(hidden, axis=-1, keepdims=True)
    deviation = jnp.sqrt(jnp.mean(centered * centered, axis=-1, keepdims=True) + epsilon)
    row = jnp.broadcast_to(deviation, (lanes, LANES)).T[:1]
    high, low = split(row)
    high = high.astype(f32)
    rest = jnp.zeros((CH // 2, lanes), f32) if rest is None else rest
    zeros = jnp.zeros((PIECE - CH - 3 - CH // 2, lanes), f32)
    return jnp.concatenate([lat, high, high, low.astype(f32), zeros, rest], axis=0).astype(bf16)


def placed(block, start):
    rows, width = block.shape
    wide = jnp.concatenate([block, jnp.zeros((rows, LANES - width), f32)], axis=1)
    return pltpu.roll(wide, start, 1) if start else wide


HELD = 17
COPIED = 11


def start_all(copies):
    for copy in copies:
        copy.start()


def build_plans(mods_ref, pos_ref, embed_ref, weight_ref, left_ref, key_plan_ref, value_plan_ref):
    blocks, slots = key_plan_ref.shape[:2]
    tokens = LANES
    embed = embed_ref[...]
    embed = embed - jnp.mean(embed, axis=-1, keepdims=True)
    row = lax.broadcasted_iota(jnp.int32, (PIECE - CH, 1), 0)
    part = lax.broadcasted_iota(jnp.int32, (PIECE, 1), 0)
    lane = lax.broadcasted_iota(jnp.int32, (1, PIECE), 1)
    plan_row = lax.broadcasted_iota(jnp.int32, (PLAN, LANES), 0)
    deviation_columns = ((plan_row == tokens + CH + 1) | (plan_row == tokens + CH + 2)).astype(bf16)
    for b in range(blocks):
        pos = pos_ref[b * tokens : (b + 1) * tokens]
        pos = pos - jnp.mean(pos, axis=-1, keepdims=True)
        for q in range(slots):
            scale = 1.0 + mods_ref[q, 1:2]
            shift_rows = jnp.where(row < 3, mods_ref[q, 0:1], 0.0)
            left_ref[q * PLAN : (q + 1) * PLAN] = jnp.concatenate(
                [pos * scale, embed * scale, shift_rows], axis=0
            ).astype(bf16)
        product = dot_nt(left_ref[...], weight_ref[:INNER])
        for q in range(slots):
            rows = product[q * PLAN : (q + 1) * PLAN]
            group = rows[tokens:]
            group = jnp.where(part == CH + 1, group - group.astype(bf16).astype(f32), group)
            key_plan_ref[b, q] = jnp.concatenate(
                [
                    jnp.concatenate([rows[:tokens].astype(bf16), group.astype(bf16)], axis=0),
                    jnp.zeros((PLAN, WIDE - INNER), bf16),
                    deviation_columns,
                ],
                axis=1,
            )
        for q in range(slots):
            product = dot_nt(weight_ref[INNER:], left_ref[q * PLAN : (q + 1) * PLAN])
            group = product[:, tokens:]
            group = jnp.where(lane == CH + 1, group - group.astype(bf16).astype(f32), group)
            value_plan_ref[b, q] = jnp.concatenate(
                [product[:, :tokens].astype(bf16), group.astype(bf16)], axis=1
            )


def gain_products(gains):
    products = jnp.concatenate(
        [gains[0:1] * gains[1:2], gains[2:3] * gains[3:4], jnp.zeros((6, HD), f32)], axis=0
    ) / math.sqrt(HD)
    place = lax.broadcasted_iota(jnp.int32, (HD, WIDE), 1)
    feature = lax.broadcasted_iota(jnp.int32, (HD, WIDE), 0)
    spread = ((place < INNER) & (lax.rem(place, HD) == feature)).astype(f32)
    return lax.dot_general(
        products, spread, (((1,), (0,)), ((), ())), preferred_element_type=f32, precision=lax.Precision.HIGHEST
    )


def head_normed(values, same_head, gain):
    values = values.astype(bf16).astype(f32)
    total = dot((values * values).astype(bf16), same_head)
    return values * lax.rsqrt(total * (1.0 / HD) + epsilon) * gain


def low_rows(lat):
    low = split(lat)[1].astype(f32)
    half = lat.shape[0] // 2
    return low[:half] + pltpu.roll(low[half:], LANES // 2, 1)


def partner_latents(piece, held, tokens, low):
    own = tokens // 2
    lane = lax.broadcasted_iota(jnp.int32, (1, LANES), 1)
    left = lane < LANES // 2
    high = jnp.where(low, piece[:CH], pltpu.roll(piece[:CH], LANES - own, 1))
    rest = piece[PIECE - CH // 2 :]
    out = jnp.where(left, jnp.concatenate([rest, pltpu.roll(rest, LANES // 2, 1)], axis=0), 0.0)
    for g in range(held):
        moved = pltpu.roll(high, LANES - g * own, 1) if g else high
        out = out + jnp.where(lane // own == g, moved, 0.0)
    return jnp.where(low, pltpu.roll(out, LANES // 2, 1), out)


def prepare_kernel(levels_ref, queue_hbm, pos_hbm, table_hbm, gains_hbm, wsi_hbm, *refs):
    sources, held = refs[:COPIED], refs[COPIED : COPIED + HELD]
    piece_ref, lat_ref, queue_ref, pos_ref, pos_shard_ref, gains_ref, weight_ref, left_ref, sems = refs[COPIED + HELD :]
    key_plan_ref, value_plan_ref, mods_ref, gain_rows_ref, pos_own_ref, wsi_ref, same_head_ref, embed_ref = held[:8]
    slots = mods_ref.shape[0]
    frames, _, tokens = queue_ref.shape
    own = pos_own_ref.shape[0]
    section, sections = lax.axis_index("tm"), lax.axis_size("tm")
    shard_token = pl.multiple_of(lax.axis_index("space") * tokens, 8)
    own_token = pl.multiple_of(shard_token + section * own, 8)
    stages = [
        [(queue_hbm, queue_ref), (sources[1], embed_ref), (pos_hbm.at[pl.ds(shard_token, tokens)], pos_shard_ref)],
        [(table_hbm.at[levels_ref[q]], mods_ref.at[q]) for q in range(slots)]
        + [(pos_hbm, pos_ref), (wsi_hbm.at[INNER:], weight_ref)],
        [
            (gains_hbm, gains_ref),
            (pos_hbm.at[pl.ds(own_token, own)], pos_own_ref),
            (wsi_hbm.at[:WIDE], wsi_ref),
        ]
        + [pair for pair in zip(sources, held[6:]) if pair[1] is not embed_ref],
    ]
    count = 0
    for i, stage in enumerate(stages):
        stages[i] = [pltpu.make_async_copy(*pair, sems.at[count + j]) for j, pair in enumerate(stage)]
        count += len(stage)
    start_all(stages[0] + stages[1])
    for copy in stages[0]:
        copy.wait()
    lat = jnp.zeros((CH, LANES), f32)
    halves = [jnp.zeros((CH, LANES), f32) for _ in range(2)]
    for g in range(frames):
        block = queue_ref[g]
        lat = lat + placed(block, g * tokens)
        for half in range(2):
            halves[half] = halves[half] + placed(block[:, half * own : (half + 1) * own], g * own)
    low = section == 0
    lat_ref[...] = jnp.where(low, halves[0], pltpu.roll(halves[1], LANES // 2, 1))
    rest = low_rows(jnp.where(low, halves[1], halves[0]))
    piece = make_piece(lat, own_hidden(lat, embed_ref[...], pos_shard_ref[...]), rest)
    for peer in range(piece_ref.shape[0]):
        piece_ref[peer] = piece
    for copy in stages[1]:
        copy.wait()
    start_all(stages[2])
    build_plans(mods_ref, pos_ref, embed_ref, weight_ref, left_ref, key_plan_ref, value_plan_ref)
    for copy in stages[2]:
        copy.wait()
    gain_rows_ref[...] = gain_products(gains_ref[...])


def step_kernel(levels_ref, pieces_ref, lat_ref, *refs, step):
    first, last = step == 0, step == STEPS - 1
    outs, (cross_ref, mixed_ref) = refs[HELD:-2], refs[-2:]
    (
        key_plan_ref,
        value_plan_ref,
        mods_ref,
        gain_rows_ref,
        pos_own_ref,
        wsi_ref,
        same_head_ref,
        embed_ref,
        head_sum_ref,
        own_head_ref,
        gather_ref,
        pos_frame_ref,
        noise_ref,
        final_ref,
        wso_ref,
        wti_ref,
        wto_ref,
    ) = refs[:HELD]
    lanes = lat_ref.shape[1]
    blocks, slots = key_plan_ref.shape[:2]
    frames = slots * FRAMES
    own = lanes // frames
    devices = pieces_ref.shape[0]
    tokens = LANES
    per_block = devices // blocks
    section, sections = lax.axis_index("tm"), lax.axis_size("tm")
    low = section == 0
    mods = [mods_ref[:, row] for row in range(8)]
    same_head = same_head_ref[...]

    lat = lat_ref[...]
    if first:
        partner = lax.axis_index("space") * sections + (sections - 1 - section)
        lat = lat + partner_latents(pieces_ref[partner].astype(f32), frames // sections, own * sections, low)
    hidden = own_hidden(lat, embed_ref[...], pos_own_ref[...])
    normed = modulated(normalized(hidden), mods[0], mods[1]).astype(bf16)
    queries = head_normed(dot_nt(normed, wsi_ref[...]), same_head, gain_rows_ref[0:1])

    for group in range(devices // PACK):
        stacked = pieces_ref[group * PACK : (group + 1) * PACK].astype(f32).reshape(LANES, lanes).T
        for part in range(PACK):
            cross_ref[group * PACK + part] = pltpu.roll(stacked, LANES - part * PIECE, 1) if part else stacked

    def turned(b, g):
        if first:
            held, rows = frames // sections, own * sections
            peers = range(b * per_block + g // held, (b + 1) * per_block, sections)
            at = g % held * rows
        else:
            rows, peers, at = own, range(b * per_block, (b + 1) * per_block), g * own
        return [cross_ref[peer, at : at + rows] for peer in peers]

    row = lax.broadcasted_iota(jnp.int32, (FRAMES * tokens, tokens), 0)
    column = lax.broadcasted_iota(jnp.int32, (FRAMES * tokens, tokens), 1)
    identity = (lax.rem(row, tokens) == column).astype(bf16)
    same_frame = (row // tokens == column // (HEADS * own)).astype(f32)
    masks = head_masks()
    head_sum = head_sum_ref[...]
    own_head = own_head_ref[...]

    for q in range(slots):
        spread = jnp.concatenate(
            [
                (queries[g * own : (g + 1) * own][None] * masks).reshape(HEADS * own, WIDE)
                for g in range(q * FRAMES, (q + 1) * FRAMES)
            ],
            axis=0,
        ).astype(bf16)
        total, mixed = 0.0, 0.0
        for b in range(blocks):
            tiles = [tile for f in range(FRAMES) for tile in turned(b, q * FRAMES + f)]
            left = jnp.concatenate([identity, jnp.concatenate(tiles, axis=0).astype(bf16)[:, :PIECE]], axis=1)
            product = dot(left, key_plan_ref[b, q])
            values = dot_nt(value_plan_ref[b, q], left).astype(bf16)
            deviation = product[:, WIDE:]
            keys = product[:, :WIDE]
            key_scale = lax.rsqrt(
                dot((keys * keys).astype(bf16), head_sum) * (1.0 / HD) + epsilon * deviation * deviation
            )
            scores = dot_nt(keys.astype(bf16), spread)
            weights = jnp.exp(scores * key_scale) * same_frame
            total = total + jnp.sum(weights, axis=0, keepdims=True)
            mixed = mixed + dot(values, (weights / deviation).astype(bf16))
        mixed_ref[:, q * LANES : (q + 1) * LANES] = (mixed * (1.0 / total) * own_head).astype(bf16)
    mixed = dot(mixed_ref[...], gather_ref[...]).T.astype(bf16)

    branch = dot(mixed, wso_ref[...])
    hidden = (
        hidden.reshape(slots, FRAMES, own, D)
        + mods[2][:, None, None, :] * branch.reshape(slots, FRAMES, own, D)
        + pos_frame_ref[...].reshape(slots, FRAMES, 1, D)
    ).reshape(lanes, D)
    normed = modulated(normalized(hidden), mods[3], mods[4]).astype(bf16)
    queries = head_normed(dot_nt(normed, wti_ref[:WIDE]), same_head, gain_rows_ref[1:2])
    keys = head_normed(dot_nt(normed, wti_ref[INNER : INNER + WIDE]), same_head, 1.0).astype(bf16)
    values = dot_nt(normed, wti_ref[2 * INNER :]).astype(bf16)
    row = lax.broadcasted_iota(jnp.int32, (lanes, lanes), 0)
    column = lax.broadcasted_iota(jnp.int32, (lanes, lanes), 1)
    same_token = (lax.rem(row, own) == lax.rem(column, own)).astype(f32)
    parts = [None] * (WIDE // LANES)
    for h in range(HEADS):
        start, stop = h * HD // LANES * LANES, -(-(h + 1) * HD // LANES) * LANES
        spread = (queries[:, start:stop] * masks[h, :, start:stop]).astype(bf16)
        weights = jnp.exp(dot_nt(spread, keys[:, start:stop])) * same_token
        total = jnp.sum(weights, axis=-1, keepdims=True)
        stop = min(stop, INNER)
        result = dot(weights.astype(bf16), values[:, start:stop]) * (1.0 / total) * masks[h, :, start:stop]
        for tile in range(start // LANES, -(-stop // LANES)):
            piece = result[:, tile * LANES - start : min((tile + 1) * LANES, stop) - start]
            parts[tile] = piece if parts[tile] is None else parts[tile] + piece
    mixed = jnp.concatenate([p.astype(bf16) for p in parts], axis=1)
    branch = dot(mixed, wto_ref[...])
    hidden = hidden + (mods[5][:, None, :] * branch.reshape(slots, FRAMES * own, D)).reshape(lanes, D)
    final = modulated(normalized(hidden), mods[6], mods[7])
    final_high, final_low = split(final)
    weight_high, weight_low = split(final_ref[...])
    velocity = dot_nt(weight_high, final_high) + dot_nt(weight_low, final_high) + dot_nt(weight_high, final_low)

    slot = lax.broadcasted_iota(jnp.int32, (1, lanes), 1) // (FRAMES * own)
    times = jnp.zeros((1, lanes), f32)
    stride = jnp.zeros((1, lanes), f32)
    before = 0.0
    for q in range(slots):
        time = (levels_ref[q].astype(f32) + 1.0) / LEVELS
        times = jnp.where(slot == q, time, times)
        stride = jnp.where(slot == q, time - before, stride)
        before = time
    noise = 0.0
    for f in range(FRAMES):
        block = noise_ref[step, f]
        block = jnp.where(low, block[:, :own], block[:, own:])
        noise = noise + placed(block, (frames - FRAMES + f) * own)
    moved = pltpu.roll(lat - stride * velocity, lanes - FRAMES * own, 1)
    moved = jnp.where(slot == slots - 1, noise, moved)
    if not last:
        lat_out, piece_out = outs
        lat_out[...] = moved
        piece = make_piece(moved, own_hidden(moved, embed_ref[...], pos_own_ref[...]))
        for peer in range(devices):
            piece_out[peer] = piece
    else:
        keep_out, send_out = outs
        held = frames // sections
        for i, result in enumerate((moved, lat - times * velocity)):
            for g in range(held):
                here = [
                    pltpu.roll(result, (lanes - (half * held + g) * own) % lanes, 1)[:, :own] for half in range(2)
                ]
                for out, block in (
                    (keep_out, jnp.where(low, here[0], here[1])),
                    (send_out, jnp.where(low, here[1], here[0])),
                ):
                    zeros = jnp.zeros_like(block)
                    out[i, g] = jnp.concatenate(
                        [jnp.where(low, block, zeros), jnp.where(low, zeros, block)], axis=1
                    )


def per_device(
    queue_latents,
    fresh_noise,
    slot_levels,
    level_table,
    embed_weight,
    spatial_in,
    spatial_out,
    temporal_in,
    temporal_out,
    norm_gains,
    final_weight,
):
    blocks, _, _, tokens = queue_latents.shape
    sections = lax.axis_size("tm")
    shards = lax.axis_size("space")
    axes = ("space", "tm")
    devices = sections * shards
    own = tokens // sections
    slots = blocks * sections
    frames = slots * FRAMES
    lanes = frames * own
    space_tokens = tokens * shards
    token_blocks = space_tokens // LANES
    partner = [(i, sections - 1 - i) for i in range(sections)]

    pos = jnp.asarray(sincos(space_tokens, D).astype(np.float32))
    pos_frame = jnp.asarray(sincos(frames, D).astype(np.float32))
    head = np.where(np.arange(WIDE) < INNER, np.arange(WIDE) // HD, -1)
    same_head = jnp.asarray(((head[:, None] == head[None, :]) & (head >= 0)[None, :]).astype(np.float32), bf16)
    lane = np.arange(LANES)
    lane_head = lane // own % HEADS
    head_sum = jnp.asarray((head[:, None] == lane_head[None, :]).astype(np.float32), bf16)
    own_head = jnp.asarray((head[:INNER, None] == lane_head[None, :]).astype(np.float32))
    packed = np.arange(slots * LANES)
    packed_lane = packed // (HEADS * own) * own + packed % own
    gather = jnp.asarray((packed_lane[:, None] == lane[None, :]).astype(np.float32), bf16)

    final_turned = jnp.transpose(final_weight)
    spatial_turned = jnp.transpose(spatial_in)
    temporal_turned = jnp.transpose(temporal_in)

    vmem = pl.BlockSpec(memory_space=pltpu.VMEM)
    smem = pl.BlockSpec(memory_space=pltpu.SMEM)
    hbm = pl.BlockSpec(memory_space=pltpu.HBM)
    dma = pltpu.SemaphoreType.DMA

    def call(kernel, out_shape, arguments, scratch, name):
        spaces = {id(vmem): pltpu.VMEM, id(hbm): pltpu.HBM}
        values = [
            pltpu.with_memory_space_constraint(value, spaces[id(spec)]) if id(spec) in spaces else value
            for value, spec in arguments
        ]
        return pl.pallas_call(
            kernel,
            out_shape=out_shape,
            in_specs=[spec for _, spec in arguments],
            out_specs=[vmem] * len(out_shape),
            scratch_shapes=scratch,
            compiler_params=pltpu.CompilerParams(vmem_limit_bytes=GRANT),
            name=name,
        )(*values)

    flat = pltpu.VMEM((CH, lanes), f32)
    piece_shape = pltpu.VMEM((devices, PIECE, lanes), bf16)
    queue = queue_latents.reshape(blocks * FRAMES, CH, tokens)
    copied = [
        same_head,
        embed_weight,
        head_sum,
        own_head,
        gather,
        pos_frame,
        fresh_noise,
        final_turned,
        spatial_out,
        temporal_turned,
        temporal_out,
    ]
    held = [
        pltpu.VMEM((token_blocks, slots, PLAN, WIDE + LANES), bf16),
        pltpu.VMEM((token_blocks, slots, INNER, PLAN), bf16),
        pltpu.VMEM((slots, 8, D), f32),
        pltpu.VMEM((8, WIDE), f32),
        pltpu.VMEM((own, D), f32),
        pltpu.VMEM((WIDE, D), bf16),
        *(pltpu.VMEM(x.shape, x.dtype) for x in copied),
    ]
    *held, pieces, lat = call(
        prepare_kernel,
        held + [piece_shape, flat],
        [(slot_levels, smem)]
        + [(x, hbm) for x in (queue, pos, level_table, norm_gains, spatial_turned, *copied)],
        [
            pltpu.VMEM(queue.shape, f32),
            pltpu.VMEM((space_tokens, D), f32),
            pltpu.VMEM((tokens, D), f32),
            pltpu.VMEM((4, HD), f32),
            pltpu.VMEM((2 * INNER, D), bf16),
            pltpu.VMEM((slots * PLAN, D), bf16),
            dma((3 + slots + 2 + 3 + COPIED,)),
        ],
        "slot_plan",
    )
    result_shape = pltpu.VMEM((2, blocks * FRAMES, CH, tokens), f32)
    for step in range(STEPS):
        last = step == STEPS - 1
        gathered = lax.all_to_all(pieces, axes, split_axis=0, concat_axis=0, tiled=True)
        lat, pieces = call(
            functools.partial(step_kernel, step=step),
            [result_shape] * 2 if last else [flat, piece_shape],
            [(slot_levels, smem)] + [(x, vmem) for x in (gathered, lat, *held)],
            [pltpu.VMEM((devices, lanes, LANES), f32), pltpu.VMEM((INNER, slots * LANES), bf16)],
            "denoise_step",
        )

    received = lax.ppermute(pieces, "tm", partner)
    return tuple((lat[i] + received[i]).reshape(queue_latents.shape) for i in range(2))


def solution(mesh):
    return jax.shard_map(
        per_device,
        mesh=mesh,
        in_specs=(
            P(("clip", "tm"), None, None, "space"),
            P("clip", None, None, "space"),
            P("clip"),
            P(),
            P(),
            P(),
            P(),
            P(),
            P(),
            P(),
            P(),
        ),
        out_specs=(P(("clip", "tm"), None, None, "space"), P(("clip", "tm"), None, None, "space")),
        check_vma=False,
    )
```

```python
import functools
import math

import jax
import jax.numpy as jnp
import numpy as np
from jax import lax
from jax.experimental import pallas as pl
from jax.experimental.pallas import tpu as pltpu
from jax.sharding import PartitionSpec as P

D = 1152
HEADS = 8
HD = 72
INNER = HEADS * HD
CH = 16
FRAMES = 2
STEPS = 3
LEVELS = 16

LANES = 128
WIDE = -(-INNER // LANES) * LANES
PIECE = 32
PACK = LANES // PIECE
PLAN = LANES + PIECE

GRANT = 26 * 1024 * 1024

epsilon = 1e-06
f32 = jnp.float32
bf16 = jnp.bfloat16


def dot(a, b):
    return lax.dot_general(a, b, (((1,), (0,)), ((), ())), preferred_element_type=f32)


def dot_nt(a, b):
    return lax.dot_general(a, b, (((1,), (1,)), ((), ())), preferred_element_type=f32)


def split(x):
    high = x.astype(bf16)
    return high, (x - high.astype(f32)).astype(bf16)


def sincos(count, width):
    half = width // 2
    rates = np.exp(-np.log(10000.0) * np.arange(half) / half)
    angles = np.arange(count)[:, None] * rates[None, :]
    return np.concatenate([np.sin(angles), np.cos(angles)], axis=-1)


def head_masks():
    shape = (HEADS, 1, WIDE)
    head = lax.broadcasted_iota(jnp.int32, shape, 0)
    position = lax.broadcasted_iota(jnp.int32, shape, 2)
    return ((position >= head * HD) & (position < (head + 1) * HD)).astype(f32)


def normalized(values):
    centered = values - jnp.mean(values, axis=-1, keepdims=True)
    return centered * lax.rsqrt(jnp.mean(centered * centered, axis=-1, keepdims=True) + epsilon)


def modulated(values, shift, scale):
    slots = shift.shape[0]
    out = values.reshape(slots, -1, D) * (1.0 + scale)[:, None, :] + shift[:, None, :]
    return out.reshape(values.shape)


def own_hidden(lat, embed, pos_own):
    lanes = lat.shape[1]
    lat_high, lat_low = split(lat)
    lat_high = lat_high.astype(f32)
    zeros = jnp.zeros((LANES - 3 * CH, lanes), f32)
    rows = jnp.concatenate([lat_high, lat_low.astype(f32), lat_high, zeros], axis=0).T.astype(bf16)
    embed_high, embed_low = split(embed)
    weights = jnp.concatenate(
        [embed_high, embed_high, embed_low, jnp.zeros((LANES - 3 * CH, D), bf16)], axis=0
    )
    own = pos_own.shape[0]
    return (dot(rows, weights).reshape(lanes // own, own, D) + pos_own[None]).reshape(lanes, D)


def make_piece(lat, hidden):
    lanes = lat.shape[1]
    centered = hidden - jnp.mean(hidden, axis=-1, keepdims=True)
    scale = lax.rsqrt(jnp.mean(centered * centered, axis=-1, keepdims=True) + epsilon)
    scale = jnp.broadcast_to(scale, (lanes, LANES)).T[:1].astype(bf16).astype(f32)
    scaled = lat * scale
    high = scaled.astype(bf16).astype(f32)
    zeros = jnp.zeros((PIECE // 2 - 3, lanes), f32)
    return jnp.concatenate([high, jnp.ones((2, lanes), f32), scale, zeros], axis=0), scaled - high


def pick(values, low, frames):
    own = LANES // 2 // frames
    lane = lax.broadcasted_iota(jnp.int32, (1, LANES), 1)
    values = jnp.where(low, values, pltpu.roll(values, LANES - own, 1))
    out = jnp.where(lane // own == 0, values, 0.0)
    for g in range(1, frames):
        out = out + jnp.where(lane // own == g, pltpu.roll(values, LANES - g * own, 1), 0.0)
    return out


def placed(block, start):
    rows, width = block.shape
    wide = jnp.concatenate([block, jnp.zeros((rows, LANES - width), f32)], axis=1)
    return pltpu.roll(wide, start, 1) if start else wide


HELD = 16
COPIED = 8


def start_all(copies):
    for copy in copies:
        copy.start()


def build_plans(mods_ref, pos_ref, embed_ref, weight_ref, left_ref, key_plan_ref, value_plan_ref):
    blocks, slots = key_plan_ref.shape[:2]
    tokens = LANES
    embed = embed_ref[...]
    embed = embed - jnp.mean(embed, axis=-1, keepdims=True)
    row = lax.broadcasted_iota(jnp.int32, (PIECE - CH, 1), 0)
    part = lax.broadcasted_iota(jnp.int32, (PIECE, 1), 0)
    for b in range(blocks):
        pos = pos_ref[b * tokens : (b + 1) * tokens]
        pos = pos - jnp.mean(pos, axis=-1, keepdims=True)
        for q in range(slots):
            scale = 1.0 + mods_ref[q, 1:2]
            shift_rows = jnp.where(row < 2, mods_ref[q, 0:1], 0.0)
            left_ref[q * PLAN : (q + 1) * PLAN] = jnp.concatenate(
                [pos * scale, embed * scale, shift_rows], axis=0
            ).astype(bf16)
        for ref, weight in ((key_plan_ref, weight_ref[:INNER]), (value_plan_ref, weight_ref[INNER:])):
            product = dot_nt(left_ref[...], weight)
            for q in range(slots):
                rows = product[q * PLAN : (q + 1) * PLAN]
                group = rows[tokens:]
                group = jnp.where(part == CH + 1, group - group.astype(bf16).astype(f32), group).astype(bf16)
                copies = (ref.shape[2] - tokens) // PIECE
                rows = jnp.concatenate([rows[:tokens].astype(bf16)] + [group] * copies, axis=0)
                if ref.shape[3] > INNER:
                    rows = jnp.concatenate([rows, jnp.zeros((rows.shape[0], ref.shape[3] - INNER), bf16)], axis=1)
                ref[b, q] = rows


def gain_products(gains):
    products = jnp.concatenate(
        [gains[0:1] * gains[1:2], gains[2:3] * gains[3:4], jnp.zeros((6, HD), f32)], axis=0
    ) / math.sqrt(HD)
    place = lax.broadcasted_iota(jnp.int32, (HD, WIDE), 1)
    feature = lax.broadcasted_iota(jnp.int32, (HD, WIDE), 0)
    spread = ((place < INNER) & (lax.rem(place, HD) == feature)).astype(f32)
    return lax.dot_general(
        products, spread, (((1,), (0,)), ((), ())), preferred_element_type=f32, precision=lax.Precision.HIGHEST
    )


def head_normed(values, same_head, gain):
    values = values.astype(bf16).astype(f32)
    total = dot((values * values).astype(bf16), same_head)
    return values * lax.rsqrt(total * (1.0 / HD) + epsilon) * gain


def partner_latents(piece, frames, low):
    lane = lax.broadcasted_iota(jnp.int32, (1, LANES), 1)
    chosen = pick(piece[: PIECE - CH // 2], low, frames)
    rest = piece[PIECE - CH // 2 :]
    rest = jnp.concatenate([rest, pltpu.roll(rest, LANES // 2, 1)], axis=0)
    lat = (chosen[:CH] + rest) / chosen[CH + 2 : CH + 3]
    lat = jnp.where(lane < LANES // 2, lat, 0.0)
    return jnp.where(low, pltpu.roll(lat, LANES // 2, 1), lat)


def prepare_kernel(levels_ref, queue_hbm, pos_hbm, table_hbm, gains_hbm, final_hbm, wsi_hbm, *refs):
    sources, held = refs[:COPIED], refs[COPIED : COPIED + HELD]
    piece_ref, lat_ref, queue_ref, pos_ref, pos_shard_ref, gains_ref, turned_ref, weight_ref, left_ref, sems = refs[
        COPIED + HELD :
    ]
    key_plan_ref, value_plan_ref, mods_ref, gain_rows_ref, rates_ref, final_ref = held[:6]
    pos_own_ref, wsi_ref, _, embed_ref = held[6:10]
    slots = mods_ref.shape[0]
    frames, _, tokens = queue_ref.shape
    own = pos_own_ref.shape[0]
    section, sections = lax.axis_index("tm"), lax.axis_size("tm")
    shard_token = pl.multiple_of(lax.axis_index("space") * tokens, 8)
    own_token = pl.multiple_of(shard_token + section * own, 8)
    stages = [
        [(queue_hbm, queue_ref), (sources[1], embed_ref), (pos_hbm.at[pl.ds(shard_token, tokens)], pos_shard_ref)],
        [(table_hbm.at[levels_ref[q]], mods_ref.at[q]) for q in range(slots)]
        + [(pos_hbm, pos_ref), (wsi_hbm.at[INNER:], weight_ref)],
        [
            (gains_hbm, gains_ref),
            (final_hbm, turned_ref),
            (pos_hbm.at[pl.ds(own_token, own)], pos_own_ref),
            (wsi_hbm.at[:WIDE], wsi_ref),
        ]
        + [pair for pair in zip(sources, held[8:]) if pair[1] is not embed_ref],
    ]
    count = 0
    for i, stage in enumerate(stages):
        stages[i] = [pltpu.make_async_copy(*pair, sems.at[count + j]) for j, pair in enumerate(stage)]
        count += len(stage)
    start_all(stages[0] + stages[1])
    for copy in stages[0]:
        copy.wait()
    lat = placed(queue_ref[0], 0)
    for g in range(1, frames):
        lat = lat + placed(queue_ref[g], g * tokens)
    low = section == 0
    mine = pick(lat, low, frames)
    lat_ref[...] = jnp.where(low, mine, pltpu.roll(mine, LANES // 2, 1))
    piece, rest = make_piece(lat, own_hidden(lat, embed_ref[...], pos_shard_ref[...]))
    rest = pick(rest, section != 0, frames)
    rest = rest[: CH // 2] + pltpu.roll(rest[CH // 2 :], LANES // 2, 1)
    piece = jnp.concatenate([piece[: PIECE - CH // 2], rest], axis=0).astype(bf16)
    for peer in range(piece_ref.shape[0]):
        piece_ref[peer] = piece
    for copy in stages[1]:
        copy.wait()
    start_all(stages[2])
    build_plans(mods_ref, pos_ref, embed_ref, weight_ref, left_ref, key_plan_ref, value_plan_ref)
    for copy in stages[2]:
        copy.wait()
    gain_rows_ref[...] = gain_products(gains_ref[...])
    high, low = split(turned_ref[...])
    final = jnp.concatenate([high.astype(f32), low.astype(f32), jnp.zeros((LANES - 2 * CH, D), f32)], axis=0)
    final_ref[...] = final.T.astype(bf16)
    lanes = lat_ref.shape[1]
    slot = lax.broadcasted_iota(jnp.int32, (1, lanes), 1) // (lanes // slots)
    times = jnp.zeros((1, lanes), f32)
    stride = jnp.zeros((1, lanes), f32)
    before = 0.0
    for q in range(slots):
        time = (levels_ref[q].astype(f32) + 1.0) / LEVELS
        times = jnp.where(slot == q, time, times)
        stride = jnp.where(slot == q, time - before, stride)
        before = time
    rates_ref[...] = jnp.concatenate([times, stride, jnp.zeros((6, lanes), f32)], axis=0)


def step_kernel(pieces_ref, lat_ref, *refs, step):
    first, last = step == 0, step == STEPS - 1
    outs, (cross_ref, mixed_ref, keys_ref, squares_ref) = refs[HELD:-4], refs[-4:]
    (
        key_plan_ref,
        value_plan_ref,
        mods_ref,
        gain_rows_ref,
        rates_ref,
        final_ref,
        pos_own_ref,
        wsi_ref,
        same_head_ref,
        embed_ref,
        head_sum_ref,
        pos_frame_ref,
        noise_ref,
        wso_ref,
        wti_ref,
        wto_ref,
    ) = refs[:HELD]
    lanes = lat_ref.shape[1]
    blocks, slots = key_plan_ref.shape[:2]
    frames = slots * FRAMES
    own = lanes // frames
    devices = pieces_ref.shape[0]
    tokens = LANES
    per_block = devices // blocks
    section, sections = lax.axis_index("tm"), lax.axis_size("tm")
    low = section == 0
    mods = [mods_ref[:, row] for row in range(8)]
    same_head = same_head_ref[...]

    lat = lat_ref[...]
    if first:
        partner = lax.axis_index("space") * sections + (sections - 1 - section)
        lat = lat + partner_latents(pieces_ref[partner].astype(f32), frames // sections, low)

    def own_side():
        hidden = own_hidden(lat, embed_ref[...], pos_own_ref[...])
        yield hidden
        normed = normalized(hidden)
        yield None
        normed = modulated(normed, mods[0], mods[1]).astype(bf16)
        yield None
        queries = dot_nt(normed, wsi_ref[...])
        yield None
        yield head_normed(queries, same_head, gain_rows_ref[0:1])

    for group in range(devices // PACK):
        stacked = pieces_ref[group * PACK : (group + 1) * PACK].astype(f32).reshape(LANES, lanes).T
        for part in range(PACK):
            cross_ref[group * PACK + part] = pltpu.roll(stacked, LANES - part * PIECE, 1) if part else stacked

    def turned(b, g):
        if first:
            held, rows = frames // sections, own * sections
            peers = range(b * per_block + g // held, (b + 1) * per_block, sections)
            at = g % held * rows
        else:
            rows, peers, at = own, range(b * per_block, (b + 1) * per_block), g * own
        return [cross_ref[peer, at : at + rows] for peer in peers]

    row = lax.broadcasted_iota(jnp.int32, (tokens, tokens), 0)
    column = lax.broadcasted_iota(jnp.int32, (tokens, tokens), 1)
    diagonal = row == column
    scale_lane = (lax.broadcasted_iota(jnp.int32, (8, LANES), 1) == CH + 2).astype(bf16)
    row = lax.broadcasted_iota(jnp.int32, (LANES, FRAMES * PIECE), 0)
    column = lax.broadcasted_iota(jnp.int32, (LANES, FRAMES * PIECE), 1)
    own_piece = (row // (HEADS * own) == column // PIECE).astype(f32)
    masks = head_masks()
    head_sum = head_sum_ref[...]

    of_frame = [slice(f * tokens, (f + 1) * tokens) for f in range(FRAMES)]
    pairs = [(b, q) for q in range(slots) for b in range(blocks)]
    rows, scales, weights, totals = {}, {}, {}, [0.0] * slots
    steps = own_side()
    hidden = next(steps)
    for b in range(blocks):
        for q in range(slots):
            tiles = [tile for f in range(FRAMES) for tile in turned(b, q * FRAMES + f)]
            rows[b, q] = jnp.concatenate(tiles, axis=0).astype(bf16)
            scales[b, q] = dot_nt(scale_lane, rows[b, q])[:1]
        for q in range(slots):
            marked = [jnp.where(diagonal, scales[b, q][:, at], 0.0).astype(bf16) for at in of_frame]
            left = jnp.concatenate([jnp.concatenate(marked, axis=0), rows[b, q][:, :PIECE]], axis=1)
            keys = dot(left, key_plan_ref[b, q])
            squares_ref[q] = (keys * keys).astype(bf16)
            keys_ref[q] = keys.astype(bf16)
            if b == 0:
                queries = next(steps, None) if q < 4 else queries
        for q in range(slots):
            sums = dot(jnp.concatenate([squares_ref[q, at] for at in of_frame], axis=1), head_sum)
            scores = []
            for f, at in enumerate(of_frame):
                g = q * FRAMES + f
                spread = (queries[g * own : (g + 1) * own][None] * masks).reshape(HEADS * own, WIDE).astype(bf16)
                scores.append(dot_nt(keys_ref[q, at], spread))
            scores = jnp.concatenate(scores, axis=1)
            weights[b, q] = jnp.exp(scores * lax.rsqrt(sums * (1.0 / HD) + epsilon))
            totals[q] = totals[q] + jnp.sum(weights[b, q], axis=0, keepdims=True)
    by_query, groups = {}, {}
    for b, q in pairs:
        by_query[b, q] = (weights[b, q] * (1.0 / totals[q])).T
    for b, q in pairs:
        pieces = jnp.concatenate([rows[b, q][at, :PIECE] for at in of_frame], axis=1)
        groups[b, q] = dot(by_query[b, q].astype(bf16), pieces) * own_piece
    for q in range(slots):
        mixed = 0.0
        for b in range(blocks):
            scaled = by_query[b, q].reshape(FRAMES, HEADS * own, tokens)
            scaled = jnp.concatenate([scaled[f] * scales[b, q][:, at] for f, at in enumerate(of_frame)], axis=0)
            met = jnp.concatenate([scaled.astype(bf16), groups[b, q].astype(bf16)], axis=1)
            mixed = mixed + dot(met, value_plan_ref[b, q])
        for f in range(FRAMES):
            g = q * FRAMES + f
            tiles = []
            for start in range(0, INNER, LANES):
                stop = min(start + LANES, INNER)
                parts = [
                    mixed[(f * HEADS + h) * own : (f * HEADS + h + 1) * own, start:stop] * masks[h, :, start:stop]
                    for h in range(start // HD, -(-stop // HD))
                ]
                tiles.append(functools.reduce(jnp.add, parts))
            mixed_ref[g * own : (g + 1) * own] = jnp.concatenate(tiles, axis=1)
    mixed = mixed_ref[...].astype(bf16)

    branch = dot(mixed, wso_ref[...])
    hidden = (
        hidden.reshape(slots, FRAMES, own, D)
        + mods[2][:, None, None, :] * branch.reshape(slots, FRAMES, own, D)
        + pos_frame_ref[...].reshape(slots, FRAMES, 1, D)
    ).reshape(lanes, D)
    normed = modulated(normalized(hidden), mods[3], mods[4]).astype(bf16)
    queries = dot_nt(normed, wti_ref[:WIDE])
    keys = dot_nt(normed, wti_ref[INNER : INNER + WIDE])
    both = head_normed(jnp.concatenate([queries, keys], axis=0), same_head, 1.0)
    queries = both[:lanes] * gain_rows_ref[1:2]
    keys = both[lanes:].astype(bf16)
    values = dot_nt(normed, wti_ref[2 * INNER :]).astype(bf16)
    row = lax.broadcasted_iota(jnp.int32, (lanes, lanes), 0)
    column = lax.broadcasted_iota(jnp.int32, (lanes, lanes), 1)
    same_token = (lax.rem(row, own) == lax.rem(column, own)).astype(f32)
    windows = [(h * HD // LANES * LANES, -(-(h + 1) * HD // LANES) * LANES) for h in range(HEADS)]
    scores = []
    for h, (start, stop) in enumerate(windows):
        spread = (queries[:, start:stop] * masks[h, :, start:stop]).astype(bf16)
        scores.append(dot_nt(spread, keys[:, start:stop]))
    weights = [jnp.exp(score) * same_token for score in scores]
    scales = [1.0 / jnp.sum(weight, axis=-1, keepdims=True) for weight in weights]
    results = []
    for (start, stop), weight in zip(windows, weights):
        results.append(dot(weight.astype(bf16), values[:, start : min(stop, INNER)]))
    parts = [[] for _ in range(WIDE // LANES)]
    for h, (start, stop) in enumerate(windows):
        stop = min(stop, INNER)
        result = results[h] * scales[h] * masks[h, :, start:stop]
        for tile in range(start // LANES, -(-stop // LANES)):
            parts[tile].append(result[:, tile * LANES - start : min((tile + 1) * LANES, stop) - start])
    mixed = jnp.concatenate([functools.reduce(jnp.add, part).astype(bf16) for part in parts], axis=1)
    branch = dot(mixed, wto_ref[...])
    hidden = hidden + (mods[5][:, None, :] * branch.reshape(slots, FRAMES * own, D)).reshape(lanes, D)
    final = modulated(normalized(hidden), mods[6], mods[7])
    final_high, final_low = split(final)
    products = dot(jnp.concatenate([final_high, final_low], axis=0), final_ref[...])
    by_high, by_low = products[:lanes].T, products[lanes:].T
    velocity = by_high[:CH] + by_high[CH : 2 * CH] + by_low[:CH]

    slot = lax.broadcasted_iota(jnp.int32, (1, lanes), 1) // (FRAMES * own)
    times, stride = rates_ref[0:1], rates_ref[1:2]
    noise = 0.0
    for f in range(FRAMES):
        block = noise_ref[step, f]
        block = jnp.where(low, block[:, :own], block[:, own:])
        noise = noise + placed(block, (frames - FRAMES + f) * own)
    moved = pltpu.roll(lat - stride * velocity, lanes - FRAMES * own, 1)
    moved = jnp.where(slot == slots - 1, noise, moved)
    if not last:
        lat_out, piece_out = outs
        lat_out[...] = moved
        piece = make_piece(moved, own_hidden(moved, embed_ref[...], pos_own_ref[...]))[0].astype(bf16)
        for peer in range(devices):
            piece_out[peer] = piece
    else:
        keep_out, send_out = outs
        held = frames // sections
        for i, result in enumerate((moved, lat - times * velocity)):
            for g in range(held):
                here = [
                    pltpu.roll(result, (lanes - (half * held + g) * own) % lanes, 1)[:, :own] for half in range(2)
                ]
                for out, block in (
                    (keep_out, jnp.where(low, here[0], here[1])),
                    (send_out, jnp.where(low, here[1], here[0])),
                ):
                    zeros = jnp.zeros_like(block)
                    out[i, g] = jnp.concatenate(
                        [jnp.where(low, block, zeros), jnp.where(low, zeros, block)], axis=1
                    )


def per_device(
    queue_latents,
    fresh_noise,
    slot_levels,
    level_table,
    embed_weight,
    spatial_in,
    spatial_out,
    temporal_in,
    temporal_out,
    norm_gains,
    final_weight,
):
    blocks, _, _, tokens = queue_latents.shape
    sections = lax.axis_size("tm")
    shards = lax.axis_size("space")
    axes = ("space", "tm")
    devices = sections * shards
    own = tokens // sections
    slots = blocks * sections
    frames = slots * FRAMES
    lanes = frames * own
    space_tokens = tokens * shards
    token_blocks = space_tokens // LANES
    partner = [(i, sections - 1 - i) for i in range(sections)]

    pos = jnp.asarray(sincos(space_tokens, D).astype(np.float32))
    pos_frame = jnp.asarray(sincos(frames, D).astype(np.float32))
    head = np.where(np.arange(WIDE) < INNER, np.arange(WIDE) // HD, -1)
    same_head = jnp.asarray(((head[:, None] == head[None, :]) & (head >= 0)[None, :]).astype(np.float32), bf16)
    lane = np.arange(LANES)
    lane_head = lane // own % HEADS
    lane_frame = lane // (HEADS * own)
    head_sum = np.concatenate(
        [(head[:, None] == lane_head[None, :]) & (lane_frame == f)[None, :] for f in range(FRAMES)], axis=0
    )
    head_sum = jnp.asarray(head_sum.astype(np.float32), bf16)

    final_turned = jnp.transpose(final_weight)
    spatial_turned = jnp.transpose(spatial_in)
    temporal_turned = jnp.transpose(temporal_in)

    vmem = pl.BlockSpec(memory_space=pltpu.VMEM)
    smem = pl.BlockSpec(memory_space=pltpu.SMEM)
    hbm = pl.BlockSpec(memory_space=pltpu.HBM)
    dma = pltpu.SemaphoreType.DMA

    def call(kernel, out_shape, arguments, scratch, name):
        spaces = {id(vmem): pltpu.VMEM, id(hbm): pltpu.HBM, id(smem): pltpu.HBM}
        values = [
            pltpu.with_memory_space_constraint(value, spaces[id(spec)]) if id(spec) in spaces else value
            for value, spec in arguments
        ]
        return pl.pallas_call(
            kernel,
            out_shape=out_shape,
            in_specs=[spec for _, spec in arguments],
            out_specs=[vmem] * len(out_shape),
            scratch_shapes=scratch,
            compiler_params=pltpu.CompilerParams(vmem_limit_bytes=GRANT),
            name=name,
        )(*values)

    flat = pltpu.VMEM((CH, lanes), f32)
    piece_shape = pltpu.VMEM((devices, PIECE, lanes), bf16)
    queue = queue_latents.reshape(blocks * FRAMES, CH, tokens)
    copied = [
        same_head,
        embed_weight,
        head_sum,
        pos_frame,
        fresh_noise,
        spatial_out,
        temporal_turned,
        temporal_out,
    ]
    held = [
        pltpu.VMEM((token_blocks, slots, PLAN, WIDE), bf16),
        pltpu.VMEM((token_blocks, slots, LANES + FRAMES * PIECE, INNER), bf16),
        pltpu.VMEM((slots, 8, D), f32),
        pltpu.VMEM((8, WIDE), f32),
        pltpu.VMEM((8, lanes), f32),
        pltpu.VMEM((D, LANES), bf16),
        pltpu.VMEM((own, D), f32),
        pltpu.VMEM((WIDE, D), bf16),
        *(pltpu.VMEM(x.shape, x.dtype) for x in copied),
    ]
    *held, pieces, lat = call(
        prepare_kernel,
        held + [piece_shape, flat],
        [(slot_levels, smem)]
        + [(x, hbm) for x in (queue, pos, level_table, norm_gains, final_turned, spatial_turned, *copied)],
        [
            pltpu.VMEM(queue.shape, f32),
            pltpu.VMEM((space_tokens, D), f32),
            pltpu.VMEM((tokens, D), f32),
            pltpu.VMEM((4, HD), f32),
            pltpu.VMEM((CH, D), f32),
            pltpu.VMEM((2 * INNER, D), bf16),
            pltpu.VMEM((slots * PLAN, D), bf16),
            dma((3 + slots + 2 + 4 + COPIED,)),
        ],
        "slot_plan",
    )
    result_shape = pltpu.VMEM((2, blocks * FRAMES, CH, tokens), f32)
    for step in range(STEPS):
        last = step == STEPS - 1
        gathered = lax.all_to_all(pieces, axes, split_axis=0, concat_axis=0, tiled=True)
        lat, pieces = call(
            functools.partial(step_kernel, step=step),
            [result_shape] * 2 if last else [flat, piece_shape],
            [(x, vmem) for x in (gathered, lat, *held)],
            [pltpu.VMEM((devices, lanes, LANES), f32), pltpu.VMEM((lanes, INNER), f32)]
            + [pltpu.VMEM((slots, FRAMES * LANES, WIDE), bf16)] * 2,
            "denoise_step",
        )

    received = lax.ppermute(pieces, "tm", partner)
    return tuple((lat[i] + received[i]).reshape(queue_latents.shape) for i in range(2))


def solution(mesh):
    return jax.shard_map(
        per_device,
        mesh=mesh,
        in_specs=(
            P(("clip", "tm"), None, None, "space"),
            P("clip", None, None, "space"),
            P("clip"),
            P(),
            P(),
            P(),
            P(),
            P(),
            P(),
            P(),
            P(),
        ),
        out_specs=(P(("clip", "tm"), None, None, "space"), P(("clip", "tm"), None, None, "space")),
        check_vma=False,
    )
```

```python
import functools
import math

import jax
import jax.numpy as jnp
import numpy as np
from jax import lax
from jax.experimental import pallas as pl
from jax.experimental.pallas import tpu as pltpu
from jax.sharding import PartitionSpec as P

D = 1152
HEADS = 8
HD = 72
INNER = HEADS * HD
CH = 16
FRAMES = 2
STEPS = 3
LEVELS = 16

LANES = 128
WIDE = -(-INNER // LANES) * LANES
PIECE = 32
SHORT = PIECE - CH // 2
PACK = LANES // PIECE
PLAN = LANES + PIECE

GRANT = 26 * 1024 * 1024

epsilon = 1e-06
f32 = jnp.float32
bf16 = jnp.bfloat16


def dot(a, b):
    return lax.dot_general(a, b, (((1,), (0,)), ((), ())), preferred_element_type=f32)


def dot_nt(a, b):
    return lax.dot_general(a, b, (((1,), (1,)), ((), ())), preferred_element_type=f32)


def split(x):
    high = x.astype(bf16)
    return high, (x - high.astype(f32)).astype(bf16)


def sincos(count, width):
    half = width // 2
    rates = np.exp(-np.log(10000.0) * np.arange(half) / half)
    angles = np.arange(count)[:, None] * rates[None, :]
    return np.concatenate([np.sin(angles), np.cos(angles)], axis=-1)


def head_masks():
    shape = (HEADS, 1, WIDE)
    head = lax.broadcasted_iota(jnp.int32, shape, 0)
    position = lax.broadcasted_iota(jnp.int32, shape, 2)
    return ((position >= head * HD) & (position < (head + 1) * HD)).astype(f32)


def normalized(values):
    centered = values - jnp.mean(values, axis=-1, keepdims=True)
    return centered * lax.rsqrt(jnp.mean(centered * centered, axis=-1, keepdims=True) + epsilon)


def modulated(values, shift, scale):
    slots = shift.shape[0]
    out = values.reshape(slots, -1, D) * (1.0 + scale)[:, None, :] + shift[:, None, :]
    return out.reshape(values.shape)


def own_hidden(lat, embed, pos_own):
    lanes = lat.shape[1]
    lat_high, lat_low = split(lat)
    lat_high = lat_high.astype(f32)
    zeros = jnp.zeros((LANES - 3 * CH, lanes), f32)
    rows = jnp.concatenate([lat_high, lat_low.astype(f32), lat_high, zeros], axis=0).T.astype(bf16)
    embed_high, embed_low = split(embed)
    weights = jnp.concatenate(
        [embed_high, embed_high, embed_low, jnp.zeros((LANES - 3 * CH, D), bf16)], axis=0
    )
    own = pos_own.shape[0]
    return (dot(rows, weights).reshape(lanes // own, own, D) + pos_own[None]).reshape(lanes, D)


def make_piece(lat, hidden):
    lanes = lat.shape[1]
    centered = hidden - jnp.mean(hidden, axis=-1, keepdims=True)
    scale = lax.rsqrt(jnp.mean(centered * centered, axis=-1, keepdims=True) + epsilon)
    scale = jnp.broadcast_to(scale, (lanes, LANES)).T[:1].astype(bf16).astype(f32)
    scaled = lat * scale
    high = scaled.astype(bf16).astype(f32)
    zeros = jnp.zeros((SHORT - CH - 3, lanes), f32)
    return jnp.concatenate([high, jnp.ones((2, lanes), f32), scale, zeros], axis=0), scaled - high


def pick(values, low, frames):
    own = LANES // 2 // frames
    lane = lax.broadcasted_iota(jnp.int32, (1, LANES), 1)
    values = jnp.where(low, values, pltpu.roll(values, LANES - own, 1))
    out = jnp.where(lane // own == 0, values, 0.0)
    for g in range(1, frames):
        out = out + jnp.where(lane // own == g, pltpu.roll(values, LANES - g * own, 1), 0.0)
    return out


def placed(block, start):
    rows, width = block.shape
    wide = jnp.concatenate([block, jnp.zeros((rows, LANES - width), f32)], axis=1)
    return pltpu.roll(wide, start, 1) if start else wide


HELD = 13
COPIED = 5
LATER = 3


def start_all(copies):
    for copy in copies:
        copy.start()


def build_plans(mods_ref, pos_ref, embed_ref, weight_ref, left_ref, key_plan_ref, value_plan_ref):
    blocks, slots = key_plan_ref.shape[:2]
    tokens = LANES
    embed = embed_ref[...]
    embed = embed - jnp.mean(embed, axis=-1, keepdims=True)
    row = lax.broadcasted_iota(jnp.int32, (PIECE - CH, 1), 0)
    part = lax.broadcasted_iota(jnp.int32, (PIECE, 1), 0)
    for b in range(blocks):
        pos = pos_ref[b * tokens : (b + 1) * tokens]
        pos = pos - jnp.mean(pos, axis=-1, keepdims=True)
        for q in range(slots):
            scale = 1.0 + mods_ref[q, 1:2]
            shift_rows = jnp.where(row < 2, mods_ref[q, 0:1], 0.0)
            left_ref[q * PLAN : (q + 1) * PLAN] = jnp.concatenate(
                [pos * scale, embed * scale, shift_rows], axis=0
            ).astype(bf16)
        for ref, weight in ((key_plan_ref, weight_ref[:INNER]), (value_plan_ref, weight_ref[INNER:])):
            product = dot_nt(left_ref[...], weight)
            for q in range(slots):
                rows = product[q * PLAN : (q + 1) * PLAN]
                group = rows[tokens:]
                group = jnp.where(part == CH + 1, group - group.astype(bf16).astype(f32), group).astype(bf16)
                copies = (ref.shape[2] - tokens) // PIECE
                rows = jnp.concatenate([rows[:tokens].astype(bf16)] + [group] * copies, axis=0)
                if ref.shape[3] > INNER:
                    rows = jnp.concatenate([rows, jnp.zeros((rows.shape[0], ref.shape[3] - INNER), bf16)], axis=1)
                ref[b, q] = rows


def gain_products(gains):
    products = jnp.concatenate(
        [gains[0:1] * gains[1:2], gains[2:3] * gains[3:4], jnp.zeros((6, HD), f32)], axis=0
    ) / math.sqrt(HD)
    place = lax.broadcasted_iota(jnp.int32, (HD, WIDE), 1)
    feature = lax.broadcasted_iota(jnp.int32, (HD, WIDE), 0)
    spread = ((place < INNER) & (lax.rem(place, HD) == feature)).astype(f32)
    return lax.dot_general(
        products, spread, (((1,), (0,)), ((), ())), preferred_element_type=f32, precision=lax.Precision.HIGHEST
    )


def head_normed(values, same_head, gain):
    values = values.astype(bf16).astype(f32)
    total = dot((values * values).astype(bf16), same_head)
    return values * lax.rsqrt(total * (1.0 / HD) + epsilon) * gain


def partner_latents(piece, frames, low):
    lane = lax.broadcasted_iota(jnp.int32, (1, LANES), 1)
    chosen = pick(piece[:SHORT], low, frames)
    rest = piece[SHORT:]
    rest = jnp.concatenate([rest, pltpu.roll(rest, LANES // 2, 1)], axis=0)
    lat = (chosen[:CH] + rest) / chosen[CH + 2 : CH + 3]
    lat = jnp.where(lane < LANES // 2, lat, 0.0)
    return jnp.where(low, pltpu.roll(lat, LANES // 2, 1), lat)


def prepare_kernel(levels_hbm, queue_hbm, pos_hbm, table_hbm, gains_hbm, final_hbm, wsi_hbm, *refs):
    sources, held = refs[:COPIED], refs[COPIED : COPIED + HELD]
    piece_ref, lat_ref, levels_ref, table_ref, queue_ref, pos_ref, pos_shard_ref, gains_ref, turned_ref, weight_ref, left_ref, sems = refs[
        COPIED + HELD :
    ]
    key_plan_ref, value_plan_ref, mods_ref, gain_rows_ref, rates_ref, final_ref = held[:6]
    pos_own_ref, wsi_ref, _, embed_ref = held[6:10]
    slots = mods_ref.shape[0]
    frames, _, tokens = queue_ref.shape
    own = pos_own_ref.shape[0]
    section, sections = lax.axis_index("tm"), lax.axis_size("tm")
    shard_token = pl.multiple_of(lax.axis_index("space") * tokens, 8)
    own_token = pl.multiple_of(shard_token + section * own, 8)
    stages = [
        [
            (levels_hbm, levels_ref),
            (queue_hbm, queue_ref),
            (sources[1], embed_ref),
            (pos_hbm.at[pl.ds(shard_token, tokens)], pos_shard_ref),
            (gains_hbm, gains_ref),
            (final_hbm, turned_ref),
        ],
        [(table_hbm, table_ref), (pos_hbm, pos_ref), (wsi_hbm.at[INNER:], weight_ref)],
        [
            (pos_hbm.at[pl.ds(own_token, own)], pos_own_ref),
            (wsi_hbm.at[:WIDE], wsi_ref),
        ]
        + [pair for pair in zip(sources, held[8:]) if pair[1] is not embed_ref],
    ]
    count = 0
    for i, stage in enumerate(stages):
        stages[i] = [pltpu.make_async_copy(*pair, sems.at[count + j]) for j, pair in enumerate(stage)]
        count += len(stage)
    for stage in stages:
        start_all(stage)
    for copy in stages[0]:
        copy.wait()
    lat = placed(queue_ref[0], 0)
    for g in range(1, frames):
        lat = lat + placed(queue_ref[g], g * tokens)
    low = section == 0
    mine = pick(lat, low, frames)
    lat_ref[...] = jnp.where(low, mine, pltpu.roll(mine, LANES // 2, 1))
    piece, rest = make_piece(lat, own_hidden(lat, embed_ref[...], pos_shard_ref[...]))
    rest = pick(rest, section != 0, frames)
    rest = rest[: CH // 2] + pltpu.roll(rest[CH // 2 :], LANES // 2, 1)
    piece = jnp.concatenate([piece, rest], axis=0).astype(bf16)
    for peer in range(piece_ref.shape[0]):
        piece_ref[peer] = piece
    gain_rows_ref[...] = gain_products(gains_ref[...])
    high, low = split(turned_ref[...])
    final = jnp.concatenate([high.astype(f32), low.astype(f32), jnp.zeros((LANES - 2 * CH, D), f32)], axis=0)
    final_ref[...] = final.T.astype(bf16)
    lanes = lat_ref.shape[1]
    slot = lax.broadcasted_iota(jnp.int32, (1, lanes), 1) // (lanes // slots)
    times = jnp.zeros((1, lanes), f32)
    stride = jnp.zeros((1, lanes), f32)
    before = 0.0
    for q in range(slots):
        time = (levels_ref[q].astype(f32) + 1.0) / LEVELS
        times = jnp.where(slot == q, time, times)
        stride = jnp.where(slot == q, time - before, stride)
        before = time
    rates_ref[...] = jnp.concatenate([times, stride, jnp.zeros((6, lanes), f32)], axis=0)
    for copy in stages[1]:
        copy.wait()
    for q in range(slots):
        mods_ref[q] = table_ref[levels_ref[q]]
    build_plans(mods_ref, pos_ref, embed_ref, weight_ref, left_ref, key_plan_ref, value_plan_ref)
    for copy in stages[2]:
        copy.wait()


def step_kernel(pieces_ref, lat_ref, *refs, step):
    first, last = step == 0, step == STEPS - 1
    held, later, refs = refs[:HELD], refs[HELD : HELD + LATER], refs[HELD + LATER :]
    outs, refs = refs[:2], refs[2:]
    copies = []
    if first:
        later_hbm, later, refs = later, refs[:LATER], refs[LATER:]
        copies = [pltpu.make_async_copy(*pair, refs[-1].at[i]) for i, pair in enumerate(zip(later_hbm, later))]
        start_all(copies)
    cross_ref, mixed_ref, keys_ref, squares_ref = refs[:4]
    wso_ref, wti_ref, wto_ref = later
    (
        key_plan_ref,
        value_plan_ref,
        mods_ref,
        gain_rows_ref,
        rates_ref,
        final_ref,
        pos_own_ref,
        wsi_ref,
        same_head_ref,
        embed_ref,
        head_sum_ref,
        pos_frame_ref,
        noise_ref,
    ) = held
    lanes = lat_ref.shape[1]
    blocks, slots = key_plan_ref.shape[:2]
    frames = slots * FRAMES
    own = lanes // frames
    devices = pieces_ref.shape[0]
    tokens = LANES
    per_block = devices // blocks
    section, sections = lax.axis_index("tm"), lax.axis_size("tm")
    low = section == 0
    mods = [mods_ref[:, row] for row in range(8)]
    same_head = same_head_ref[...]

    lat = lat_ref[...]
    if first:
        partner = lax.axis_index("space") * sections + (sections - 1 - section)
        lat = lat + partner_latents(pieces_ref[partner].astype(f32), frames // sections, low)

    def own_side():
        hidden = own_hidden(lat, embed_ref[...], pos_own_ref[...])
        yield hidden
        normed = normalized(hidden)
        yield None
        normed = modulated(normed, mods[0], mods[1]).astype(bf16)
        yield None
        queries = dot_nt(normed, wsi_ref[...])
        yield None
        yield head_normed(queries, same_head, gain_rows_ref[0:1])

    for group in range(devices // PACK):
        stacked = pieces_ref[group * PACK : (group + 1) * PACK].astype(f32)
        if not first:
            stacked = jnp.concatenate([stacked, jnp.zeros((PACK, PIECE - SHORT, lanes), f32)], axis=1)
        stacked = stacked.reshape(LANES, lanes).T
        for part in range(PACK):
            cross_ref[group * PACK + part] = pltpu.roll(stacked, LANES - part * PIECE, 1) if part else stacked

    def turned(b, g):
        if first:
            held, rows = frames // sections, own * sections
            peers = range(b * per_block + g // held, (b + 1) * per_block, sections)
            at = g % held * rows
        else:
            rows, peers, at = own, range(b * per_block, (b + 1) * per_block), g * own
        return [cross_ref[peer, at : at + rows] for peer in peers]

    row = lax.broadcasted_iota(jnp.int32, (tokens, tokens), 0)
    column = lax.broadcasted_iota(jnp.int32, (tokens, tokens), 1)
    diagonal = row == column
    scale_lane = (lax.broadcasted_iota(jnp.int32, (8, LANES), 1) == CH + 2).astype(bf16)
    row = lax.broadcasted_iota(jnp.int32, (LANES, FRAMES * PIECE), 0)
    column = lax.broadcasted_iota(jnp.int32, (LANES, FRAMES * PIECE), 1)
    own_piece = (row // (HEADS * own) == column // PIECE).astype(f32)
    masks = head_masks()
    head_sum = head_sum_ref[...]

    of_frame = [slice(f * tokens, (f + 1) * tokens) for f in range(FRAMES)]
    pairs = [(b, q) for q in range(slots) for b in range(blocks)]
    rows, scales, weights, totals = {}, {}, {}, [0.0] * slots
    steps = own_side()
    hidden = next(steps)
    for b in range(blocks):
        for q in range(slots):
            tiles = [tile for f in range(FRAMES) for tile in turned(b, q * FRAMES + f)]
            rows[b, q] = jnp.concatenate(tiles, axis=0).astype(bf16)
            scales[b, q] = dot_nt(scale_lane, rows[b, q])[:1]
        for q in range(slots):
            marked = [jnp.where(diagonal, scales[b, q][:, at], 0.0).astype(bf16) for at in of_frame]
            left = jnp.concatenate([jnp.concatenate(marked, axis=0), rows[b, q][:, :PIECE]], axis=1)
            keys = dot(left, key_plan_ref[b, q])
            squares_ref[q] = (keys * keys).astype(bf16)
            keys_ref[q] = keys.astype(bf16)
            if b == 0:
                queries = next(steps, None) if q < 4 else queries
        for q in range(slots):
            sums = dot(jnp.concatenate([squares_ref[q, at] for at in of_frame], axis=1), head_sum)
            scores = []
            for f, at in enumerate(of_frame):
                g = q * FRAMES + f
                spread = (queries[g * own : (g + 1) * own][None] * masks).reshape(HEADS * own, WIDE).astype(bf16)
                scores.append(dot_nt(keys_ref[q, at], spread))
            scores = jnp.concatenate(scores, axis=1)
            weights[b, q] = jnp.exp(scores * lax.rsqrt(sums * (1.0 / HD) + epsilon))
            totals[q] = totals[q] + jnp.sum(weights[b, q], axis=0, keepdims=True)
    by_query, groups = {}, {}
    for b, q in pairs:
        by_query[b, q] = (weights[b, q] * (1.0 / totals[q])).T
    for b, q in pairs:
        pieces = jnp.concatenate([rows[b, q][at, :PIECE] for at in of_frame], axis=1)
        groups[b, q] = dot(by_query[b, q].astype(bf16), pieces) * own_piece
    for q in range(slots):
        mixed = 0.0
        for b in range(blocks):
            scaled = by_query[b, q].reshape(FRAMES, HEADS * own, tokens)
            scaled = jnp.concatenate([scaled[f] * scales[b, q][:, at] for f, at in enumerate(of_frame)], axis=0)
            met = jnp.concatenate([scaled.astype(bf16), groups[b, q].astype(bf16)], axis=1)
            mixed = mixed + dot(met, value_plan_ref[b, q])
        for f in range(FRAMES):
            g = q * FRAMES + f
            tiles = []
            for start in range(0, INNER, LANES):
                stop = min(start + LANES, INNER)
                parts = [
                    mixed[(f * HEADS + h) * own : (f * HEADS + h + 1) * own, start:stop] * masks[h, :, start:stop]
                    for h in range(start // HD, -(-stop // HD))
                ]
                tiles.append(functools.reduce(jnp.add, parts))
            mixed_ref[g * own : (g + 1) * own] = jnp.concatenate(tiles, axis=1)
    mixed = mixed_ref[...].astype(bf16)

    for copy in copies:
        copy.wait()
    branch = dot(mixed, wso_ref[...])
    hidden = (
        hidden.reshape(slots, FRAMES, own, D)
        + mods[2][:, None, None, :] * branch.reshape(slots, FRAMES, own, D)
        + pos_frame_ref[...].reshape(slots, FRAMES, 1, D)
    ).reshape(lanes, D)
    normed = modulated(normalized(hidden), mods[3], mods[4]).astype(bf16)
    queries = dot_nt(normed, wti_ref[:WIDE])
    keys = dot_nt(normed, wti_ref[INNER : INNER + WIDE])
    both = head_normed(jnp.concatenate([queries, keys], axis=0), same_head, 1.0)
    queries = both[:lanes] * gain_rows_ref[1:2]
    keys = both[lanes:].astype(bf16)
    values = dot_nt(normed, wti_ref[2 * INNER :]).astype(bf16)
    row = lax.broadcasted_iota(jnp.int32, (lanes, lanes), 0)
    column = lax.broadcasted_iota(jnp.int32, (lanes, lanes), 1)
    same_token = (lax.rem(row, own) == lax.rem(column, own)).astype(f32)
    windows = [(h * HD // LANES * LANES, -(-(h + 1) * HD // LANES) * LANES) for h in range(HEADS)]
    scores = []
    for h, (start, stop) in enumerate(windows):
        spread = (queries[:, start:stop] * masks[h, :, start:stop]).astype(bf16)
        scores.append(dot_nt(spread, keys[:, start:stop]))
    weights = [jnp.exp(score) * same_token for score in scores]
    scales = [1.0 / jnp.sum(weight, axis=-1, keepdims=True) for weight in weights]
    results = []
    for (start, stop), weight in zip(windows, weights):
        results.append(dot(weight.astype(bf16), values[:, start : min(stop, INNER)]))
    parts = [[] for _ in range(WIDE // LANES)]
    for h, (start, stop) in enumerate(windows):
        stop = min(stop, INNER)
        result = results[h] * scales[h] * masks[h, :, start:stop]
        for tile in range(start // LANES, -(-stop // LANES)):
            parts[tile].append(result[:, tile * LANES - start : min((tile + 1) * LANES, stop) - start])
    mixed = jnp.concatenate([functools.reduce(jnp.add, part).astype(bf16) for part in parts], axis=1)
    branch = dot(mixed, wto_ref[...])
    hidden = hidden + (mods[5][:, None, :] * branch.reshape(slots, FRAMES * own, D)).reshape(lanes, D)
    final = modulated(normalized(hidden), mods[6], mods[7])
    final_high, final_low = split(final)
    products = dot(jnp.concatenate([final_high, final_low], axis=0), final_ref[...])
    by_high, by_low = products[:lanes].T, products[lanes:].T
    velocity = by_high[:CH] + by_high[CH : 2 * CH] + by_low[:CH]

    slot = lax.broadcasted_iota(jnp.int32, (1, lanes), 1) // (FRAMES * own)
    times, stride = rates_ref[0:1], rates_ref[1:2]
    noise = 0.0
    for f in range(FRAMES):
        block = noise_ref[step, f]
        block = jnp.where(low, block[:, :own], block[:, own:])
        noise = noise + placed(block, (frames - FRAMES + f) * own)
    moved = pltpu.roll(lat - stride * velocity, lanes - FRAMES * own, 1)
    moved = jnp.where(slot == slots - 1, noise, moved)
    if not last:
        lat_out, piece_out = outs
        lat_out[...] = moved
        piece = make_piece(moved, own_hidden(moved, embed_ref[...], pos_own_ref[...]))[0].astype(bf16)
        for peer in range(devices):
            piece_out[peer] = piece
    else:
        keep_out, send_out = outs
        held = frames // sections
        for i, result in enumerate((moved, lat - times * velocity)):
            for g in range(held):
                here = [
                    pltpu.roll(result, (lanes - (half * held + g) * own) % lanes, 1)[:, :own] for half in range(2)
                ]
                for out, block in (
                    (keep_out, jnp.where(low, here[0], here[1])),
                    (send_out, jnp.where(low, here[1], here[0])),
                ):
                    zeros = jnp.zeros_like(block)
                    out[i, g] = jnp.concatenate(
                        [jnp.where(low, block, zeros), jnp.where(low, zeros, block)], axis=1
                    )


def per_device(
    queue_latents,
    fresh_noise,
    slot_levels,
    level_table,
    embed_weight,
    spatial_in,
    spatial_out,
    temporal_in,
    temporal_out,
    norm_gains,
    final_weight,
):
    blocks, _, _, tokens = queue_latents.shape
    sections = lax.axis_size("tm")
    shards = lax.axis_size("space")
    axes = ("space", "tm")
    devices = sections * shards
    own = tokens // sections
    slots = blocks * sections
    frames = slots * FRAMES
    lanes = frames * own
    space_tokens = tokens * shards
    token_blocks = space_tokens // LANES
    partner = [(i, sections - 1 - i) for i in range(sections)]

    pos = jnp.asarray(sincos(space_tokens, D).astype(np.float32))
    pos_frame = jnp.asarray(sincos(frames, D).astype(np.float32))
    head = np.where(np.arange(WIDE) < INNER, np.arange(WIDE) // HD, -1)
    same_head = jnp.asarray(((head[:, None] == head[None, :]) & (head >= 0)[None, :]).astype(np.float32), bf16)
    lane = np.arange(LANES)
    lane_head = lane // own % HEADS
    lane_frame = lane // (HEADS * own)
    head_sum = np.concatenate(
        [(head[:, None] == lane_head[None, :]) & (lane_frame == f)[None, :] for f in range(FRAMES)], axis=0
    )
    head_sum = jnp.asarray(head_sum.astype(np.float32), bf16)

    final_turned = jnp.transpose(final_weight)
    spatial_turned = jnp.transpose(spatial_in)
    temporal_turned = jnp.transpose(temporal_in)

    vmem = pl.BlockSpec(memory_space=pltpu.VMEM)
    hbm = pl.BlockSpec(memory_space=pltpu.HBM)
    dma = pltpu.SemaphoreType.DMA

    def call(kernel, out_shape, arguments, scratch, name):
        spaces = {id(vmem): pltpu.VMEM, id(hbm): pltpu.HBM}
        values = [pltpu.with_memory_space_constraint(value, spaces[id(spec)]) for value, spec in arguments]
        return pl.pallas_call(
            kernel,
            out_shape=out_shape,
            in_specs=[spec for _, spec in arguments],
            out_specs=[vmem] * len(out_shape),
            scratch_shapes=scratch,
            compiler_params=pltpu.CompilerParams(vmem_limit_bytes=GRANT),
            name=name,
        )(*values)

    flat = pltpu.VMEM((CH, lanes), f32)
    first_piece_shape = pltpu.VMEM((devices, PIECE, lanes), bf16)
    piece_shape = pltpu.VMEM((devices, SHORT, lanes), bf16)
    queue = queue_latents.reshape(blocks * FRAMES, CH, tokens)
    copied = [
        same_head,
        embed_weight,
        head_sum,
        pos_frame,
        fresh_noise,
    ]
    later = [spatial_out, temporal_turned, temporal_out]
    held = [
        pltpu.VMEM((token_blocks, slots, PLAN, WIDE), bf16),
        pltpu.VMEM((token_blocks, slots, LANES + FRAMES * PIECE, INNER), bf16),
        pltpu.VMEM((slots, 8, D), f32),
        pltpu.VMEM((8, WIDE), f32),
        pltpu.VMEM((8, lanes), f32),
        pltpu.VMEM((D, LANES), bf16),
        pltpu.VMEM((own, D), f32),
        pltpu.VMEM((WIDE, D), bf16),
        *(pltpu.VMEM(x.shape, x.dtype) for x in copied),
    ]
    *held, pieces, lat = call(
        prepare_kernel,
        held + [first_piece_shape, flat],
        [(x, hbm) for x in (slot_levels, queue, pos, level_table, norm_gains, final_turned, spatial_turned, *copied)],
        [
            pltpu.SMEM((slots,), jnp.int32),
            pltpu.VMEM(level_table.shape, f32),
            pltpu.VMEM(queue.shape, f32),
            pltpu.VMEM((space_tokens, D), f32),
            pltpu.VMEM((tokens, D), f32),
            pltpu.VMEM((4, HD), f32),
            pltpu.VMEM((CH, D), f32),
            pltpu.VMEM((2 * INNER, D), bf16),
            pltpu.VMEM((slots * PLAN, D), bf16),
            dma((11 + COPIED,)),
        ],
        "slot_plan",
    )
    result_shape = pltpu.VMEM((2, blocks * FRAMES, CH, tokens), f32)
    for step in range(STEPS):
        last = step == STEPS - 1
        gathered = lax.all_to_all(pieces, axes, split_axis=0, concat_axis=0, tiled=True)
        out_shape = [result_shape] * 2 if last else [flat, piece_shape]
        scratch = [pltpu.VMEM((devices, lanes, LANES), f32), pltpu.VMEM((lanes, INNER), f32)]
        scratch += [pltpu.VMEM((slots, FRAMES * LANES, WIDE), bf16)] * 2
        if step == 0:
            out_shape += [pltpu.VMEM(x.shape, x.dtype) for x in later]
            scratch += [dma((LATER,))]
        lat, pieces, *brought = call(
            functools.partial(step_kernel, step=step),
            out_shape,
            [(x, vmem) for x in (gathered, lat, *held)] + [(x, hbm if step == 0 else vmem) for x in later],
            scratch,
            "denoise_step",
        )
        later = brought or later

    received = lax.ppermute(pieces, "tm", partner)
    return tuple((lat[i] + received[i]).reshape(queue_latents.shape) for i in range(2))


def solution(mesh):
    return jax.shard_map(
        per_device,
        mesh=mesh,
        in_specs=(
            P(("clip", "tm"), None, None, "space"),
            P("clip", None, None, "space"),
            P("clip"),
            P(),
            P(),
            P(),
            P(),
            P(),
            P(),
            P(),
            P(),
        ),
        out_specs=(P(("clip", "tm"), None, None, "space"), P(("clip", "tm"), None, None, "space")),
        check_vma=False,
    )
```

```python
import functools
import math

import jax
import jax.numpy as jnp
import numpy as np
from jax import lax
from jax.experimental import pallas as pl
from jax.experimental.pallas import tpu as pltpu
from jax.sharding import PartitionSpec as P

D = 1152
HEADS = 8
HD = 72
INNER = HEADS * HD
CH = 16
FRAMES = 2
STEPS = 3
LEVELS = 16

LANES = 128
WIDE = -(-INNER // LANES) * LANES
PIECE = 32
SHORT = PIECE - CH // 2
PACK = LANES // PIECE
PLAN = LANES + PIECE

GRANT = 26 * 1024 * 1024

epsilon = 1e-06
f32 = jnp.float32
bf16 = jnp.bfloat16


def dot(a, b):
    return lax.dot_general(a, b, (((1,), (0,)), ((), ())), preferred_element_type=f32)


def dot_nt(a, b):
    return lax.dot_general(a, b, (((1,), (1,)), ((), ())), preferred_element_type=f32)


def split(x):
    high = x.astype(bf16)
    return high, (x - high.astype(f32)).astype(bf16)


def sincos(count, width):
    half = width // 2
    rates = np.exp(-np.log(10000.0) * np.arange(half) / half)
    angles = np.arange(count)[:, None] * rates[None, :]
    return np.concatenate([np.sin(angles), np.cos(angles)], axis=-1)


def head_masks():
    shape = (HEADS, 1, WIDE)
    head = lax.broadcasted_iota(jnp.int32, shape, 0)
    position = lax.broadcasted_iota(jnp.int32, shape, 2)
    return ((position >= head * HD) & (position < (head + 1) * HD)).astype(f32)


def normalized(values):
    centered = values - jnp.mean(values, axis=-1, keepdims=True)
    return centered * lax.rsqrt(jnp.mean(centered * centered, axis=-1, keepdims=True) + epsilon)


def modulated(values, shift, scale):
    slots = shift.shape[0]
    out = values.reshape(slots, -1, D) * (1.0 + scale)[:, None, :] + shift[:, None, :]
    return out.reshape(values.shape)


def own_hidden(lat, embed, pos_own):
    lanes = lat.shape[1]
    lat_high, lat_low = split(lat)
    lat_high = lat_high.astype(f32)
    zeros = jnp.zeros((LANES - 3 * CH, lanes), f32)
    rows = jnp.concatenate([lat_high, lat_low.astype(f32), lat_high, zeros], axis=0).T.astype(bf16)
    embed_high, embed_low = split(embed)
    weights = jnp.concatenate(
        [embed_high, embed_high, embed_low, jnp.zeros((LANES - 3 * CH, D), bf16)], axis=0
    )
    own = pos_own.shape[0]
    return (dot(rows, weights).reshape(lanes // own, own, D) + pos_own[None]).reshape(lanes, D)


def make_piece(lat, hidden):
    lanes = lat.shape[1]
    centered = hidden - jnp.mean(hidden, axis=-1, keepdims=True)
    scale = lax.rsqrt(jnp.mean(centered * centered, axis=-1, keepdims=True) + epsilon)
    scale = jnp.broadcast_to(scale, (lanes, LANES)).T[:1].astype(bf16).astype(f32)
    scaled = lat * scale
    high = scaled.astype(bf16).astype(f32)
    zeros = jnp.zeros((SHORT - CH - 3, lanes), f32)
    return jnp.concatenate([high, jnp.ones((2, lanes), f32), scale, zeros], axis=0), scaled - high


def pick(values, low, frames):
    own = LANES // 2 // frames
    lane = lax.broadcasted_iota(jnp.int32, (1, LANES), 1)
    values = jnp.where(low, values, pltpu.roll(values, LANES - own, 1))
    out = jnp.where(lane // own == 0, values, 0.0)
    for g in range(1, frames):
        out = out + jnp.where(lane // own == g, pltpu.roll(values, LANES - g * own, 1), 0.0)
    return out


def placed(block, start):
    rows, width = block.shape
    wide = jnp.concatenate([block, jnp.zeros((rows, LANES - width), f32)], axis=1)
    return pltpu.roll(wide, start, 1) if start else wide


HELD = 13
COPIED = 5
LATER = 3


def start_all(copies):
    for copy in copies:
        copy.start()


def build_plans(mods_ref, pos_ref, embed_ref, weight_ref, left_ref, key_plan_ref, value_plan_ref, query_ref):
    blocks, slots = key_plan_ref.shape[:2]
    tokens = LANES
    embed = embed_ref[...]
    embed = embed - jnp.mean(embed, axis=-1, keepdims=True)
    row = lax.broadcasted_iota(jnp.int32, (PIECE - CH, 1), 0)
    part = lax.broadcasted_iota(jnp.int32, (PIECE, 1), 0)
    for b in range(blocks):
        pos = pos_ref[b * tokens : (b + 1) * tokens]
        pos = pos - jnp.mean(pos, axis=-1, keepdims=True)
        for q in range(slots):
            scale = 1.0 + mods_ref[q, 1:2]
            shift_rows = jnp.where(row < 2, mods_ref[q, 0:1], 0.0)
            left_ref[q * PLAN : (q + 1) * PLAN] = jnp.concatenate(
                [pos * scale, embed * scale, shift_rows], axis=0
            ).astype(bf16)
        for ref, weight in ((key_plan_ref, weight_ref[INNER : 2 * INNER]), (value_plan_ref, weight_ref[2 * INNER :])):
            product = dot_nt(left_ref[...], weight)
            for q in range(slots):
                rows = product[q * PLAN : (q + 1) * PLAN]
                group = rows[tokens:]
                group = jnp.where(part == CH + 1, group - group.astype(bf16).astype(f32), group).astype(bf16)
                copies = (ref.shape[2] - tokens) // PIECE
                rows = jnp.concatenate([rows[:tokens].astype(bf16)] + [group] * copies, axis=0)
                if ref.shape[3] > INNER:
                    rows = jnp.concatenate([rows, jnp.zeros((rows.shape[0], ref.shape[3] - INNER), bf16)], axis=1)
                ref[b, q] = rows
                if b == 0 and ref is key_plan_ref:
                    for start in range(q * LANES, WIDE, slots * LANES):
                        query_ref[:, start : start + LANES] = weight_ref[start : start + LANES].T


def gain_products(gains):
    products = jnp.concatenate(
        [gains[0:1] * gains[1:2], gains[2:3] * gains[3:4], jnp.zeros((6, HD), f32)], axis=0
    ) / math.sqrt(HD)
    place = lax.broadcasted_iota(jnp.int32, (HD, WIDE), 1)
    feature = lax.broadcasted_iota(jnp.int32, (HD, WIDE), 0)
    spread = ((place < INNER) & (lax.rem(place, HD) == feature)).astype(f32)
    return lax.dot_general(
        products, spread, (((1,), (0,)), ((), ())), preferred_element_type=f32, precision=lax.Precision.HIGHEST
    )


def head_normed(values, same_head, gain):
    values = values.astype(bf16).astype(f32)
    total = dot((values * values).astype(bf16), same_head)
    return values * lax.rsqrt(total * (1.0 / HD) + epsilon) * gain


def partner_latents(piece, frames, low):
    lane = lax.broadcasted_iota(jnp.int32, (1, LANES), 1)
    chosen = pick(piece[:SHORT], low, frames)
    rest = piece[SHORT:]
    rest = jnp.concatenate([rest, pltpu.roll(rest, LANES // 2, 1)], axis=0)
    lat = (chosen[:CH] + rest) / chosen[CH + 2 : CH + 3]
    lat = jnp.where(lane < LANES // 2, lat, 0.0)
    return jnp.where(low, pltpu.roll(lat, LANES // 2, 1), lat)


def prepare_kernel(levels_hbm, queue_hbm, pos_hbm, table_hbm, gains_hbm, final_hbm, wsi_hbm, *refs):
    sources, held = refs[:COPIED], refs[COPIED : COPIED + HELD]
    piece_ref, lat_ref, levels_ref, table_ref, queue_ref, pos_ref, pos_shard_ref, gains_ref, turned_ref, weight_ref, left_ref, sems = refs[
        COPIED + HELD :
    ]
    key_plan_ref, value_plan_ref, mods_ref, gain_rows_ref, rates_ref, final_ref = held[:6]
    pos_own_ref, wsi_ref, _, embed_ref = held[6:10]
    slots = mods_ref.shape[0]
    frames, _, tokens = queue_ref.shape
    own = pos_own_ref.shape[0]
    section, sections = lax.axis_index("tm"), lax.axis_size("tm")
    shard_token = pl.multiple_of(lax.axis_index("space") * tokens, 8)
    own_token = pl.multiple_of(shard_token + section * own, 8)
    stages = [
        [
            (levels_hbm, levels_ref),
            (queue_hbm, queue_ref),
            (sources[1], embed_ref),
            (pos_hbm.at[pl.ds(shard_token, tokens)], pos_shard_ref),
            (gains_hbm, gains_ref),
            (final_hbm, turned_ref),
        ],
        [(table_hbm, table_ref), (pos_hbm, pos_ref), (wsi_hbm, weight_ref)],
        [
            (pos_hbm.at[pl.ds(own_token, own)], pos_own_ref),
        ]
        + [pair for pair in zip(sources, held[8:]) if pair[1] is not embed_ref],
    ]
    count = 0
    for i, stage in enumerate(stages):
        stages[i] = [pltpu.make_async_copy(*pair, sems.at[count + j]) for j, pair in enumerate(stage)]
        count += len(stage)
    for stage in stages:
        start_all(stage)
    for copy in stages[0]:
        copy.wait()
    lat = placed(queue_ref[0], 0)
    for g in range(1, frames):
        lat = lat + placed(queue_ref[g], g * tokens)
    low = section == 0
    mine = pick(lat, low, frames)
    lat_ref[...] = jnp.where(low, mine, pltpu.roll(mine, LANES // 2, 1))
    piece, rest = make_piece(lat, own_hidden(lat, embed_ref[...], pos_shard_ref[...]))
    rest = pick(rest, section != 0, frames)
    rest = rest[: CH // 2] + pltpu.roll(rest[CH // 2 :], LANES // 2, 1)
    piece = jnp.concatenate([piece, rest], axis=0).astype(bf16)
    for peer in range(piece_ref.shape[0]):
        piece_ref[peer] = piece
    gain_rows_ref[...] = gain_products(gains_ref[...])
    high, low = split(turned_ref[...])
    final = jnp.concatenate([high.astype(f32), low.astype(f32), jnp.zeros((LANES - 2 * CH, D), f32)], axis=0)
    final_ref[...] = final.T.astype(bf16)
    lanes = lat_ref.shape[1]
    slot = lax.broadcasted_iota(jnp.int32, (1, lanes), 1) // (lanes // slots)
    times = jnp.zeros((1, lanes), f32)
    stride = jnp.zeros((1, lanes), f32)
    before = 0.0
    for q in range(slots):
        time = (levels_ref[q].astype(f32) + 1.0) / LEVELS
        times = jnp.where(slot == q, time, times)
        stride = jnp.where(slot == q, time - before, stride)
        before = time
    rates_ref[...] = jnp.concatenate([times, stride, jnp.zeros((6, lanes), f32)], axis=0)
    for copy in stages[1]:
        copy.wait()
    for q in range(slots):
        mods_ref[q] = table_ref[levels_ref[q]]
    build_plans(mods_ref, pos_ref, embed_ref, weight_ref, left_ref, key_plan_ref, value_plan_ref, wsi_ref)
    for copy in stages[2]:
        copy.wait()


def step_kernel(pieces_ref, lat_ref, *refs, step):
    first, last = step == 0, step == STEPS - 1
    held, later, refs = refs[:HELD], refs[HELD : HELD + LATER], refs[HELD + LATER :]
    outs, refs = refs[:2], refs[2:]
    copies = []
    if first:
        later_hbm, later, refs = later, refs[:LATER], refs[LATER:]
        wti_raw = refs[-2]
        targets = (later[0], wti_raw, later[2])
        copies = [pltpu.make_async_copy(*pair, refs[-1].at[i]) for i, pair in enumerate(zip(later_hbm, targets))]
        start_all(copies)
    cross_ref, mixed_ref, keys_ref, squares_ref = refs[:4]
    wso_ref, wti_ref, wto_ref = later
    (
        key_plan_ref,
        value_plan_ref,
        mods_ref,
        gain_rows_ref,
        rates_ref,
        final_ref,
        pos_own_ref,
        wsi_ref,
        same_head_ref,
        embed_ref,
        head_sum_ref,
        pos_frame_ref,
        noise_ref,
    ) = held
    lanes = lat_ref.shape[1]
    blocks, slots = key_plan_ref.shape[:2]
    frames = slots * FRAMES
    own = lanes // frames
    devices = pieces_ref.shape[0]
    tokens = LANES
    per_block = devices // blocks
    section, sections = lax.axis_index("tm"), lax.axis_size("tm")
    low = section == 0
    mods = [mods_ref[:, row] for row in range(8)]
    same_head = same_head_ref[...]

    lat = lat_ref[...]
    if first:
        partner = lax.axis_index("space") * sections + (sections - 1 - section)
        lat = lat + partner_latents(pieces_ref[partner].astype(f32), frames // sections, low)

    def own_side():
        hidden = own_hidden(lat, embed_ref[...], pos_own_ref[...])
        yield hidden
        normed = normalized(hidden)
        yield None
        normed = modulated(normed, mods[0], mods[1]).astype(bf16)
        yield None
        queries = dot(normed, wsi_ref[...])
        yield None
        yield head_normed(queries, same_head, gain_rows_ref[0:1])

    for group in range(devices // PACK):
        stacked = pieces_ref[group * PACK : (group + 1) * PACK].astype(f32)
        if not first:
            stacked = jnp.concatenate([stacked, jnp.zeros((PACK, PIECE - SHORT, lanes), f32)], axis=1)
        stacked = stacked.reshape(LANES, lanes).T
        for part in range(PACK):
            cross_ref[group * PACK + part] = pltpu.roll(stacked, LANES - part * PIECE, 1) if part else stacked

    def turned(b, g):
        if first:
            held, rows = frames // sections, own * sections
            peers = range(b * per_block + g // held, (b + 1) * per_block, sections)
            at = g % held * rows
        else:
            rows, peers, at = own, range(b * per_block, (b + 1) * per_block), g * own
        return [cross_ref[peer, at : at + rows] for peer in peers]

    row = lax.broadcasted_iota(jnp.int32, (tokens, tokens), 0)
    column = lax.broadcasted_iota(jnp.int32, (tokens, tokens), 1)
    diagonal = row == column
    scale_lane = (lax.broadcasted_iota(jnp.int32, (8, LANES), 1) == CH + 2).astype(bf16)
    row = lax.broadcasted_iota(jnp.int32, (LANES, FRAMES * PIECE), 0)
    column = lax.broadcasted_iota(jnp.int32, (LANES, FRAMES * PIECE), 1)
    own_piece = (row // (HEADS * own) == column // PIECE).astype(f32)
    masks = head_masks()
    head_sum = head_sum_ref[...]

    turns = []
    if first:
        for i, width in enumerate((WIDE, WIDE, INNER)):
            for start in range(0, width, LANES):
                stop = min(start + LANES, width)
                turns.append((slice(i * WIDE + start, i * WIDE + stop), slice(i * INNER + start, i * INNER + stop)))
    of_frame = [slice(f * tokens, (f + 1) * tokens) for f in range(FRAMES)]
    pairs = [(b, q) for q in range(slots) for b in range(blocks)]
    rows, scales, weights, totals = {}, {}, {}, [0.0] * slots
    steps = own_side()
    hidden = next(steps)
    for b in range(blocks):
        for q in range(slots):
            tiles = [tile for f in range(FRAMES) for tile in turned(b, q * FRAMES + f)]
            rows[b, q] = jnp.concatenate(tiles, axis=0).astype(bf16)
            scales[b, q] = dot_nt(scale_lane, rows[b, q])[:1]
        for q in range(slots):
            marked = [jnp.where(diagonal, scales[b, q][:, at], 0.0).astype(bf16) for at in of_frame]
            left = jnp.concatenate([jnp.concatenate(marked, axis=0), rows[b, q][:, :PIECE]], axis=1)
            keys = dot(left, key_plan_ref[b, q])
            squares_ref[q] = (keys * keys).astype(bf16)
            keys_ref[q] = keys.astype(bf16)
            if b == 0:
                queries = next(steps, None) if q < 4 else queries
        if b == blocks - 1:
            for copy in copies:
                copy.wait()
        for q in range(slots):
            if b == blocks - 1:
                for to, source in turns[q :: slots]:
                    wti_ref[:, to] = wti_raw[source].T
            sums = dot(jnp.concatenate([squares_ref[q, at] for at in of_frame], axis=1), head_sum)
            scores = []
            for f, at in enumerate(of_frame):
                g = q * FRAMES + f
                spread = (queries[g * own : (g + 1) * own][None] * masks).reshape(HEADS * own, WIDE).astype(bf16)
                scores.append(dot_nt(keys_ref[q, at], spread))
            scores = jnp.concatenate(scores, axis=1)
            weights[b, q] = jnp.exp(scores * lax.rsqrt(sums * (1.0 / HD) + epsilon))
            totals[q] = totals[q] + jnp.sum(weights[b, q], axis=0, keepdims=True)
    by_query, groups = {}, {}
    for b, q in pairs:
        by_query[b, q] = (weights[b, q] * (1.0 / totals[q])).T
    for b, q in pairs:
        pieces = jnp.concatenate([rows[b, q][at, :PIECE] for at in of_frame], axis=1)
        groups[b, q] = dot(by_query[b, q].astype(bf16), pieces) * own_piece
    for q in range(slots):
        mixed = 0.0
        for b in range(blocks):
            scaled = by_query[b, q].reshape(FRAMES, HEADS * own, tokens)
            scaled = jnp.concatenate([scaled[f] * scales[b, q][:, at] for f, at in enumerate(of_frame)], axis=0)
            met = jnp.concatenate([scaled.astype(bf16), groups[b, q].astype(bf16)], axis=1)
            mixed = mixed + dot(met, value_plan_ref[b, q])
        for f in range(FRAMES):
            g = q * FRAMES + f
            tiles = []
            for start in range(0, INNER, LANES):
                stop = min(start + LANES, INNER)
                parts = [
                    mixed[(f * HEADS + h) * own : (f * HEADS + h + 1) * own, start:stop] * masks[h, :, start:stop]
                    for h in range(start // HD, -(-stop // HD))
                ]
                tiles.append(functools.reduce(jnp.add, parts))
            mixed_ref[g * own : (g + 1) * own] = jnp.concatenate(tiles, axis=1)
    mixed = mixed_ref[...].astype(bf16)

    branch = dot(mixed, wso_ref[...])
    hidden = (
        hidden.reshape(slots, FRAMES, own, D)
        + mods[2][:, None, None, :] * branch.reshape(slots, FRAMES, own, D)
        + pos_frame_ref[...].reshape(slots, FRAMES, 1, D)
    ).reshape(lanes, D)
    normed = modulated(normalized(hidden), mods[3], mods[4]).astype(bf16)
    projected = dot(normed, wti_ref[...])
    queries, keys = projected[:, :WIDE], projected[:, WIDE : 2 * WIDE]
    values = projected[:, 2 * WIDE :].astype(bf16)
    both = head_normed(jnp.concatenate([queries, keys], axis=0), same_head, 1.0)
    queries = both[:lanes] * gain_rows_ref[1:2]
    keys = both[lanes:].astype(bf16)
    row = lax.broadcasted_iota(jnp.int32, (lanes, lanes), 0)
    column = lax.broadcasted_iota(jnp.int32, (lanes, lanes), 1)
    same_token = (lax.rem(row, own) == lax.rem(column, own)).astype(f32)
    windows = [(h * HD // LANES * LANES, -(-(h + 1) * HD // LANES) * LANES) for h in range(HEADS)]
    scores = []
    for h, (start, stop) in enumerate(windows):
        spread = (queries[:, start:stop] * masks[h, :, start:stop]).astype(bf16)
        scores.append(dot_nt(spread, keys[:, start:stop]))
    weights = [jnp.exp(score) * same_token for score in scores]
    scales = [1.0 / jnp.sum(weight, axis=-1, keepdims=True) for weight in weights]
    results = []
    for (start, stop), weight in zip(windows, weights):
        results.append(dot(weight.astype(bf16), values[:, start : min(stop, INNER)]))
    parts = [[] for _ in range(WIDE // LANES)]
    for h, (start, stop) in enumerate(windows):
        stop = min(stop, INNER)
        result = results[h] * scales[h] * masks[h, :, start:stop]
        for tile in range(start // LANES, -(-stop // LANES)):
            parts[tile].append(result[:, tile * LANES - start : min((tile + 1) * LANES, stop) - start])
    mixed = jnp.concatenate([functools.reduce(jnp.add, part).astype(bf16) for part in parts], axis=1)
    branch = dot(mixed, wto_ref[...])
    hidden = hidden + (mods[5][:, None, :] * branch.reshape(slots, FRAMES * own, D)).reshape(lanes, D)
    final = modulated(normalized(hidden), mods[6], mods[7])
    final_high, final_low = split(final)
    products = dot(jnp.concatenate([final_high, final_low], axis=0), final_ref[...])
    by_high, by_low = products[:lanes].T, products[lanes:].T
    velocity = by_high[:CH] + by_high[CH : 2 * CH] + by_low[:CH]

    slot = lax.broadcasted_iota(jnp.int32, (1, lanes), 1) // (FRAMES * own)
    times, stride = rates_ref[0:1], rates_ref[1:2]
    noise = 0.0
    for f in range(FRAMES):
        block = noise_ref[step, f]
        block = jnp.where(low, block[:, :own], block[:, own:])
        noise = noise + placed(block, (frames - FRAMES + f) * own)
    moved = pltpu.roll(lat - stride * velocity, lanes - FRAMES * own, 1)
    moved = jnp.where(slot == slots - 1, noise, moved)
    if not last:
        lat_out, piece_out = outs
        lat_out[...] = moved
        piece = make_piece(moved, own_hidden(moved, embed_ref[...], pos_own_ref[...]))[0].astype(bf16)
        for peer in range(devices):
            piece_out[peer] = piece
    else:
        keep_out, send_out = outs
        held = frames // sections
        for i, result in enumerate((moved, lat - times * velocity)):
            for g in range(held):
                here = [
                    pltpu.roll(result, (lanes - (half * held + g) * own) % lanes, 1)[:, :own] for half in range(2)
                ]
                for out, block in (
                    (keep_out, jnp.where(low, here[0], here[1])),
                    (send_out, jnp.where(low, here[1], here[0])),
                ):
                    zeros = jnp.zeros_like(block)
                    out[i, g] = jnp.concatenate(
                        [jnp.where(low, block, zeros), jnp.where(low, zeros, block)], axis=1
                    )


def per_device(
    queue_latents,
    fresh_noise,
    slot_levels,
    level_table,
    embed_weight,
    spatial_in,
    spatial_out,
    temporal_in,
    temporal_out,
    norm_gains,
    final_weight,
):
    blocks, _, _, tokens = queue_latents.shape
    sections = lax.axis_size("tm")
    shards = lax.axis_size("space")
    axes = ("space", "tm")
    devices = sections * shards
    own = tokens // sections
    slots = blocks * sections
    frames = slots * FRAMES
    lanes = frames * own
    space_tokens = tokens * shards
    token_blocks = space_tokens // LANES
    partner = [(i, sections - 1 - i) for i in range(sections)]

    pos = jnp.asarray(sincos(space_tokens, D).astype(np.float32))
    pos_frame = jnp.asarray(sincos(frames, D).astype(np.float32))
    head = np.where(np.arange(WIDE) < INNER, np.arange(WIDE) // HD, -1)
    same_head = jnp.asarray(((head[:, None] == head[None, :]) & (head >= 0)[None, :]).astype(np.float32), bf16)
    lane = np.arange(LANES)
    lane_head = lane // own % HEADS
    lane_frame = lane // (HEADS * own)
    head_sum = np.concatenate(
        [(head[:, None] == lane_head[None, :]) & (lane_frame == f)[None, :] for f in range(FRAMES)], axis=0
    )
    head_sum = jnp.asarray(head_sum.astype(np.float32), bf16)

    final_turned = jnp.transpose(final_weight)
    spatial_turned = jnp.transpose(spatial_in)
    temporal_turned = jnp.transpose(temporal_in)

    vmem = pl.BlockSpec(memory_space=pltpu.VMEM)
    hbm = pl.BlockSpec(memory_space=pltpu.HBM)
    dma = pltpu.SemaphoreType.DMA

    def call(kernel, out_shape, arguments, scratch, name):
        spaces = {id(vmem): pltpu.VMEM, id(hbm): pltpu.HBM}
        values = [pltpu.with_memory_space_constraint(value, spaces[id(spec)]) for value, spec in arguments]
        return pl.pallas_call(
            kernel,
            out_shape=out_shape,
            in_specs=[spec for _, spec in arguments],
            out_specs=[vmem] * len(out_shape),
            scratch_shapes=scratch,
            compiler_params=pltpu.CompilerParams(vmem_limit_bytes=GRANT),
            name=name,
        )(*values)

    flat = pltpu.VMEM((CH, lanes), f32)
    first_piece_shape = pltpu.VMEM((devices, PIECE, lanes), bf16)
    piece_shape = pltpu.VMEM((devices, SHORT, lanes), bf16)
    queue = queue_latents.reshape(blocks * FRAMES, CH, tokens)
    copied = [
        same_head,
        embed_weight,
        head_sum,
        pos_frame,
        fresh_noise,
    ]
    later = [spatial_out, temporal_turned, temporal_out]
    held = [
        pltpu.VMEM((token_blocks, slots, PLAN, WIDE), bf16),
        pltpu.VMEM((token_blocks, slots, LANES + FRAMES * PIECE, INNER), bf16),
        pltpu.VMEM((slots, 8, D), f32),
        pltpu.VMEM((8, WIDE), f32),
        pltpu.VMEM((8, lanes), f32),
        pltpu.VMEM((D, LANES), bf16),
        pltpu.VMEM((own, D), f32),
        pltpu.VMEM((D, WIDE), bf16),
        *(pltpu.VMEM(x.shape, x.dtype) for x in copied),
    ]
    *held, pieces, lat = call(
        prepare_kernel,
        held + [first_piece_shape, flat],
        [(x, hbm) for x in (slot_levels, queue, pos, level_table, norm_gains, final_turned, spatial_turned, *copied)],
        [
            pltpu.SMEM((slots,), jnp.int32),
            pltpu.VMEM(level_table.shape, f32),
            pltpu.VMEM(queue.shape, f32),
            pltpu.VMEM((space_tokens, D), f32),
            pltpu.VMEM((tokens, D), f32),
            pltpu.VMEM((4, HD), f32),
            pltpu.VMEM((CH, D), f32),
            pltpu.VMEM((3 * INNER, D), bf16),
            pltpu.VMEM((slots * PLAN, D), bf16),
            dma((11 + COPIED,)),
        ],
        "slot_plan",
    )
    result_shape = pltpu.VMEM((2, blocks * FRAMES, CH, tokens), f32)
    for step in range(STEPS):
        last = step == STEPS - 1
        gathered = lax.all_to_all(pieces, axes, split_axis=0, concat_axis=0, tiled=True)
        out_shape = [result_shape] * 2 if last else [flat, piece_shape]
        scratch = [pltpu.VMEM((devices, lanes, LANES), f32), pltpu.VMEM((lanes, INNER), f32)]
        scratch += [pltpu.VMEM((slots, FRAMES * LANES, WIDE), bf16)] * 2
        if step == 0:
            later_shapes = (spatial_out.shape, (D, 2 * WIDE + INNER), temporal_out.shape)
            out_shape += [pltpu.VMEM(shape, bf16) for shape in later_shapes]
            scratch += [pltpu.VMEM(temporal_turned.shape, bf16), dma((LATER,))]
        lat, pieces, *brought = call(
            functools.partial(step_kernel, step=step),
            out_shape,
            [(x, vmem) for x in (gathered, lat, *held)] + [(x, hbm if step == 0 else vmem) for x in later],
            scratch,
            "denoise_step",
        )
        later = brought or later

    received = lax.ppermute(pieces, "tm", partner)
    return tuple((lat[i] + received[i]).reshape(queue_latents.shape) for i in range(2))


def solution(mesh):
    return jax.shard_map(
        per_device,
        mesh=mesh,
        in_specs=(
            P(("clip", "tm"), None, None, "space"),
            P("clip", None, None, "space"),
            P("clip"),
            P(),
            P(),
            P(),
            P(),
            P(),
            P(),
            P(),
            P(),
        ),
        out_specs=(P(("clip", "tm"), None, None, "space"), P(("clip", "tm"), None, None, "space")),
        check_vma=False,
    )
```

```python
import functools
import math

import jax
import jax.numpy as jnp
import numpy as np
from jax import lax
from jax.experimental import pallas as pl
from jax.experimental.pallas import tpu as pltpu
from jax.sharding import PartitionSpec as P

D = 1152
HEADS = 8
HD = 72
INNER = HEADS * HD
CH = 16
FRAMES = 2
STEPS = 3
LEVELS = 16

LANES = 128
WIDE = -(-INNER // LANES) * LANES
PIECE = 32
SHORT = PIECE - CH // 2
PACK = LANES // PIECE
PLAN = LANES + PIECE

GRANT = 26 * 1024 * 1024

epsilon = 1e-06
f32 = jnp.float32
bf16 = jnp.bfloat16


def dot(a, b):
    return lax.dot_general(a, b, (((1,), (0,)), ((), ())), preferred_element_type=f32)


def dot_nt(a, b):
    return lax.dot_general(a, b, (((1,), (1,)), ((), ())), preferred_element_type=f32)


def split(x):
    high = x.astype(bf16)
    return high, (x - high.astype(f32)).astype(bf16)


def sincos(count, width):
    half = width // 2
    rates = np.exp(-np.log(10000.0) * np.arange(half) / half)
    angles = np.arange(count)[:, None] * rates[None, :]
    return np.concatenate([np.sin(angles), np.cos(angles)], axis=-1)


def head_masks():
    shape = (HEADS, 1, WIDE)
    head = lax.broadcasted_iota(jnp.int32, shape, 0)
    position = lax.broadcasted_iota(jnp.int32, shape, 2)
    return ((position >= head * HD) & (position < (head + 1) * HD)).astype(f32)


def normalized(values):
    centered = values - jnp.mean(values, axis=-1, keepdims=True)
    return centered * lax.rsqrt(jnp.mean(centered * centered, axis=-1, keepdims=True) + epsilon)


def modulated(values, shift, scale):
    slots = shift.shape[0]
    out = values.reshape(slots, -1, D) * (1.0 + scale)[:, None, :] + shift[:, None, :]
    return out.reshape(values.shape)


def own_hidden(lat, embed, pos_own):
    lanes = lat.shape[1]
    lat_high, lat_low = split(lat)
    lat_high = lat_high.astype(f32)
    zeros = jnp.zeros((LANES - 3 * CH, lanes), f32)
    rows = jnp.concatenate([lat_high, lat_low.astype(f32), lat_high, zeros], axis=0).T.astype(bf16)
    embed_high, embed_low = split(embed)
    weights = jnp.concatenate(
        [embed_high, embed_high, embed_low, jnp.zeros((LANES - 3 * CH, D), bf16)], axis=0
    )
    own = pos_own.shape[0]
    return (dot(rows, weights).reshape(lanes // own, own, D) + pos_own[None]).reshape(lanes, D)


def make_piece(lat, hidden):
    lanes = lat.shape[1]
    centered = hidden - jnp.mean(hidden, axis=-1, keepdims=True)
    scale = lax.rsqrt(jnp.mean(centered * centered, axis=-1, keepdims=True) + epsilon)
    scale = jnp.broadcast_to(scale, (lanes, LANES)).T[:1].astype(bf16).astype(f32)
    scaled = lat * scale
    high = scaled.astype(bf16).astype(f32)
    zeros = jnp.zeros((SHORT - CH - 3, lanes), f32)
    return jnp.concatenate([high, jnp.ones((2, lanes), f32), scale, zeros], axis=0), scaled - high


def pick(values, low, frames):
    own = LANES // 2 // frames
    lane = lax.broadcasted_iota(jnp.int32, (1, LANES), 1)
    values = jnp.where(low, values, pltpu.roll(values, LANES - own, 1))
    out = jnp.where(lane // own == 0, values, 0.0)
    for g in range(1, frames):
        out = out + jnp.where(lane // own == g, pltpu.roll(values, LANES - g * own, 1), 0.0)
    return out


def placed(block, start):
    rows, width = block.shape
    wide = jnp.concatenate([block, jnp.zeros((rows, LANES - width), f32)], axis=1)
    return pltpu.roll(wide, start, 1) if start else wide


HELD = 13
COPIED = 8
LATER = 3


def start_all(copies):
    for copy in copies:
        copy.start()


def build_plans(mods_ref, pos_ref, embed_ref, weight_ref, left_ref, key_plan_ref, value_plan_ref, query_ref):
    blocks, slots = key_plan_ref.shape[:2]
    tokens = LANES
    embed = embed_ref[...]
    embed = embed - jnp.mean(embed, axis=-1, keepdims=True)
    row = lax.broadcasted_iota(jnp.int32, (PIECE - CH, 1), 0)
    part = lax.broadcasted_iota(jnp.int32, (PIECE, 1), 0)
    for b in range(blocks):
        pos = pos_ref[b * tokens : (b + 1) * tokens]
        pos = pos - jnp.mean(pos, axis=-1, keepdims=True)
        for q in range(slots):
            scale = 1.0 + mods_ref[q, 1:2]
            shift_rows = jnp.where(row < 2, mods_ref[q, 0:1], 0.0)
            left_ref[q * PLAN : (q + 1) * PLAN] = jnp.concatenate(
                [pos * scale, embed * scale, shift_rows], axis=0
            ).astype(bf16)
        for ref, weight in ((key_plan_ref, weight_ref[INNER : 2 * INNER]), (value_plan_ref, weight_ref[2 * INNER :])):
            product = dot_nt(left_ref[...], weight)
            for q in range(slots):
                rows = product[q * PLAN : (q + 1) * PLAN]
                group = rows[tokens:]
                group = jnp.where(part == CH + 1, group - group.astype(bf16).astype(f32), group).astype(bf16)
                copies = (ref.shape[2] - tokens) // PIECE
                rows = jnp.concatenate([rows[:tokens].astype(bf16)] + [group] * copies, axis=0)
                if ref.shape[3] > INNER:
                    rows = jnp.concatenate([rows, jnp.zeros((rows.shape[0], ref.shape[3] - INNER), bf16)], axis=1)
                ref[b, q] = rows
                if b == 0 and ref is key_plan_ref:
                    for start in range(q * LANES, WIDE, slots * LANES):
                        query_ref[:, start : start + LANES] = weight_ref[start : start + LANES].T


def gain_products(gains):
    products = jnp.concatenate(
        [gains[0:1] * gains[1:2], gains[2:3] * gains[3:4], jnp.zeros((6, HD), f32)], axis=0
    ) / math.sqrt(HD)
    place = lax.broadcasted_iota(jnp.int32, (HD, WIDE), 1)
    feature = lax.broadcasted_iota(jnp.int32, (HD, WIDE), 0)
    spread = ((place < INNER) & (lax.rem(place, HD) == feature)).astype(f32)
    return lax.dot_general(
        products, spread, (((1,), (0,)), ((), ())), preferred_element_type=f32, precision=lax.Precision.HIGHEST
    )


def head_normed(values, same_head, gain):
    values = values.astype(bf16).astype(f32)
    total = dot((values * values).astype(bf16), same_head)
    return values * lax.rsqrt(total * (1.0 / HD) + epsilon) * gain


def partner_latents(piece, frames, low):
    lane = lax.broadcasted_iota(jnp.int32, (1, LANES), 1)
    chosen = pick(piece[:SHORT], low, frames)
    rest = piece[SHORT:]
    rest = jnp.concatenate([rest, pltpu.roll(rest, LANES // 2, 1)], axis=0)
    lat = (chosen[:CH] + rest) / chosen[CH + 2 : CH + 3]
    lat = jnp.where(lane < LANES // 2, lat, 0.0)
    return jnp.where(low, pltpu.roll(lat, LANES // 2, 1), lat)


def prepare_kernel(levels_hbm, queue_hbm, pos_hbm, table_hbm, gains_hbm, final_hbm, wsi_hbm, *refs):
    sources, held = refs[:COPIED], refs[COPIED : COPIED + HELD + LATER]
    piece_ref, lat_ref, levels_ref, table_ref, queue_ref, pos_ref, pos_shard_ref, gains_ref, turned_ref, weight_ref, left_ref, sems = refs[
        COPIED + HELD + LATER :
    ]
    key_plan_ref, value_plan_ref, mods_ref, gain_rows_ref, rates_ref, final_ref = held[:6]
    pos_own_ref, wsi_ref, _, embed_ref = held[6:10]
    slots = mods_ref.shape[0]
    frames, _, tokens = queue_ref.shape
    own = pos_own_ref.shape[0]
    section, sections = lax.axis_index("tm"), lax.axis_size("tm")
    shard_token = pl.multiple_of(lax.axis_index("space") * tokens, 8)
    own_token = pl.multiple_of(shard_token + section * own, 8)
    stages = [
        [
            (levels_hbm, levels_ref),
            (queue_hbm, queue_ref),
            (sources[1], embed_ref),
            (pos_hbm.at[pl.ds(shard_token, tokens)], pos_shard_ref),
            (gains_hbm, gains_ref),
            (final_hbm, turned_ref),
        ],
        [(table_hbm, table_ref), (pos_hbm, pos_ref), (wsi_hbm, weight_ref)],
        [
            (pos_hbm.at[pl.ds(own_token, own)], pos_own_ref),
        ]
        + [pair for pair in zip(sources, held[8:]) if pair[1] is not embed_ref],
    ]
    count = 0
    for i, stage in enumerate(stages):
        stages[i] = [pltpu.make_async_copy(*pair, sems.at[count + j]) for j, pair in enumerate(stage)]
        count += len(stage)
    for stage in stages:
        start_all(stage)
    for copy in stages[0]:
        copy.wait()
    lat = placed(queue_ref[0], 0)
    for g in range(1, frames):
        lat = lat + placed(queue_ref[g], g * tokens)
    low = section == 0
    mine = pick(lat, low, frames)
    lat_ref[...] = jnp.where(low, mine, pltpu.roll(mine, LANES // 2, 1))
    piece, rest = make_piece(lat, own_hidden(lat, embed_ref[...], pos_shard_ref[...]))
    rest = pick(rest, section != 0, frames)
    rest = rest[: CH // 2] + pltpu.roll(rest[CH // 2 :], LANES // 2, 1)
    piece = jnp.concatenate([piece, rest], axis=0).astype(bf16)
    for peer in range(piece_ref.shape[0]):
        piece_ref[peer] = piece
    gain_rows_ref[...] = gain_products(gains_ref[...])
    high, low = split(turned_ref[...])
    final = jnp.concatenate([high.astype(f32), low.astype(f32), jnp.zeros((LANES - 2 * CH, D), f32)], axis=0)
    final_ref[...] = final.T.astype(bf16)
    lanes = lat_ref.shape[1]
    slot = lax.broadcasted_iota(jnp.int32, (1, lanes), 1) // (lanes // slots)
    times = jnp.zeros((1, lanes), f32)
    stride = jnp.zeros((1, lanes), f32)
    before = 0.0
    for q in range(slots):
        time = (levels_ref[q].astype(f32) + 1.0) / LEVELS
        times = jnp.where(slot == q, time, times)
        stride = jnp.where(slot == q, time - before, stride)
        before = time
    rates_ref[...] = jnp.concatenate([times, stride, jnp.zeros((6, lanes), f32)], axis=0)
    for copy in stages[1]:
        copy.wait()
    for q in range(slots):
        mods_ref[q] = table_ref[levels_ref[q]]
    build_plans(mods_ref, pos_ref, embed_ref, weight_ref, left_ref, key_plan_ref, value_plan_ref, wsi_ref)
    for copy in stages[2]:
        copy.wait()


def step_kernel(pieces_ref, lat_ref, *refs, step):
    first, last = step == 0, step == STEPS - 1
    held, later, refs = refs[:HELD], refs[HELD : HELD + LATER], refs[HELD + LATER :]
    outs, refs = refs[:2], refs[2:]
    wso_ref, wti_ref, wto_ref = later
    if first:
        wti_raw, wti_ref, refs = wti_ref, refs[0], refs[1:]
    cross_ref, mixed_ref, keys_ref, squares_ref = refs
    (
        key_plan_ref,
        value_plan_ref,
        mods_ref,
        gain_rows_ref,
        rates_ref,
        final_ref,
        pos_own_ref,
        wsi_ref,
        same_head_ref,
        embed_ref,
        head_sum_ref,
        pos_frame_ref,
        noise_ref,
    ) = held
    lanes = lat_ref.shape[1]
    blocks, slots = key_plan_ref.shape[:2]
    frames = slots * FRAMES
    own = lanes // frames
    devices = pieces_ref.shape[0]
    tokens = LANES
    per_block = devices // blocks
    section, sections = lax.axis_index("tm"), lax.axis_size("tm")
    low = section == 0
    mods = [mods_ref[:, row] for row in range(8)]
    same_head = same_head_ref[...]

    lat = lat_ref[...]
    if first:
        partner = lax.axis_index("space") * sections + (sections - 1 - section)
        lat = lat + partner_latents(pieces_ref[partner].astype(f32), frames // sections, low)

    def own_side():
        hidden = own_hidden(lat, embed_ref[...], pos_own_ref[...])
        yield hidden
        normed = normalized(hidden)
        yield None
        normed = modulated(normed, mods[0], mods[1]).astype(bf16)
        yield None
        queries = dot(normed, wsi_ref[...])
        yield None
        yield head_normed(queries, same_head, gain_rows_ref[0:1])

    for group in range(devices // PACK):
        stacked = pieces_ref[group * PACK : (group + 1) * PACK].astype(f32)
        if not first:
            stacked = jnp.concatenate([stacked, jnp.zeros((PACK, PIECE - SHORT, lanes), f32)], axis=1)
        stacked = stacked.reshape(LANES, lanes).T
        for part in range(PACK):
            cross_ref[group * PACK + part] = pltpu.roll(stacked, LANES - part * PIECE, 1) if part else stacked

    def turned(b, g):
        if first:
            held, rows = frames // sections, own * sections
            peers = range(b * per_block + g // held, (b + 1) * per_block, sections)
            at = g % held * rows
        else:
            rows, peers, at = own, range(b * per_block, (b + 1) * per_block), g * own
        return [cross_ref[peer, at : at + rows] for peer in peers]

    row = lax.broadcasted_iota(jnp.int32, (tokens, tokens), 0)
    column = lax.broadcasted_iota(jnp.int32, (tokens, tokens), 1)
    diagonal = row == column
    scale_lane = (lax.broadcasted_iota(jnp.int32, (8, LANES), 1) == CH + 2).astype(bf16)
    row = lax.broadcasted_iota(jnp.int32, (LANES, FRAMES * PIECE), 0)
    column = lax.broadcasted_iota(jnp.int32, (LANES, FRAMES * PIECE), 1)
    own_piece = (row // (HEADS * own) == column // PIECE).astype(f32)
    masks = head_masks()
    head_sum = head_sum_ref[...]

    turns = []
    if first:
        for i, width in enumerate((WIDE, WIDE, INNER)):
            for start in range(0, width, LANES):
                stop = min(start + LANES, width)
                turns.append((slice(i * WIDE + start, i * WIDE + stop), slice(i * INNER + start, i * INNER + stop)))
    of_frame = [slice(f * tokens, (f + 1) * tokens) for f in range(FRAMES)]
    pairs = [(b, q) for q in range(slots) for b in range(blocks)]
    rows, scales, weights, totals = {}, {}, {}, [0.0] * slots
    steps = own_side()
    hidden = next(steps)
    for b in range(blocks):
        for q in range(slots):
            tiles = [tile for f in range(FRAMES) for tile in turned(b, q * FRAMES + f)]
            rows[b, q] = jnp.concatenate(tiles, axis=0).astype(bf16)
            scales[b, q] = dot_nt(scale_lane, rows[b, q])[:1]
        for q in range(slots):
            marked = [jnp.where(diagonal, scales[b, q][:, at], 0.0).astype(bf16) for at in of_frame]
            left = jnp.concatenate([jnp.concatenate(marked, axis=0), rows[b, q][:, :PIECE]], axis=1)
            keys = dot(left, key_plan_ref[b, q])
            squares_ref[q] = (keys * keys).astype(bf16)
            keys_ref[q] = keys.astype(bf16)
            if b == 0:
                queries = next(steps, None) if q < 4 else queries
        for q in range(slots):
            if b == blocks - 1:
                for to, source in turns[q :: slots]:
                    wti_ref[:, to] = wti_raw[source].T
            sums = dot(jnp.concatenate([squares_ref[q, at] for at in of_frame], axis=1), head_sum)
            scores = []
            for f, at in enumerate(of_frame):
                g = q * FRAMES + f
                spread = (queries[g * own : (g + 1) * own][None] * masks).reshape(HEADS * own, WIDE).astype(bf16)
                scores.append(dot_nt(keys_ref[q, at], spread))
            scores = jnp.concatenate(scores, axis=1)
            weights[b, q] = jnp.exp(scores * lax.rsqrt(sums * (1.0 / HD) + epsilon))
            totals[q] = totals[q] + jnp.sum(weights[b, q], axis=0, keepdims=True)
    by_query, groups = {}, {}
    for b, q in pairs:
        by_query[b, q] = (weights[b, q] * (1.0 / totals[q])).T
    for b, q in pairs:
        pieces = jnp.concatenate([rows[b, q][at, :PIECE] for at in of_frame], axis=1)
        groups[b, q] = dot(by_query[b, q].astype(bf16), pieces) * own_piece
    for q in range(slots):
        mixed = 0.0
        for b in range(blocks):
            scaled = by_query[b, q].reshape(FRAMES, HEADS * own, tokens)
            scaled = jnp.concatenate([scaled[f] * scales[b, q][:, at] for f, at in enumerate(of_frame)], axis=0)
            met = jnp.concatenate([scaled.astype(bf16), groups[b, q].astype(bf16)], axis=1)
            mixed = mixed + dot(met, value_plan_ref[b, q])
        for f in range(FRAMES):
            g = q * FRAMES + f
            tiles = []
            for start in range(0, INNER, LANES):
                stop = min(start + LANES, INNER)
                parts = [
                    mixed[(f * HEADS + h) * own : (f * HEADS + h + 1) * own, start:stop] * masks[h, :, start:stop]
                    for h in range(start // HD, -(-stop // HD))
                ]
                tiles.append(functools.reduce(jnp.add, parts))
            mixed_ref[g * own : (g + 1) * own] = jnp.concatenate(tiles, axis=1)
    mixed = mixed_ref[...].astype(bf16)

    branch = dot(mixed, wso_ref[...])
    hidden = (
        hidden.reshape(slots, FRAMES, own, D)
        + mods[2][:, None, None, :] * branch.reshape(slots, FRAMES, own, D)
        + pos_frame_ref[...].reshape(slots, FRAMES, 1, D)
    ).reshape(lanes, D)
    normed = modulated(normalized(hidden), mods[3], mods[4]).astype(bf16)
    projected = dot(normed, wti_ref[...])
    queries, keys = projected[:, :WIDE], projected[:, WIDE : 2 * WIDE]
    values = projected[:, 2 * WIDE :].astype(bf16)
    both = head_normed(jnp.concatenate([queries, keys], axis=0), same_head, 1.0)
    queries = both[:lanes] * gain_rows_ref[1:2]
    keys = both[lanes:].astype(bf16)
    row = lax.broadcasted_iota(jnp.int32, (lanes, lanes), 0)
    column = lax.broadcasted_iota(jnp.int32, (lanes, lanes), 1)
    same_token = (lax.rem(row, own) == lax.rem(column, own)).astype(f32)
    windows = [(h * HD // LANES * LANES, -(-(h + 1) * HD // LANES) * LANES) for h in range(HEADS)]
    scores = []
    for h, (start, stop) in enumerate(windows):
        spread = (queries[:, start:stop] * masks[h, :, start:stop]).astype(bf16)
        scores.append(dot_nt(spread, keys[:, start:stop]))
    weights = [jnp.exp(score) * same_token for score in scores]
    scales = [1.0 / jnp.sum(weight, axis=-1, keepdims=True) for weight in weights]
    results = []
    for (start, stop), weight in zip(windows, weights):
        results.append(dot(weight.astype(bf16), values[:, start : min(stop, INNER)]))
    parts = [[] for _ in range(WIDE // LANES)]
    for h, (start, stop) in enumerate(windows):
        stop = min(stop, INNER)
        result = results[h] * scales[h] * masks[h, :, start:stop]
        for tile in range(start // LANES, -(-stop // LANES)):
            parts[tile].append(result[:, tile * LANES - start : min((tile + 1) * LANES, stop) - start])
    mixed = jnp.concatenate([functools.reduce(jnp.add, part).astype(bf16) for part in parts], axis=1)
    branch = dot(mixed, wto_ref[...])
    hidden = hidden + (mods[5][:, None, :] * branch.reshape(slots, FRAMES * own, D)).reshape(lanes, D)
    final = modulated(normalized(hidden), mods[6], mods[7])
    final_high, final_low = split(final)
    products = dot(jnp.concatenate([final_high, final_low], axis=0), final_ref[...])
    by_high, by_low = products[:lanes].T, products[lanes:].T
    velocity = by_high[:CH] + by_high[CH : 2 * CH] + by_low[:CH]

    slot = lax.broadcasted_iota(jnp.int32, (1, lanes), 1) // (FRAMES * own)
    times, stride = rates_ref[0:1], rates_ref[1:2]
    noise = 0.0
    for f in range(FRAMES):
        block = noise_ref[step, f]
        block = jnp.where(low, block[:, :own], block[:, own:])
        noise = noise + placed(block, (frames - FRAMES + f) * own)
    moved = pltpu.roll(lat - stride * velocity, lanes - FRAMES * own, 1)
    moved = jnp.where(slot == slots - 1, noise, moved)
    if not last:
        lat_out, piece_out = outs
        lat_out[...] = moved
        piece = make_piece(moved, own_hidden(moved, embed_ref[...], pos_own_ref[...]))[0].astype(bf16)
        for peer in range(devices):
            piece_out[peer] = piece
    else:
        keep_out, send_out = outs
        held = frames // sections
        for i, result in enumerate((moved, lat - times * velocity)):
            for g in range(held):
                here = [
                    pltpu.roll(result, (lanes - (half * held + g) * own) % lanes, 1)[:, :own] for half in range(2)
                ]
                for out, block in (
                    (keep_out, jnp.where(low, here[0], here[1])),
                    (send_out, jnp.where(low, here[1], here[0])),
                ):
                    zeros = jnp.zeros_like(block)
                    out[i, g] = jnp.concatenate(
                        [jnp.where(low, block, zeros), jnp.where(low, zeros, block)], axis=1
                    )


def per_device(
    queue_latents,
    fresh_noise,
    slot_levels,
    level_table,
    embed_weight,
    spatial_in,
    spatial_out,
    temporal_in,
    temporal_out,
    norm_gains,
    final_weight,
):
    blocks, _, _, tokens = queue_latents.shape
    sections = lax.axis_size("tm")
    shards = lax.axis_size("space")
    axes = ("space", "tm")
    devices = sections * shards
    own = tokens // sections
    slots = blocks * sections
    frames = slots * FRAMES
    lanes = frames * own
    space_tokens = tokens * shards
    token_blocks = space_tokens // LANES
    partner = [(i, sections - 1 - i) for i in range(sections)]

    pos = jnp.asarray(sincos(space_tokens, D).astype(np.float32))
    pos_frame = jnp.asarray(sincos(frames, D).astype(np.float32))
    head = np.where(np.arange(WIDE) < INNER, np.arange(WIDE) // HD, -1)
    same_head = jnp.asarray(((head[:, None] == head[None, :]) & (head >= 0)[None, :]).astype(np.float32), bf16)
    lane = np.arange(LANES)
    lane_head = lane // own % HEADS
    lane_frame = lane // (HEADS * own)
    head_sum = np.concatenate(
        [(head[:, None] == lane_head[None, :]) & (lane_frame == f)[None, :] for f in range(FRAMES)], axis=0
    )
    head_sum = jnp.asarray(head_sum.astype(np.float32), bf16)

    final_turned = jnp.transpose(final_weight)
    spatial_turned = jnp.transpose(spatial_in)
    temporal_turned = jnp.transpose(temporal_in)

    vmem = pl.BlockSpec(memory_space=pltpu.VMEM)
    hbm = pl.BlockSpec(memory_space=pltpu.HBM)
    dma = pltpu.SemaphoreType.DMA

    def call(kernel, out_shape, arguments, scratch, name):
        spaces = {id(vmem): pltpu.VMEM, id(hbm): pltpu.HBM}
        values = [pltpu.with_memory_space_constraint(value, spaces[id(spec)]) for value, spec in arguments]
        return pl.pallas_call(
            kernel,
            out_shape=out_shape,
            in_specs=[spec for _, spec in arguments],
            out_specs=[vmem] * len(out_shape),
            scratch_shapes=scratch,
            compiler_params=pltpu.CompilerParams(vmem_limit_bytes=GRANT),
            name=name,
        )(*values)

    flat = pltpu.VMEM((CH, lanes), f32)
    first_piece_shape = pltpu.VMEM((devices, PIECE, lanes), bf16)
    piece_shape = pltpu.VMEM((devices, SHORT, lanes), bf16)
    queue = queue_latents.reshape(blocks * FRAMES, CH, tokens)
    copied = [
        same_head,
        embed_weight,
        head_sum,
        pos_frame,
        fresh_noise,
        spatial_out,
        temporal_turned,
        temporal_out,
    ]
    held = [
        pltpu.VMEM((token_blocks, slots, PLAN, WIDE), bf16),
        pltpu.VMEM((token_blocks, slots, LANES + FRAMES * PIECE, INNER), bf16),
        pltpu.VMEM((slots, 8, D), f32),
        pltpu.VMEM((8, WIDE), f32),
        pltpu.VMEM((8, lanes), f32),
        pltpu.VMEM((D, LANES), bf16),
        pltpu.VMEM((own, D), f32),
        pltpu.VMEM((D, WIDE), bf16),
        *(pltpu.VMEM(x.shape, x.dtype) for x in copied),
    ]
    *held, pieces, lat = call(
        prepare_kernel,
        held + [first_piece_shape, flat],
        [(x, hbm) for x in (slot_levels, queue, pos, level_table, norm_gains, final_turned, spatial_turned, *copied)],
        [
            pltpu.SMEM((slots,), jnp.int32),
            pltpu.VMEM(level_table.shape, f32),
            pltpu.VMEM(queue.shape, f32),
            pltpu.VMEM((space_tokens, D), f32),
            pltpu.VMEM((tokens, D), f32),
            pltpu.VMEM((4, HD), f32),
            pltpu.VMEM((CH, D), f32),
            pltpu.VMEM((3 * INNER, D), bf16),
            pltpu.VMEM((slots * PLAN, D), bf16),
            dma((11 + COPIED,)),
        ],
        "slot_plan",
    )
    held, later = held[:HELD], held[HELD:]
    result_shape = pltpu.VMEM((2, blocks * FRAMES, CH, tokens), f32)
    for step in range(STEPS):
        last = step == STEPS - 1
        gathered = lax.all_to_all(pieces, axes, split_axis=0, concat_axis=0, tiled=True)
        out_shape = [result_shape] * 2 if last else [flat, piece_shape]
        scratch = [pltpu.VMEM((devices, lanes, LANES), f32), pltpu.VMEM((lanes, INNER), f32)]
        scratch += [pltpu.VMEM((slots, FRAMES * LANES, WIDE), bf16)] * 2
        if step == 0:
            out_shape += [pltpu.VMEM((D, 2 * WIDE + INNER), bf16)]
        lat, pieces, *made = call(
            functools.partial(step_kernel, step=step),
            out_shape,
            [(x, vmem) for x in (gathered, lat, *held, *later)],
            scratch,
            "denoise_step",
        )
        if made:
            later = [later[0], *made, later[2]]

    received = lax.ppermute(pieces, "tm", partner)
    return tuple((lat[i] + received[i]).reshape(queue_latents.shape) for i in range(2))


def solution(mesh):
    return jax.shard_map(
        per_device,
        mesh=mesh,
        in_specs=(
            P(("clip", "tm"), None, None, "space"),
            P("clip", None, None, "space"),
            P("clip"),
            P(),
            P(),
            P(),
            P(),
            P(),
            P(),
            P(),
            P(),
        ),
        out_specs=(P(("clip", "tm"), None, None, "space"), P(("clip", "tm"), None, None, "space")),
        check_vma=False,
    )
```

```python
import functools
import math

import jax
import jax.numpy as jnp
import numpy as np
from jax import lax
from jax.experimental import pallas as pl
from jax.experimental.pallas import tpu as pltpu
from jax.sharding import PartitionSpec as P

D = 1152
HEADS = 8
HD = 72
INNER = HEADS * HD
CH = 16
FRAMES = 2
STEPS = 3
LEVELS = 16

LANES = 128
WIDE = -(-INNER // LANES) * LANES
PIECE = 32
SHORT = PIECE - CH // 2
PACK = LANES // PIECE
PLAN = LANES + PIECE

GRANT = 26 * 1024 * 1024

epsilon = 1e-06
f32 = jnp.float32
bf16 = jnp.bfloat16


def dot(a, b):
    return lax.dot_general(a, b, (((1,), (0,)), ((), ())), preferred_element_type=f32)


def dot_nt(a, b):
    return lax.dot_general(a, b, (((1,), (1,)), ((), ())), preferred_element_type=f32)


def split(x):
    high = x.astype(bf16)
    return high, (x - high.astype(f32)).astype(bf16)


def sincos(count, width):
    half = width // 2
    rates = np.exp(-np.log(10000.0) * np.arange(half) / half)
    angles = np.arange(count)[:, None] * rates[None, :]
    return np.concatenate([np.sin(angles), np.cos(angles)], axis=-1)


def head_masks():
    shape = (HEADS, 1, WIDE)
    head = lax.broadcasted_iota(jnp.int32, shape, 0)
    position = lax.broadcasted_iota(jnp.int32, shape, 2)
    return ((position >= head * HD) & (position < (head + 1) * HD)).astype(f32)


def normalized(values):
    centered = values - jnp.mean(values, axis=-1, keepdims=True)
    return centered * lax.rsqrt(jnp.mean(centered * centered, axis=-1, keepdims=True) + epsilon)


def modulated(values, shift, scale):
    slots = shift.shape[0]
    out = values.reshape(slots, -1, D) * (1.0 + scale)[:, None, :] + shift[:, None, :]
    return out.reshape(values.shape)


def own_hidden(lat, embed, pos_own):
    lanes = lat.shape[1]
    lat_high, lat_low = split(lat)
    lat_high = lat_high.astype(f32)
    zeros = jnp.zeros((LANES - 3 * CH, lanes), f32)
    rows = jnp.concatenate([lat_high, lat_low.astype(f32), lat_high, zeros], axis=0).T.astype(bf16)
    embed_high, embed_low = split(embed)
    weights = jnp.concatenate(
        [embed_high, embed_high, embed_low, jnp.zeros((LANES - 3 * CH, D), bf16)], axis=0
    )
    own = pos_own.shape[0]
    return (dot(rows, weights).reshape(lanes // own, own, D) + pos_own[None]).reshape(lanes, D)


def make_piece(lat, hidden):
    lanes = lat.shape[1]
    centered = hidden - jnp.mean(hidden, axis=-1, keepdims=True)
    scale = lax.rsqrt(jnp.mean(centered * centered, axis=-1, keepdims=True) + epsilon)
    scale = jnp.broadcast_to(scale, (lanes, LANES)).T[:1].astype(bf16).astype(f32)
    scaled = lat * scale
    high = scaled.astype(bf16).astype(f32)
    zeros = jnp.zeros((SHORT - CH - 3, lanes), f32)
    return jnp.concatenate([high, jnp.ones((2, lanes), f32), scale, zeros], axis=0), scaled - high


def pick(values, low, frames):
    own = LANES // 2 // frames
    lane = lax.broadcasted_iota(jnp.int32, (1, LANES), 1)
    values = jnp.where(low, values, pltpu.roll(values, LANES - own, 1))
    out = jnp.where(lane // own == 0, values, 0.0)
    for g in range(1, frames):
        out = out + jnp.where(lane // own == g, pltpu.roll(values, LANES - g * own, 1), 0.0)
    return out


def placed(block, start):
    rows, width = block.shape
    wide = jnp.concatenate([block, jnp.zeros((rows, LANES - width), f32)], axis=1)
    return pltpu.roll(wide, start, 1) if start else wide


HELD = 13
COPIED = 8
LATER = 3


def start_all(copies):
    for copy in copies:
        copy.start()


def build_plans(mods_ref, pos_ref, embed_ref, weight_ref, left_ref, key_plan_ref, value_plan_ref, query_ref):
    blocks, slots = key_plan_ref.shape[:2]
    tokens = LANES
    embed = embed_ref[...]
    embed = embed - jnp.mean(embed, axis=-1, keepdims=True)
    row = lax.broadcasted_iota(jnp.int32, (PIECE - CH, 1), 0)
    part = lax.broadcasted_iota(jnp.int32, (PIECE, 1), 0)
    for b in range(blocks):
        pos = pos_ref[b * tokens : (b + 1) * tokens]
        pos = pos - jnp.mean(pos, axis=-1, keepdims=True)
        for q in range(slots):
            scale = 1.0 + mods_ref[q, 1:2]
            shift_rows = jnp.where(row < 2, mods_ref[q, 0:1], 0.0)
            left_ref[q * PLAN : (q + 1) * PLAN] = jnp.concatenate(
                [pos * scale, embed * scale, shift_rows], axis=0
            ).astype(bf16)
        for ref, weight in ((key_plan_ref, weight_ref[INNER : 2 * INNER]), (value_plan_ref, weight_ref[2 * INNER :])):
            product = dot_nt(left_ref[...], weight)
            for q in range(slots):
                rows = product[q * PLAN : (q + 1) * PLAN]
                group = rows[tokens:]
                group = jnp.where(part == CH + 1, group - group.astype(bf16).astype(f32), group).astype(bf16)
                copies = (ref.shape[2] - tokens) // PIECE
                rows = jnp.concatenate([rows[:tokens].astype(bf16)] + [group] * copies, axis=0)
                if ref.shape[3] > INNER:
                    rows = jnp.concatenate([rows, jnp.zeros((rows.shape[0], ref.shape[3] - INNER), bf16)], axis=1)
                ref[b, q] = rows
                if b == 0 and ref is key_plan_ref:
                    for start in range(q * LANES, WIDE, slots * LANES):
                        query_ref[:, start : start + LANES] = weight_ref[start : start + LANES].T


def gain_products(gains):
    products = jnp.concatenate(
        [gains[0:1] * gains[1:2], gains[2:3] * gains[3:4], jnp.zeros((6, HD), f32)], axis=0
    ) / math.sqrt(HD)
    place = lax.broadcasted_iota(jnp.int32, (HD, WIDE), 1)
    feature = lax.broadcasted_iota(jnp.int32, (HD, WIDE), 0)
    spread = ((place < INNER) & (lax.rem(place, HD) == feature)).astype(f32)
    return lax.dot_general(
        products, spread, (((1,), (0,)), ((), ())), preferred_element_type=f32, precision=lax.Precision.HIGHEST
    )


def head_normed(values, same_head, gain):
    values = values.astype(bf16).astype(f32)
    total = dot((values * values).astype(bf16), same_head)
    return values * lax.rsqrt(total * (1.0 / HD) + epsilon) * gain


def partner_latents(piece, frames, low):
    lane = lax.broadcasted_iota(jnp.int32, (1, LANES), 1)
    chosen = pick(piece[:SHORT], low, frames)
    rest = piece[SHORT:]
    rest = jnp.concatenate([rest, pltpu.roll(rest, LANES // 2, 1)], axis=0)
    lat = (chosen[:CH] + rest) / chosen[CH + 2 : CH + 3]
    lat = jnp.where(lane < LANES // 2, lat, 0.0)
    return jnp.where(low, pltpu.roll(lat, LANES // 2, 1), lat)


def prepare_kernel(levels_hbm, queue_hbm, pos_hbm, table_hbm, gains_hbm, final_hbm, wsi_hbm, *refs):
    sources, held = refs[:COPIED], refs[COPIED : COPIED + HELD + LATER]
    piece_ref, lat_ref, levels_ref, table_ref, queue_ref, pos_ref, pos_shard_ref, gains_ref, turned_ref, weight_ref, left_ref, sems = refs[
        COPIED + HELD + LATER :
    ]
    key_plan_ref, value_plan_ref, mods_ref, gain_rows_ref, rates_ref, final_ref = held[:6]
    pos_own_ref, wsi_ref, _, embed_ref = held[6:10]
    slots = mods_ref.shape[0]
    frames, _, tokens = queue_ref.shape
    own = pos_own_ref.shape[0]
    section, sections = lax.axis_index("tm"), lax.axis_size("tm")
    shard_token = pl.multiple_of(lax.axis_index("space") * tokens, 8)
    own_token = pl.multiple_of(shard_token + section * own, 8)
    stages = [
        [
            (levels_hbm, levels_ref),
            (queue_hbm, queue_ref),
            (sources[1], embed_ref),
            (pos_hbm.at[pl.ds(shard_token, tokens)], pos_shard_ref),
            (gains_hbm, gains_ref),
            (final_hbm, turned_ref),
        ],
        [(table_hbm, table_ref), (pos_hbm, pos_ref), (wsi_hbm, weight_ref)],
        [
            (pos_hbm.at[pl.ds(own_token, own)], pos_own_ref),
        ]
        + [pair for pair in zip(sources, held[8:]) if pair[1] is not embed_ref],
    ]
    count = 0
    for i, stage in enumerate(stages):
        stages[i] = [pltpu.make_async_copy(*pair, sems.at[count + j]) for j, pair in enumerate(stage)]
        count += len(stage)
    for stage in stages:
        start_all(stage)
    for copy in stages[0]:
        copy.wait()
    lat = placed(queue_ref[0], 0)
    for g in range(1, frames):
        lat = lat + placed(queue_ref[g], g * tokens)
    low = section == 0
    mine = pick(lat, low, frames)
    lat_ref[...] = jnp.where(low, mine, pltpu.roll(mine, LANES // 2, 1))
    piece, rest = make_piece(lat, own_hidden(lat, embed_ref[...], pos_shard_ref[...]))
    rest = pick(rest, section != 0, frames)
    rest = rest[: CH // 2] + pltpu.roll(rest[CH // 2 :], LANES // 2, 1)
    piece = jnp.concatenate([piece, rest], axis=0).astype(bf16)
    for peer in range(piece_ref.shape[0]):
        piece_ref[peer] = piece
    gain_rows_ref[...] = gain_products(gains_ref[...])
    high, low = split(turned_ref[...])
    final = jnp.concatenate([high.astype(f32), low.astype(f32), jnp.zeros((LANES - 2 * CH, D), f32)], axis=0)
    final_ref[...] = final.T.astype(bf16)
    lanes = lat_ref.shape[1]
    slot = lax.broadcasted_iota(jnp.int32, (1, lanes), 1) // (lanes // slots)
    times = jnp.zeros((1, lanes), f32)
    stride = jnp.zeros((1, lanes), f32)
    before = 0.0
    for q in range(slots):
        time = (levels_ref[q].astype(f32) + 1.0) / LEVELS
        times = jnp.where(slot == q, time, times)
        stride = jnp.where(slot == q, time - before, stride)
        before = time
    rates_ref[...] = jnp.concatenate([times, stride, jnp.zeros((6, lanes), f32)], axis=0)
    for copy in stages[1]:
        copy.wait()
    for q in range(slots):
        mods_ref[q] = table_ref[levels_ref[q]]
    build_plans(mods_ref, pos_ref, embed_ref, weight_ref, left_ref, key_plan_ref, value_plan_ref, wsi_ref)
    for copy in stages[2]:
        copy.wait()


def step_kernel(pieces_ref, lat_ref, *refs, step):
    first, last = step == 0, step == STEPS - 1
    held, later, refs = refs[:HELD], refs[HELD : HELD + LATER], refs[HELD + LATER :]
    outs, refs = refs[:2], refs[2:]
    wso_ref, wti_ref, wto_ref = later
    if first:
        wti_raw, wti_ref, refs = wti_ref, refs[0], refs[1:]
    cross_ref, mixed_ref, keys_ref, squares_ref = refs
    (
        key_plan_ref,
        value_plan_ref,
        mods_ref,
        gain_rows_ref,
        rates_ref,
        final_ref,
        pos_own_ref,
        wsi_ref,
        same_head_ref,
        embed_ref,
        head_sum_ref,
        pos_frame_ref,
        noise_ref,
    ) = held
    lanes = lat_ref.shape[1]
    blocks, slots = key_plan_ref.shape[:2]
    frames = slots * FRAMES
    own = lanes // frames
    devices = pieces_ref.shape[0]
    tokens = LANES
    per_block = devices // blocks
    section, sections = lax.axis_index("tm"), lax.axis_size("tm")
    low = section == 0
    mods = [mods_ref[:, row] for row in range(8)]
    same_head = same_head_ref[...]

    lat = lat_ref[...]
    if first:
        partner = lax.axis_index("space") * sections + (sections - 1 - section)
        lat = lat + partner_latents(pieces_ref[partner].astype(f32), frames // sections, low)

    def own_side():
        hidden = own_hidden(lat, embed_ref[...], pos_own_ref[...])
        yield hidden
        normed = normalized(hidden)
        yield None
        normed = modulated(normed, mods[0], mods[1]).astype(bf16)
        yield None
        queries = dot(normed, wsi_ref[...])
        yield None
        yield head_normed(queries, same_head, gain_rows_ref[0:1])

    for group in range(devices // PACK):
        stacked = pieces_ref[group * PACK : (group + 1) * PACK].astype(f32)
        if not first:
            stacked = jnp.concatenate([stacked, jnp.zeros((PACK, PIECE - SHORT, lanes), f32)], axis=1)
        stacked = stacked.reshape(LANES, lanes).T
        for part in range(PACK):
            cross_ref[group * PACK + part] = pltpu.roll(stacked, LANES - part * PIECE, 1) if part else stacked

    def turned(b, g):
        if first:
            held, rows = frames // sections, own * sections
            peers = range(b * per_block + g // held, (b + 1) * per_block, sections)
            at = g % held * rows
        else:
            rows, peers, at = own, range(b * per_block, (b + 1) * per_block), g * own
        return [cross_ref[peer, at : at + rows] for peer in peers]

    row = lax.broadcasted_iota(jnp.int32, (tokens, tokens), 0)
    column = lax.broadcasted_iota(jnp.int32, (tokens, tokens), 1)
    diagonal = row == column
    scale_lane = (lax.broadcasted_iota(jnp.int32, (8, LANES), 1) == CH + 2).astype(bf16)
    row = lax.broadcasted_iota(jnp.int32, (LANES, FRAMES * PIECE), 0)
    column = lax.broadcasted_iota(jnp.int32, (LANES, FRAMES * PIECE), 1)
    own_piece = (row // (HEADS * own) == column // PIECE).astype(f32)
    masks = head_masks()
    head_sum = head_sum_ref[...]

    turns = []
    if first:
        for i, width in enumerate((WIDE, WIDE, INNER)):
            for start in range(0, width, LANES):
                stop = min(start + LANES, width)
                turns.append((slice(i * WIDE + start, i * WIDE + stop), slice(i * INNER + start, i * INNER + stop)))
    of_frame = [slice(f * tokens, (f + 1) * tokens) for f in range(FRAMES)]
    pairs = [(b, q) for q in range(slots) for b in range(blocks)]
    rows, scales, weights, totals = {}, {}, {}, [0.0] * slots
    steps = own_side()
    hidden = next(steps)
    for b in range(blocks):
        for q in range(slots):
            tiles = [tile for f in range(FRAMES) for tile in turned(b, q * FRAMES + f)]
            rows[b, q] = jnp.concatenate(tiles, axis=0).astype(bf16)
            scales[b, q] = dot_nt(scale_lane, rows[b, q])[:1]
        for q in range(slots):
            marked = [jnp.where(diagonal, scales[b, q][:, at], 0.0).astype(bf16) for at in of_frame]
            left = jnp.concatenate([jnp.concatenate(marked, axis=0), rows[b, q][:, :PIECE]], axis=1)
            keys = dot(left, key_plan_ref[b, q])
            squares_ref[q] = (keys * keys).astype(bf16)
            keys_ref[q] = keys.astype(bf16)
            if b == 0:
                queries = next(steps, None) if q < 4 else queries
        products = {}
        for q in range(slots):
            if b == blocks - 1:
                for to, source in turns[q :: slots]:
                    wti_ref[:, to] = wti_raw[source].T
            sums = dot(jnp.concatenate([squares_ref[q, at] for at in of_frame], axis=1), head_sum)
            scores = []
            for f, at in enumerate(of_frame):
                g = q * FRAMES + f
                spread = (queries[g * own : (g + 1) * own][None] * masks).reshape(HEADS * own, WIDE).astype(bf16)
                scores.append(dot_nt(keys_ref[q, at], spread))
            products[q] = sums, scores
        for q in range(slots):
            sums, scores = products[q]
            scores = jnp.concatenate(scores, axis=1)
            weights[b, q] = jnp.exp(scores * lax.rsqrt(sums * (1.0 / HD) + epsilon))
            totals[q] = totals[q] + jnp.sum(weights[b, q], axis=0, keepdims=True)
    by_query, groups = {}, {}
    for b, q in pairs:
        by_query[b, q] = (weights[b, q] * (1.0 / totals[q])).T
    for b, q in pairs:
        pieces = jnp.concatenate([rows[b, q][at, :PIECE] for at in of_frame], axis=1)
        groups[b, q] = dot(by_query[b, q].astype(bf16), pieces) * own_piece
    for q in range(slots):
        mixed = 0.0
        for b in range(blocks):
            scaled = by_query[b, q].reshape(FRAMES, HEADS * own, tokens)
            scaled = jnp.concatenate([scaled[f] * scales[b, q][:, at] for f, at in enumerate(of_frame)], axis=0)
            met = jnp.concatenate([scaled.astype(bf16), groups[b, q].astype(bf16)], axis=1)
            mixed = mixed + dot(met, value_plan_ref[b, q])
        for f in range(FRAMES):
            g = q * FRAMES + f
            tiles = []
            for start in range(0, INNER, LANES):
                stop = min(start + LANES, INNER)
                parts = [
                    mixed[(f * HEADS + h) * own : (f * HEADS + h + 1) * own, start:stop] * masks[h, :, start:stop]
                    for h in range(start // HD, -(-stop // HD))
                ]
                tiles.append(functools.reduce(jnp.add, parts))
            mixed_ref[g * own : (g + 1) * own] = jnp.concatenate(tiles, axis=1)
    mixed = mixed_ref[...].astype(bf16)

    branch = dot(mixed, wso_ref[...])
    hidden = (
        hidden.reshape(slots, FRAMES, own, D)
        + mods[2][:, None, None, :] * branch.reshape(slots, FRAMES, own, D)
        + pos_frame_ref[...].reshape(slots, FRAMES, 1, D)
    ).reshape(lanes, D)
    normed = modulated(normalized(hidden), mods[3], mods[4]).astype(bf16)
    projected = dot(normed, wti_ref[...])
    queries, keys = projected[:, :WIDE], projected[:, WIDE : 2 * WIDE]
    values = projected[:, 2 * WIDE :].astype(bf16)
    both = head_normed(jnp.concatenate([queries, keys], axis=0), same_head, 1.0)
    queries = both[:lanes] * gain_rows_ref[1:2]
    keys = both[lanes:].astype(bf16)
    row = lax.broadcasted_iota(jnp.int32, (lanes, lanes), 0)
    column = lax.broadcasted_iota(jnp.int32, (lanes, lanes), 1)
    same_token = (lax.rem(row, own) == lax.rem(column, own)).astype(f32)
    windows = [(h * HD // LANES * LANES, -(-(h + 1) * HD // LANES) * LANES) for h in range(HEADS)]
    scores = []
    for h, (start, stop) in enumerate(windows):
        spread = (queries[:, start:stop] * masks[h, :, start:stop]).astype(bf16)
        scores.append(dot_nt(spread, keys[:, start:stop]))
    weights = [jnp.exp(score) * same_token for score in scores]
    scales = [1.0 / jnp.sum(weight, axis=-1, keepdims=True) for weight in weights]
    results = []
    for (start, stop), weight in zip(windows, weights):
        results.append(dot(weight.astype(bf16), values[:, start : min(stop, INNER)]))
    parts = [[] for _ in range(WIDE // LANES)]
    for h, (start, stop) in enumerate(windows):
        stop = min(stop, INNER)
        result = results[h] * scales[h] * masks[h, :, start:stop]
        for tile in range(start // LANES, -(-stop // LANES)):
            parts[tile].append(result[:, tile * LANES - start : min((tile + 1) * LANES, stop) - start])
    mixed = jnp.concatenate([functools.reduce(jnp.add, part).astype(bf16) for part in parts], axis=1)
    branch = dot(mixed, wto_ref[...])
    hidden = hidden + (mods[5][:, None, :] * branch.reshape(slots, FRAMES * own, D)).reshape(lanes, D)
    final = modulated(normalized(hidden), mods[6], mods[7])
    final_high, final_low = split(final)
    products = dot(jnp.concatenate([final_high, final_low], axis=0), final_ref[...])
    by_high, by_low = products[:lanes].T, products[lanes:].T
    velocity = by_high[:CH] + by_high[CH : 2 * CH] + by_low[:CH]

    slot = lax.broadcasted_iota(jnp.int32, (1, lanes), 1) // (FRAMES * own)
    times, stride = rates_ref[0:1], rates_ref[1:2]
    noise = 0.0
    for f in range(FRAMES):
        block = noise_ref[step, f]
        block = jnp.where(low, block[:, :own], block[:, own:])
        noise = noise + placed(block, (frames - FRAMES + f) * own)
    moved = pltpu.roll(lat - stride * velocity, lanes - FRAMES * own, 1)
    moved = jnp.where(slot == slots - 1, noise, moved)
    if not last:
        lat_out, piece_out = outs
        lat_out[...] = moved
        piece = make_piece(moved, own_hidden(moved, embed_ref[...], pos_own_ref[...]))[0].astype(bf16)
        for peer in range(devices):
            piece_out[peer] = piece
    else:
        keep_out, send_out = outs
        held = frames // sections
        for i, result in enumerate((moved, lat - times * velocity)):
            for g in range(held):
                here = [
                    pltpu.roll(result, (lanes - (half * held + g) * own) % lanes, 1)[:, :own] for half in range(2)
                ]
                for out, block in (
                    (keep_out, jnp.where(low, here[0], here[1])),
                    (send_out, jnp.where(low, here[1], here[0])),
                ):
                    zeros = jnp.zeros_like(block)
                    out[i, g] = jnp.concatenate(
                        [jnp.where(low, block, zeros), jnp.where(low, zeros, block)], axis=1
                    )


def per_device(
    queue_latents,
    fresh_noise,
    slot_levels,
    level_table,
    embed_weight,
    spatial_in,
    spatial_out,
    temporal_in,
    temporal_out,
    norm_gains,
    final_weight,
):
    blocks, _, _, tokens = queue_latents.shape
    sections = lax.axis_size("tm")
    shards = lax.axis_size("space")
    axes = ("space", "tm")
    devices = sections * shards
    own = tokens // sections
    slots = blocks * sections
    frames = slots * FRAMES
    lanes = frames * own
    space_tokens = tokens * shards
    token_blocks = space_tokens // LANES
    partner = [(i, sections - 1 - i) for i in range(sections)]

    pos = jnp.asarray(sincos(space_tokens, D).astype(np.float32))
    pos_frame = jnp.asarray(sincos(frames, D).astype(np.float32))
    head = np.where(np.arange(WIDE) < INNER, np.arange(WIDE) // HD, -1)
    same_head = jnp.asarray(((head[:, None] == head[None, :]) & (head >= 0)[None, :]).astype(np.float32), bf16)
    lane = np.arange(LANES)
    lane_head = lane // own % HEADS
    lane_frame = lane // (HEADS * own)
    head_sum = np.concatenate(
        [(head[:, None] == lane_head[None, :]) & (lane_frame == f)[None, :] for f in range(FRAMES)], axis=0
    )
    head_sum = jnp.asarray(head_sum.astype(np.float32), bf16)

    final_turned = jnp.transpose(final_weight)
    spatial_turned = jnp.transpose(spatial_in)
    temporal_turned = jnp.transpose(temporal_in)

    vmem = pl.BlockSpec(memory_space=pltpu.VMEM)
    hbm = pl.BlockSpec(memory_space=pltpu.HBM)
    dma = pltpu.SemaphoreType.DMA

    def call(kernel, out_shape, arguments, scratch, name):
        spaces = {id(vmem): pltpu.VMEM, id(hbm): pltpu.HBM}
        values = [pltpu.with_memory_space_constraint(value, spaces[id(spec)]) for value, spec in arguments]
        return pl.pallas_call(
            kernel,
            out_shape=out_shape,
            in_specs=[spec for _, spec in arguments],
            out_specs=[vmem] * len(out_shape),
            scratch_shapes=scratch,
            compiler_params=pltpu.CompilerParams(vmem_limit_bytes=GRANT),
            name=name,
        )(*values)

    flat = pltpu.VMEM((CH, lanes), f32)
    first_piece_shape = pltpu.VMEM((devices, PIECE, lanes), bf16)
    piece_shape = pltpu.VMEM((devices, SHORT, lanes), bf16)
    queue = queue_latents.reshape(blocks * FRAMES, CH, tokens)
    copied = [
        same_head,
        embed_weight,
        head_sum,
        pos_frame,
        fresh_noise,
        spatial_out,
        temporal_turned,
        temporal_out,
    ]
    held = [
        pltpu.VMEM((token_blocks, slots, PLAN, WIDE), bf16),
        pltpu.VMEM((token_blocks, slots, LANES + FRAMES * PIECE, INNER), bf16),
        pltpu.VMEM((slots, 8, D), f32),
        pltpu.VMEM((8, WIDE), f32),
        pltpu.VMEM((8, lanes), f32),
        pltpu.VMEM((D, LANES), bf16),
        pltpu.VMEM((own, D), f32),
        pltpu.VMEM((D, WIDE), bf16),
        *(pltpu.VMEM(x.shape, x.dtype) for x in copied),
    ]
    *held, pieces, lat = call(
        prepare_kernel,
        held + [first_piece_shape, flat],
        [(x, hbm) for x in (slot_levels, queue, pos, level_table, norm_gains, final_turned, spatial_turned, *copied)],
        [
            pltpu.SMEM((slots,), jnp.int32),
            pltpu.VMEM(level_table.shape, f32),
            pltpu.VMEM(queue.shape, f32),
            pltpu.VMEM((space_tokens, D), f32),
            pltpu.VMEM((tokens, D), f32),
            pltpu.VMEM((4, HD), f32),
            pltpu.VMEM((CH, D), f32),
            pltpu.VMEM((3 * INNER, D), bf16),
            pltpu.VMEM((slots * PLAN, D), bf16),
            dma((11 + COPIED,)),
        ],
        "slot_plan",
    )
    held, later = held[:HELD], held[HELD:]
    result_shape = pltpu.VMEM((2, blocks * FRAMES, CH, tokens), f32)
    for step in range(STEPS):
        last = step == STEPS - 1
        gathered = lax.all_to_all(pieces, axes, split_axis=0, concat_axis=0, tiled=True)
        out_shape = [result_shape] * 2 if last else [flat, piece_shape]
        scratch = [pltpu.VMEM((devices, lanes, LANES), f32), pltpu.VMEM((lanes, INNER), f32)]
        scratch += [pltpu.VMEM((slots, FRAMES * LANES, WIDE), bf16)] * 2
        if step == 0:
            out_shape += [pltpu.VMEM((D, 2 * WIDE + INNER), bf16)]
        lat, pieces, *made = call(
            functools.partial(step_kernel, step=step),
            out_shape,
            [(x, vmem) for x in (gathered, lat, *held, *later)],
            scratch,
            "denoise_step",
        )
        if made:
            later = [later[0], *made, later[2]]

    received = lax.ppermute(pieces, "tm", partner)
    return tuple((lat[i] + received[i]).reshape(queue_latents.shape) for i in range(2))


def solution(mesh):
    return jax.shard_map(
        per_device,
        mesh=mesh,
        in_specs=(
            P(("clip", "tm"), None, None, "space"),
            P("clip", None, None, "space"),
            P("clip"),
            P(),
            P(),
            P(),
            P(),
            P(),
            P(),
            P(),
            P(),
        ),
        out_specs=(P(("clip", "tm"), None, None, "space"), P(("clip", "tm"), None, None, "space")),
        check_vma=False,
    )
```

```python
import functools
import math

import jax
import jax.numpy as jnp
import numpy as np
from jax import lax
from jax.experimental import pallas as pl
from jax.experimental.pallas import tpu as pltpu
from jax.sharding import PartitionSpec as P

D = 1152
HEADS = 8
HD = 72
INNER = HEADS * HD
CH = 16
FRAMES = 2
STEPS = 3
LEVELS = 16

LANES = 128
WIDE = -(-INNER // LANES) * LANES
PIECE = 32
SHORT = PIECE - CH // 2
PACK = LANES // PIECE
PLAN = LANES + PIECE

GRANT = 26 * 1024 * 1024

epsilon = 1e-06
f32 = jnp.float32
bf16 = jnp.bfloat16


def dot(a, b):
    return lax.dot_general(a, b, (((1,), (0,)), ((), ())), preferred_element_type=f32)


def dot_nt(a, b):
    return lax.dot_general(a, b, (((1,), (1,)), ((), ())), preferred_element_type=f32)


def split(x):
    high = x.astype(bf16)
    return high, (x - high.astype(f32)).astype(bf16)


def sincos(count, width):
    half = width // 2
    rates = np.exp(-np.log(10000.0) * np.arange(half) / half)
    angles = np.arange(count)[:, None] * rates[None, :]
    return np.concatenate([np.sin(angles), np.cos(angles)], axis=-1)


def head_masks():
    shape = (HEADS, 1, WIDE)
    head = lax.broadcasted_iota(jnp.int32, shape, 0)
    position = lax.broadcasted_iota(jnp.int32, shape, 2)
    return ((position >= head * HD) & (position < (head + 1) * HD)).astype(f32)


def normalized(values):
    centered = values - jnp.mean(values, axis=-1, keepdims=True)
    return centered * lax.rsqrt(jnp.mean(centered * centered, axis=-1, keepdims=True) + epsilon)


def modulated(values, shift, scale):
    slots = shift.shape[0]
    out = values.reshape(slots, -1, D) * (1.0 + scale)[:, None, :] + shift[:, None, :]
    return out.reshape(values.shape)


def own_hidden(lat, embed, pos_own):
    lanes = lat.shape[1]
    lat_high, lat_low = split(lat)
    lat_high = lat_high.astype(f32)
    zeros = jnp.zeros((LANES - 3 * CH, lanes), f32)
    rows = jnp.concatenate([lat_high, lat_low.astype(f32), lat_high, zeros], axis=0).T.astype(bf16)
    embed_high, embed_low = split(embed)
    weights = jnp.concatenate(
        [embed_high, embed_high, embed_low, jnp.zeros((LANES - 3 * CH, D), bf16)], axis=0
    )
    own = pos_own.shape[0]
    return (dot(rows, weights).reshape(lanes // own, own, D) + pos_own[None]).reshape(lanes, D)


def make_piece(lat, hidden):
    lanes = lat.shape[1]
    centered = hidden - jnp.mean(hidden, axis=-1, keepdims=True)
    scale = lax.rsqrt(jnp.mean(centered * centered, axis=-1, keepdims=True) + epsilon)
    scale = jnp.broadcast_to(scale, (lanes, LANES)).T[:1].astype(bf16).astype(f32)
    scaled = lat * scale
    high = scaled.astype(bf16).astype(f32)
    zeros = jnp.zeros((SHORT - CH - 3, lanes), f32)
    return jnp.concatenate([high, jnp.ones((2, lanes), f32), scale, zeros], axis=0), scaled - high


def pick(values, low, frames):
    own = LANES // 2 // frames
    lane = lax.broadcasted_iota(jnp.int32, (1, LANES), 1)
    values = jnp.where(low, values, pltpu.roll(values, LANES - own, 1))
    out = jnp.where(lane // own == 0, values, 0.0)
    for g in range(1, frames):
        out = out + jnp.where(lane // own == g, pltpu.roll(values, LANES - g * own, 1), 0.0)
    return out


def placed(block, start):
    rows, width = block.shape
    wide = jnp.concatenate([block, jnp.zeros((rows, LANES - width), f32)], axis=1)
    return pltpu.roll(wide, start, 1) if start else wide


HELD = 13
COPIED = 8
LATER = 3


def start_all(copies):
    for copy in copies:
        copy.start()


def build_plans(mods_ref, pos_ref, embed_ref, weight_ref, left_ref, key_plan_ref, value_plan_ref, query_ref):
    blocks, slots = key_plan_ref.shape[:2]
    tokens = LANES
    embed = embed_ref[...]
    embed = embed - jnp.mean(embed, axis=-1, keepdims=True)
    row = lax.broadcasted_iota(jnp.int32, (PIECE - CH, 1), 0)
    part = lax.broadcasted_iota(jnp.int32, (PIECE, 1), 0)
    for b in range(blocks):
        pos = pos_ref[b * tokens : (b + 1) * tokens]
        pos = pos - jnp.mean(pos, axis=-1, keepdims=True)
        for q in range(slots):
            scale = 1.0 + mods_ref[q, 1:2]
            shift_rows = jnp.where(row < 2, mods_ref[q, 0:1], 0.0)
            left_ref[q * PLAN : (q + 1) * PLAN] = jnp.concatenate(
                [pos * scale, embed * scale, shift_rows], axis=0
            ).astype(bf16)
        products = [dot_nt(left_ref[...], weight_ref[i * INNER : (i + 1) * INNER]) for i in (1, 2)]
        for ref, product in zip((key_plan_ref, value_plan_ref), products):
            for q in range(slots):
                rows = product[q * PLAN : (q + 1) * PLAN]
                group = rows[tokens:]
                group = jnp.where(part == CH + 1, group - group.astype(bf16).astype(f32), group).astype(bf16)
                copies = (ref.shape[2] - tokens) // PIECE
                rows = jnp.concatenate([rows[:tokens].astype(bf16)] + [group] * copies, axis=0)
                if ref.shape[3] > INNER:
                    rows = jnp.concatenate([rows, jnp.zeros((rows.shape[0], ref.shape[3] - INNER), bf16)], axis=1)
                ref[b, q] = rows
                if b == 0 and ref is key_plan_ref:
                    for start in range(q * LANES, WIDE, slots * LANES):
                        query_ref[:, start : start + LANES] = weight_ref[start : start + LANES].T


def gain_products(gains):
    products = jnp.concatenate(
        [gains[0:1] * gains[1:2], gains[2:3] * gains[3:4], jnp.zeros((6, HD), f32)], axis=0
    ) / math.sqrt(HD)
    place = lax.broadcasted_iota(jnp.int32, (HD, WIDE), 1)
    feature = lax.broadcasted_iota(jnp.int32, (HD, WIDE), 0)
    spread = ((place < INNER) & (lax.rem(place, HD) == feature)).astype(f32)
    return lax.dot_general(
        products, spread, (((1,), (0,)), ((), ())), preferred_element_type=f32, precision=lax.Precision.HIGHEST
    )


def head_normed(values, same_head, gain):
    values = values.astype(bf16).astype(f32)
    total = dot((values * values).astype(bf16), same_head)
    return values * lax.rsqrt(total * (1.0 / HD) + epsilon) * gain


def partner_latents(piece, frames, low):
    lane = lax.broadcasted_iota(jnp.int32, (1, LANES), 1)
    chosen = pick(piece[:SHORT], low, frames)
    rest = piece[SHORT:]
    rest = jnp.concatenate([rest, pltpu.roll(rest, LANES // 2, 1)], axis=0)
    lat = (chosen[:CH] + rest) / chosen[CH + 2 : CH + 3]
    lat = jnp.where(lane < LANES // 2, lat, 0.0)
    return jnp.where(low, pltpu.roll(lat, LANES // 2, 1), lat)


def prepare_kernel(levels_hbm, queue_hbm, pos_hbm, table_hbm, gains_hbm, final_hbm, wsi_hbm, *refs):
    sources, held = refs[:COPIED], refs[COPIED : COPIED + HELD + LATER]
    piece_ref, lat_ref, levels_ref, table_ref, queue_ref, pos_ref, pos_shard_ref, gains_ref, turned_ref, weight_ref, left_ref, sems = refs[
        COPIED + HELD + LATER :
    ]
    key_plan_ref, value_plan_ref, mods_ref, gain_rows_ref, rates_ref, final_ref = held[:6]
    pos_own_ref, wsi_ref, _, embed_ref = held[6:10]
    slots = mods_ref.shape[0]
    frames, _, tokens = queue_ref.shape
    own = pos_own_ref.shape[0]
    section, sections = lax.axis_index("tm"), lax.axis_size("tm")
    shard_token = pl.multiple_of(lax.axis_index("space") * tokens, 8)
    own_token = pl.multiple_of(shard_token + section * own, 8)
    stages = [
        [
            (levels_hbm, levels_ref),
            (queue_hbm, queue_ref),
            (sources[1], embed_ref),
            (pos_hbm.at[pl.ds(shard_token, tokens)], pos_shard_ref),
            (gains_hbm, gains_ref),
            (final_hbm, turned_ref),
        ],
        [(table_hbm, table_ref), (pos_hbm, pos_ref), (wsi_hbm, weight_ref)],
        [
            (pos_hbm.at[pl.ds(own_token, own)], pos_own_ref),
        ]
        + [pair for pair in zip(sources, held[8:]) if pair[1] is not embed_ref],
    ]
    count = 0
    for i, stage in enumerate(stages):
        stages[i] = [pltpu.make_async_copy(*pair, sems.at[count + j]) for j, pair in enumerate(stage)]
        count += len(stage)
    for stage in stages:
        start_all(stage)
    for copy in stages[0]:
        copy.wait()
    lat = placed(queue_ref[0], 0)
    for g in range(1, frames):
        lat = lat + placed(queue_ref[g], g * tokens)
    low = section == 0
    mine = pick(lat, low, frames)
    lat_ref[...] = jnp.where(low, mine, pltpu.roll(mine, LANES // 2, 1))
    piece, rest = make_piece(lat, own_hidden(lat, embed_ref[...], pos_shard_ref[...]))
    rest = pick(rest, section != 0, frames)
    rest = rest[: CH // 2] + pltpu.roll(rest[CH // 2 :], LANES // 2, 1)
    piece = jnp.concatenate([piece, rest], axis=0).astype(bf16)
    for peer in range(piece_ref.shape[0]):
        piece_ref[peer] = piece
    gain_rows_ref[...] = gain_products(gains_ref[...])
    high, low = split(turned_ref[...])
    final = jnp.concatenate([high.astype(f32), low.astype(f32), jnp.zeros((LANES - 2 * CH, D), f32)], axis=0)
    final_ref[...] = final.T.astype(bf16)
    lanes = lat_ref.shape[1]
    slot = lax.broadcasted_iota(jnp.int32, (1, lanes), 1) // (lanes // slots)
    times = jnp.zeros((1, lanes), f32)
    stride = jnp.zeros((1, lanes), f32)
    before = 0.0
    for q in range(slots):
        time = (levels_ref[q].astype(f32) + 1.0) / LEVELS
        times = jnp.where(slot == q, time, times)
        stride = jnp.where(slot == q, time - before, stride)
        before = time
    rates_ref[...] = jnp.concatenate([times, stride, jnp.zeros((6, lanes), f32)], axis=0)
    for copy in stages[1]:
        copy.wait()
    for q in range(slots):
        mods_ref[q] = table_ref[levels_ref[q]]
    build_plans(mods_ref, pos_ref, embed_ref, weight_ref, left_ref, key_plan_ref, value_plan_ref, wsi_ref)
    for copy in stages[2]:
        copy.wait()


def step_kernel(pieces_ref, lat_ref, *refs, step):
    first, last = step == 0, step == STEPS - 1
    held, later, refs = refs[:HELD], refs[HELD : HELD + LATER], refs[HELD + LATER :]
    outs, refs = refs[:2], refs[2:]
    wso_ref, wti_ref, wto_ref = later
    if first:
        wti_raw, wti_ref, refs = wti_ref, refs[0], refs[1:]
    cross_ref, mixed_ref, keys_ref, squares_ref = refs
    (
        key_plan_ref,
        value_plan_ref,
        mods_ref,
        gain_rows_ref,
        rates_ref,
        final_ref,
        pos_own_ref,
        wsi_ref,
        same_head_ref,
        embed_ref,
        head_sum_ref,
        pos_frame_ref,
        noise_ref,
    ) = held
    lanes = lat_ref.shape[1]
    blocks, slots = key_plan_ref.shape[:2]
    frames = slots * FRAMES
    own = lanes // frames
    devices = pieces_ref.shape[0]
    tokens = LANES
    per_block = devices // blocks
    section, sections = lax.axis_index("tm"), lax.axis_size("tm")
    low = section == 0
    mods = [mods_ref[:, row] for row in range(8)]
    same_head = same_head_ref[...]

    lat = lat_ref[...]
    if first:
        partner = lax.axis_index("space") * sections + (sections - 1 - section)
        lat = lat + partner_latents(pieces_ref[partner].astype(f32), frames // sections, low)

    def own_side():
        hidden = own_hidden(lat, embed_ref[...], pos_own_ref[...])
        yield hidden
        normed = normalized(hidden)
        yield None
        normed = modulated(normed, mods[0], mods[1]).astype(bf16)
        yield None
        queries = dot(normed, wsi_ref[...])
        yield None
        yield head_normed(queries, same_head, gain_rows_ref[0:1])

    for group in range(devices // PACK):
        stacked = pieces_ref[group * PACK : (group + 1) * PACK].astype(f32)
        if not first:
            stacked = jnp.concatenate([stacked, jnp.zeros((PACK, PIECE - SHORT, lanes), f32)], axis=1)
        stacked = stacked.reshape(LANES, lanes).T
        for part in range(PACK):
            cross_ref[group * PACK + part] = pltpu.roll(stacked, LANES - part * PIECE, 1) if part else stacked

    def turned(b, g):
        if first:
            held, rows = frames // sections, own * sections
            peers = range(b * per_block + g // held, (b + 1) * per_block, sections)
            at = g % held * rows
        else:
            rows, peers, at = own, range(b * per_block, (b + 1) * per_block), g * own
        return [cross_ref[peer, at : at + rows] for peer in peers]

    row = lax.broadcasted_iota(jnp.int32, (tokens, tokens), 0)
    column = lax.broadcasted_iota(jnp.int32, (tokens, tokens), 1)
    diagonal = row == column
    scale_lane = (lax.broadcasted_iota(jnp.int32, (8, LANES), 1) == CH + 2).astype(bf16)
    row = lax.broadcasted_iota(jnp.int32, (LANES, FRAMES * PIECE), 0)
    column = lax.broadcasted_iota(jnp.int32, (LANES, FRAMES * PIECE), 1)
    own_piece = (row // (HEADS * own) == column // PIECE).astype(f32)
    masks = head_masks()
    head_sum = head_sum_ref[...]

    turns = []
    if first:
        for i, width in enumerate((WIDE, WIDE, INNER)):
            for start in range(0, width, LANES):
                stop = min(start + LANES, width)
                turns.append((slice(i * WIDE + start, i * WIDE + stop), slice(i * INNER + start, i * INNER + stop)))
    of_frame = [slice(f * tokens, (f + 1) * tokens) for f in range(FRAMES)]
    pairs = [(b, q) for q in range(slots) for b in range(blocks)]
    rows, scales, weights, totals = {}, {}, {}, [0.0] * slots
    steps = own_side()
    hidden = next(steps)
    for b in range(blocks):
        for q in range(slots):
            tiles = [tile for f in range(FRAMES) for tile in turned(b, q * FRAMES + f)]
            rows[b, q] = jnp.concatenate(tiles, axis=0).astype(bf16)
            scales[b, q] = dot_nt(scale_lane, rows[b, q])[:1]
        for q in range(slots):
            marked = [jnp.where(diagonal, scales[b, q][:, at], 0.0).astype(bf16) for at in of_frame]
            left = jnp.concatenate([jnp.concatenate(marked, axis=0), rows[b, q][:, :PIECE]], axis=1)
            keys = dot(left, key_plan_ref[b, q])
            squares_ref[q] = (keys * keys).astype(bf16)
            keys_ref[q] = keys.astype(bf16)
            if b == 0:
                queries = next(steps, None) if q < 4 else queries
        products = {}
        for q in range(slots):
            if b == blocks - 1:
                for to, source in turns[q :: slots]:
                    wti_ref[:, to] = wti_raw[source].T
            sums = dot(jnp.concatenate([squares_ref[q, at] for at in of_frame], axis=1), head_sum)
            scores = []
            for f, at in enumerate(of_frame):
                g = q * FRAMES + f
                spread = (queries[g * own : (g + 1) * own][None] * masks).reshape(HEADS * own, WIDE).astype(bf16)
                scores.append(dot_nt(keys_ref[q, at], spread))
            products[q] = sums, scores
        for q in range(slots):
            sums, scores = products[q]
            scores = jnp.concatenate(scores, axis=1)
            weights[b, q] = jnp.exp(scores * lax.rsqrt(sums * (1.0 / HD) + epsilon))
            totals[q] = totals[q] + jnp.sum(weights[b, q], axis=0, keepdims=True)
    by_query, groups = {}, {}
    for b, q in pairs:
        by_query[b, q] = (weights[b, q] * (1.0 / totals[q])).T
    for b, q in pairs:
        pieces = jnp.concatenate([rows[b, q][at, :PIECE] for at in of_frame], axis=1)
        groups[b, q] = dot(by_query[b, q].astype(bf16), pieces) * own_piece
    for q in range(slots):
        mixed = 0.0
        for b in range(blocks):
            scaled = by_query[b, q].reshape(FRAMES, HEADS * own, tokens)
            scaled = jnp.concatenate([scaled[f] * scales[b, q][:, at] for f, at in enumerate(of_frame)], axis=0)
            met = jnp.concatenate([scaled.astype(bf16), groups[b, q].astype(bf16)], axis=1)
            mixed = mixed + dot(met, value_plan_ref[b, q])
        for f in range(FRAMES):
            g = q * FRAMES + f
            tiles = []
            for start in range(0, INNER, LANES):
                stop = min(start + LANES, INNER)
                parts = [
                    mixed[(f * HEADS + h) * own : (f * HEADS + h + 1) * own, start:stop] * masks[h, :, start:stop]
                    for h in range(start // HD, -(-stop // HD))
                ]
                tiles.append(functools.reduce(jnp.add, parts))
            mixed_ref[g * own : (g + 1) * own] = jnp.concatenate(tiles, axis=1)
    mixed = mixed_ref[...].astype(bf16)

    branch = dot(mixed, wso_ref[...])
    hidden = (
        hidden.reshape(slots, FRAMES, own, D)
        + mods[2][:, None, None, :] * branch.reshape(slots, FRAMES, own, D)
        + pos_frame_ref[...].reshape(slots, FRAMES, 1, D)
    ).reshape(lanes, D)
    normed = modulated(normalized(hidden), mods[3], mods[4]).astype(bf16)
    projected = dot(normed, wti_ref[...])
    queries, keys = projected[:, :WIDE], projected[:, WIDE : 2 * WIDE]
    values = projected[:, 2 * WIDE :].astype(bf16)
    both = head_normed(jnp.concatenate([queries, keys], axis=0), same_head, 1.0)
    queries = both[:lanes] * gain_rows_ref[1:2]
    keys = both[lanes:].astype(bf16)
    row = lax.broadcasted_iota(jnp.int32, (lanes, lanes), 0)
    column = lax.broadcasted_iota(jnp.int32, (lanes, lanes), 1)
    same_token = (lax.rem(row, own) == lax.rem(column, own)).astype(f32)
    windows = [(h * HD // LANES * LANES, -(-(h + 1) * HD // LANES) * LANES) for h in range(HEADS)]
    scores = []
    for h, (start, stop) in enumerate(windows):
        spread = (queries[:, start:stop] * masks[h, :, start:stop]).astype(bf16)
        scores.append(dot_nt(spread, keys[:, start:stop]))
    weights = [jnp.exp(score) * same_token for score in scores]
    scales = [1.0 / jnp.sum(weight, axis=-1, keepdims=True) for weight in weights]
    results = []
    for (start, stop), weight in zip(windows, weights):
        results.append(dot(weight.astype(bf16), values[:, start : min(stop, INNER)]))
    parts = [[] for _ in range(WIDE // LANES)]
    for h, (start, stop) in enumerate(windows):
        stop = min(stop, INNER)
        result = results[h] * scales[h] * masks[h, :, start:stop]
        for tile in range(start // LANES, -(-stop // LANES)):
            parts[tile].append(result[:, tile * LANES - start : min((tile + 1) * LANES, stop) - start])
    mixed = jnp.concatenate([functools.reduce(jnp.add, part).astype(bf16) for part in parts], axis=1)
    branch = dot(mixed, wto_ref[...])
    hidden = hidden + (mods[5][:, None, :] * branch.reshape(slots, FRAMES * own, D)).reshape(lanes, D)
    final = modulated(normalized(hidden), mods[6], mods[7])
    final_high, final_low = split(final)
    products = dot(jnp.concatenate([final_high, final_low], axis=0), final_ref[...])
    by_high, by_low = products[:lanes].T, products[lanes:].T
    velocity = by_high[:CH] + by_high[CH : 2 * CH] + by_low[:CH]

    slot = lax.broadcasted_iota(jnp.int32, (1, lanes), 1) // (FRAMES * own)
    times, stride = rates_ref[0:1], rates_ref[1:2]
    noise = 0.0
    for f in range(FRAMES):
        block = noise_ref[step, f]
        block = jnp.where(low, block[:, :own], block[:, own:])
        noise = noise + placed(block, (frames - FRAMES + f) * own)
    moved = pltpu.roll(lat - stride * velocity, lanes - FRAMES * own, 1)
    moved = jnp.where(slot == slots - 1, noise, moved)
    if not last:
        lat_out, piece_out = outs
        lat_out[...] = moved
        piece = make_piece(moved, own_hidden(moved, embed_ref[...], pos_own_ref[...]))[0].astype(bf16)
        for peer in range(devices):
            piece_out[peer] = piece
    else:
        keep_out, send_out = outs
        held = frames // sections
        for i, result in enumerate((moved, lat - times * velocity)):
            for g in range(held):
                here = [
                    pltpu.roll(result, (lanes - (half * held + g) * own) % lanes, 1)[:, :own] for half in range(2)
                ]
                for out, block in (
                    (keep_out, jnp.where(low, here[0], here[1])),
                    (send_out, jnp.where(low, here[1], here[0])),
                ):
                    zeros = jnp.zeros_like(block)
                    out[i, g] = jnp.concatenate(
                        [jnp.where(low, block, zeros), jnp.where(low, zeros, block)], axis=1
                    )


def per_device(
    queue_latents,
    fresh_noise,
    slot_levels,
    level_table,
    embed_weight,
    spatial_in,
    spatial_out,
    temporal_in,
    temporal_out,
    norm_gains,
    final_weight,
):
    blocks, _, _, tokens = queue_latents.shape
    sections = lax.axis_size("tm")
    shards = lax.axis_size("space")
    axes = ("space", "tm")
    devices = sections * shards
    own = tokens // sections
    slots = blocks * sections
    frames = slots * FRAMES
    lanes = frames * own
    space_tokens = tokens * shards
    token_blocks = space_tokens // LANES
    partner = [(i, sections - 1 - i) for i in range(sections)]

    pos = jnp.asarray(sincos(space_tokens, D).astype(np.float32))
    pos_frame = jnp.asarray(sincos(frames, D).astype(np.float32))
    head = np.where(np.arange(WIDE) < INNER, np.arange(WIDE) // HD, -1)
    same_head = jnp.asarray(((head[:, None] == head[None, :]) & (head >= 0)[None, :]).astype(np.float32), bf16)
    lane = np.arange(LANES)
    lane_head = lane // own % HEADS
    lane_frame = lane // (HEADS * own)
    head_sum = np.concatenate(
        [(head[:, None] == lane_head[None, :]) & (lane_frame == f)[None, :] for f in range(FRAMES)], axis=0
    )
    head_sum = jnp.asarray(head_sum.astype(np.float32), bf16)

    final_turned = jnp.transpose(final_weight)
    spatial_turned = jnp.transpose(spatial_in)
    temporal_turned = jnp.transpose(temporal_in)

    vmem = pl.BlockSpec(memory_space=pltpu.VMEM)
    hbm = pl.BlockSpec(memory_space=pltpu.HBM)
    dma = pltpu.SemaphoreType.DMA

    def call(kernel, out_shape, arguments, scratch, name):
        spaces = {id(vmem): pltpu.VMEM, id(hbm): pltpu.HBM}
        values = [pltpu.with_memory_space_constraint(value, spaces[id(spec)]) for value, spec in arguments]
        return pl.pallas_call(
            kernel,
            out_shape=out_shape,
            in_specs=[spec for _, spec in arguments],
            out_specs=[vmem] * len(out_shape),
            scratch_shapes=scratch,
            compiler_params=pltpu.CompilerParams(vmem_limit_bytes=GRANT),
            name=name,
        )(*values)

    flat = pltpu.VMEM((CH, lanes), f32)
    first_piece_shape = pltpu.VMEM((devices, PIECE, lanes), bf16)
    piece_shape = pltpu.VMEM((devices, SHORT, lanes), bf16)
    queue = queue_latents.reshape(blocks * FRAMES, CH, tokens)
    copied = [
        same_head,
        embed_weight,
        head_sum,
        pos_frame,
        fresh_noise,
        spatial_out,
        temporal_turned,
        temporal_out,
    ]
    held = [
        pltpu.VMEM((token_blocks, slots, PLAN, WIDE), bf16),
        pltpu.VMEM((token_blocks, slots, LANES + FRAMES * PIECE, INNER), bf16),
        pltpu.VMEM((slots, 8, D), f32),
        pltpu.VMEM((8, WIDE), f32),
        pltpu.VMEM((8, lanes), f32),
        pltpu.VMEM((D, LANES), bf16),
        pltpu.VMEM((own, D), f32),
        pltpu.VMEM((D, WIDE), bf16),
        *(pltpu.VMEM(x.shape, x.dtype) for x in copied),
    ]
    *held, pieces, lat = call(
        prepare_kernel,
        held + [first_piece_shape, flat],
        [(x, hbm) for x in (slot_levels, queue, pos, level_table, norm_gains, final_turned, spatial_turned, *copied)],
        [
            pltpu.SMEM((slots,), jnp.int32),
            pltpu.VMEM(level_table.shape, f32),
            pltpu.VMEM(queue.shape, f32),
            pltpu.VMEM((space_tokens, D), f32),
            pltpu.VMEM((tokens, D), f32),
            pltpu.VMEM((4, HD), f32),
            pltpu.VMEM((CH, D), f32),
            pltpu.VMEM((3 * INNER, D), bf16),
            pltpu.VMEM((slots * PLAN, D), bf16),
            dma((11 + COPIED,)),
        ],
        "slot_plan",
    )
    held, later = held[:HELD], held[HELD:]
    result_shape = pltpu.VMEM((2, blocks * FRAMES, CH, tokens), f32)
    for step in range(STEPS):
        last = step == STEPS - 1
        gathered = lax.all_to_all(pieces, axes, split_axis=0, concat_axis=0, tiled=True)
        out_shape = [result_shape] * 2 if last else [flat, piece_shape]
        scratch = [pltpu.VMEM((devices, lanes, LANES), f32), pltpu.VMEM((lanes, INNER), f32)]
        scratch += [pltpu.VMEM((slots, FRAMES * LANES, WIDE), bf16)] * 2
        if step == 0:
            out_shape += [pltpu.VMEM((D, 2 * WIDE + INNER), bf16)]
        lat, pieces, *made = call(
            functools.partial(step_kernel, step=step),
            out_shape,
            [(x, vmem) for x in (gathered, lat, *held, *later)],
            scratch,
            "denoise_step",
        )
        if made:
            later = [later[0], *made, later[2]]

    received = lax.ppermute(pieces, "tm", partner)
    return tuple((lat[i] + received[i]).reshape(queue_latents.shape) for i in range(2))


def solution(mesh):
    return jax.shard_map(
        per_device,
        mesh=mesh,
        in_specs=(
            P(("clip", "tm"), None, None, "space"),
            P("clip", None, None, "space"),
            P("clip"),
            P(),
            P(),
            P(),
            P(),
            P(),
            P(),
            P(),
            P(),
        ),
        out_specs=(P(("clip", "tm"), None, None, "space"), P(("clip", "tm"), None, None, "space")),
        check_vma=False,
    )
```
